32 devices in a mesh: gx: 8 (over y, x, core), gy: 4 (over z).
Axes of the slice: x: 2, y: 2, z: 4, core: 2. Of those that a mesh axis runs over, the one named last changes fastest.
Arguments:
- velocity: float32 [3, 128, 64, 512], P(None, 'gx', 'gy'), may hold values from -6 to 6
- stress: float32 [6, 128, 64, 512], P(None, 'gx', 'gy'), may hold values from -6 to 6
- pier_velocity: float32 [128, 16], P('gx', 'gy'), may hold values from -6 to 6
- buoyancy: float32 [128, 64, 512], P('gx', 'gy'), may hold values from 0.5 to 2
- layer: int32 [128], P('gx'), may hold values from 0 to 7, as said below
- lame_table: float32 [8], replicated, may hold values from 0.3 to 1.2
- shear_table: float32 [8], replicated, may hold values from 0.2 to 0.8
- relax_table: float32 [8], replicated, may hold values from 0.6 to 0.95
- impedance: float32 [16], P('gy'), may hold values from 0.5 to 2
- footprint: int32 [16, 16], replicated, may hold values from 0 to 32767, as said below
- damp_inverse: float32 [128, 128], replicated
Outputs:
- velocity_out: float32 [3, 128, 64, 512], P(None, 'gx', 'gy')
- stress_out: float32 [6, 128, 64, 512], P(None, 'gx', 'gy')
- pier_out: float32 [128, 16], P('gx', 'gy')
The draws below stay inside these ranges and needn't reach their ends.
Inputs may be any that keep to these rules, and one draw needn't show every extreme that they name: `footprint`: row p lists the 16 cells of a square of 4 by 4 cells, row by row; squares may intersect and lie anywhere in the plane. `layer`: non-decreasing along depth; the first cell is in layer 0 and the last in layer 7.
All inputs are finite; a program needn't handle non-finite values.
Results may differ from the reference program's by a relative error of at most 0.00011.
Values sent between devices are 32-bit elements; how exact they have to be, the bound alone decides.
A program may use at most 192 MiB of HBM per device.

```python
import math
import jax
import jax.numpy as jnp
from jax import lax

NX = 512
FOOT_SIDE = 4
NLAYER = 8
STEPS = 2
NZ = 128
NY = 64
NPIER = 16
FOOT = 16


def draw_damp_inverse(key, part):
    key_diag, key_off = jax.random.split(jax.random.fold_in(key, 7))
    diagonal = jax.random.uniform(key_diag, (NZ,), jnp.float32, 0.6, 1.0)
    spread = jax.random.normal(key_off, (NZ, NZ), jnp.float32) * (0.5 / math.sqrt(NZ))
    return jnp.eye(NZ, dtype=jnp.float32) * diagonal[:, None] + spread


def draw_footprint(key, part):
    key_rows, key_cols, key_high, key_low = jax.random.split(jax.random.fold_in(key, 11), 4)
    rows = jax.random.randint(key_rows, (NPIER,), 0, NY - FOOT_SIDE + 1)
    cols = jax.random.randint(key_cols, (NPIER,), 0, NX - FOOT_SIDE + 1)
    high = jax.random.randint(key_high, (), 0, NPIER)
    low = (high + 1 + jax.random.randint(key_low, (), 0, NPIER - 1)) % NPIER
    pier_ids = jnp.arange(NPIER, dtype=jnp.int32)
    rows = jnp.where(pier_ids == high, NY - FOOT_SIDE, rows)
    rows = jnp.where(pier_ids == low, 0, rows)
    cols = jnp.where(pier_ids == high, NX - FOOT_SIDE, cols)
    cols = jnp.where(pier_ids == low, 0, cols)
    offsets = jnp.arange(FOOT, dtype=jnp.int32)
    cells = (rows[:, None] + offsets[None, :] // FOOT_SIDE) * NX + cols[:, None] + offsets[None, :] % FOOT_SIDE
    return cells.astype(jnp.int32)


def draw_layer(key, part):
    depth_ids = jnp.arange(NZ, dtype=jnp.int32)
    rises = (jax.random.randint(jax.random.fold_in(key, 23), (NZ,), 0, NZ) < NLAYER).astype(jnp.int32)
    rises = jnp.where(depth_ids == 0, 0, rises)
    levels = jnp.minimum(jnp.cumsum(rises), NLAYER - 1)
    return jnp.where(depth_ids == NZ - 1, NLAYER - 1, levels).astype(jnp.int32)


def level_of(key, extent, shards, least, high):
    gain = 1.0
    for dim, parts in shards:
        steps = jax.random.uniform(jax.random.fold_in(jax.random.fold_in(key, 6), dim), (parts,), jnp.float32, least / len(shards), high / len(shards))
        gain = gain * jnp.repeat(jnp.exp(steps), extent[dim] // parts).reshape((-1,) + (1,) * (len(extent) - 1 - dim))
    return gain


def centred(stream_key, dims, scale, reach, cuts=(), held_as=jnp.bfloat16):
    drawn = scale * jax.random.normal(stream_key, dims, jnp.float32)
    if cuts:
        drawn = drawn * level_of(stream_key, dims, cuts, -0.22, 0.18)
    return jnp.clip(drawn, -reach, reach).astype(held_as)


def setup_inputs(seed: int = 0) -> dict:
    keys = jax.random.split(jax.random.key(seed), 12)
    velocity = centred(keys[0], (3, NZ, NY, NX), 1.0, 6.0, ((1, 8), (2, 4)), jnp.float32)
    stress = centred(keys[1], (6, NZ, NY, NX), 1.0, 6.0, ((1, 8), (2, 4)), jnp.float32)
    pier_velocity = centred(keys[2], (NZ, NPIER), 1.0, 6.0, ((0, 8), (1, 4)), jnp.float32)
    buoyancy = jnp.clip(jnp.exp(math.log(2.0) - 1.3862944 * jax.random.uniform(keys[3], (NZ, NY, NX), jnp.float32) ** level_of(keys[3], (NZ, NY, NX), ((0, 8), (1, 4)), -0.2, 0.2)), 0.5, 2.0)
    layer = draw_layer(jax.random.fold_in(keys[11], 71), 0)
    lame_table = jnp.clip(jnp.exp(jax.random.uniform(keys[5], (NLAYER,), jnp.float32, math.log(0.3), math.log(1.2))), 0.3, 1.2)
    shear_table = jnp.clip(jnp.exp(jax.random.uniform(keys[6], (NLAYER,), jnp.float32, math.log(0.2), math.log(0.8))), 0.2, 0.8)
    relax_table = jnp.clip(jax.random.uniform(keys[7], (NLAYER,), jnp.float32, 0.6, 0.95), 0.6, 0.95)
    impedance = jnp.clip(jnp.exp(math.log(2.0) - 1.3862944 * jax.random.uniform(keys[8], (NPIER,), jnp.float32) ** level_of(keys[8], (NPIER,), ((0, 4),), -0.2, 0.2)), 0.5, 2.0)
    footprint = draw_footprint(jax.random.fold_in(keys[11], 71), 0)
    damp_inverse = draw_damp_inverse(jax.random.fold_in(keys[11], 71), 0)
    return {"velocity": velocity, "stress": stress, "pier_velocity": pier_velocity, "buoyancy": buoyancy, "layer": layer, "lame_table": lame_table, "shear_table": shear_table, "relax_table": relax_table, "impedance": impedance, "footprint": footprint, "damp_inverse": damp_inverse}


grid_ratio = 0.25
soil_gain = 0.2
pier_gain = 0.5


def forward_diff(padded, along):
    center = padded[1:-1, 1:-1, 1:-1]
    if along == 0:
        return padded[2:, 1:-1, 1:-1] - center
    if along == 1:
        return padded[1:-1, 2:, 1:-1] - center
    return padded[1:-1, 1:-1, 2:] - center


def backward_diff(padded, along):
    center = padded[1:-1, 1:-1, 1:-1]
    if along == 0:
        return center - padded[:-2, 1:-1, 1:-1]
    if along == 1:
        return center - padded[1:-1, :-2, 1:-1]
    return center - padded[1:-1, 1:-1, :-2]


def move_velocity(velocity, padded, buoyancy):
    scaled = grid_ratio * buoyancy
    first = velocity[0] + scaled * (backward_diff(padded[0], 2) + forward_diff(padded[3], 1) + forward_diff(padded[4], 0))
    second = velocity[1] + scaled * (forward_diff(padded[3], 2) + backward_diff(padded[1], 1) + forward_diff(padded[5], 0))
    third = velocity[2] + scaled * (forward_diff(padded[4], 2) + forward_diff(padded[5], 1) + backward_diff(padded[2], 0))
    return jnp.stack([first, second, third])


def move_stress(stress, padded, lame_first, shear_mod, relax):
    strain_x = forward_diff(padded[0], 2)
    strain_y = forward_diff(padded[1], 1)
    strain_z = forward_diff(padded[2], 0)
    modulus = lame_first + 2.0 * shear_mod
    normal_x = relax * stress[0] + grid_ratio * (modulus * strain_x + lame_first * (strain_y + strain_z))
    normal_y = relax * stress[1] + grid_ratio * (modulus * strain_y + lame_first * (strain_x + strain_z))
    normal_z = relax * stress[2] + grid_ratio * (modulus * strain_z + lame_first * (strain_x + strain_y))
    shear_xy = relax * stress[3] + grid_ratio * shear_mod * (backward_diff(padded[0], 1) + backward_diff(padded[1], 2))
    shear_xz = relax * stress[4] + grid_ratio * shear_mod * (backward_diff(padded[0], 0) + backward_diff(padded[2], 2))
    shear_yz = relax * stress[5] + grid_ratio * shear_mod * (backward_diff(padded[1], 0) + backward_diff(padded[2], 1))
    return jnp.stack([normal_x, normal_y, normal_z, shear_xy, shear_xz, shear_yz])


def layer_values(layer, table):
    levels = jnp.arange(table.shape[0], dtype=jnp.int32)
    onehot = (layer[:, None] == levels[None, :]).astype(table.dtype)
    return jnp.sum(onehot * table[None, :], axis=1)[:, None, None]


def reference(velocity, stress, pier_velocity, buoyancy, layer, lame_table, shear_table, relax_table, impedance, footprint, damp_inverse):
    lame_first = layer_values(layer, lame_table)
    shear_mod = layer_values(layer, shear_table)
    relax = layer_values(layer, relax_table)
    cells = footprint.reshape(-1)
    for time_step in range(STEPS):
        padded = jnp.pad(stress, ((0, 0), (1, 1), (1, 1), (1, 1)))
        velocity = move_velocity(velocity, padded, buoyancy)
        vertical = velocity[2].reshape(NZ, NY * NX)
        mean_speed = jnp.sum(vertical[:, cells].reshape(NZ, NPIER, FOOT), axis=2) / FOOT
        force = impedance[None, :] * (pier_velocity - mean_speed)
        pier_velocity = pier_velocity - pier_gain * force
        vertical = vertical.at[:, cells].add(soil_gain * jnp.repeat(force, FOOT, axis=1))
        velocity = jnp.stack([velocity[0], velocity[1], vertical.reshape(NZ, NY, NX)])
        flat = velocity.reshape(3, NZ, NY * NX)
        velocity = jnp.einsum("zk,fkm->fzm", damp_inverse, flat, precision=lax.Precision.HIGHEST).reshape(3, NZ, NY, NX)
        padded = jnp.pad(velocity, ((0, 0), (1, 1), (1, 1), (1, 1)))
        stress = move_stress(stress, padded, lame_first, shear_mod, relax)
    return (velocity, stress, pier_velocity)
```

```python
import functools
import jax
import jax.numpy as jnp
from jax import lax
from jax.experimental import pallas as pl
from jax.experimental.pallas import tpu as pltpu
from jax.sharding import PartitionSpec as P

STEPS = 2
FOOT = 16


grid_ratio = 0.25
soil_gain = 0.2
pier_gain = 0.5


def extended(cells, sides, width):
    for axis, dim in sides:
        count = lax.axis_size(axis)
        ends = count - 1
        head = lax.slice_in_dim(cells, 0, width, axis=dim)
        tail = lax.slice_in_dim(cells, cells.shape[dim] - width, cells.shape[dim], axis=dim)
        cells = jnp.concatenate(
            [
                lax.ppermute(tail, axis, [(i, (i + 1) % count) for i in range(ends)]),
                cells,
                lax.ppermute(head, axis, [((i + 1) % count, i) for i in range(ends)]),
            ],
            axis=dim,
        )
    return cells


def forward_diff(padded, along):
    center = padded[1:-1, 1:-1, 1:-1]
    if along == 0:
        return padded[2:, 1:-1, 1:-1] - center
    if along == 1:
        return padded[1:-1, 2:, 1:-1] - center
    return padded[1:-1, 1:-1, 2:] - center


def backward_diff(padded, along):
    center = padded[1:-1, 1:-1, 1:-1]
    if along == 0:
        return center - padded[:-2, 1:-1, 1:-1]
    if along == 1:
        return center - padded[1:-1, :-2, 1:-1]
    return center - padded[1:-1, 1:-1, :-2]


def move_velocity(velocity, padded, buoyancy):
    scaled = grid_ratio * buoyancy
    first = velocity[0] + scaled * (
        backward_diff(padded[0], 2) + forward_diff(padded[3], 1) + forward_diff(padded[4], 0)
    )
    second = velocity[1] + scaled * (
        forward_diff(padded[3], 2) + backward_diff(padded[1], 1) + forward_diff(padded[5], 0)
    )
    third = velocity[2] + scaled * (
        forward_diff(padded[4], 2) + forward_diff(padded[5], 1) + backward_diff(padded[2], 0)
    )
    return jnp.stack([first, second, third])


def move_stress(stress, padded, lame_first, shear_mod, relax):
    strain_x = forward_diff(padded[0], 2)
    strain_y = forward_diff(padded[1], 1)
    strain_z = forward_diff(padded[2], 0)
    modulus = lame_first + 2.0 * shear_mod
    normal_x = relax * stress[0] + grid_ratio * (
        modulus * strain_x + lame_first * (strain_y + strain_z)
    )
    normal_y = relax * stress[1] + grid_ratio * (
        modulus * strain_y + lame_first * (strain_x + strain_z)
    )
    normal_z = relax * stress[2] + grid_ratio * (
        modulus * strain_z + lame_first * (strain_x + strain_y)
    )
    shear_xy = relax * stress[3] + grid_ratio * shear_mod * (
        backward_diff(padded[0], 1) + backward_diff(padded[1], 2)
    )
    shear_xz = relax * stress[4] + grid_ratio * shear_mod * (
        backward_diff(padded[0], 0) + backward_diff(padded[2], 2)
    )
    shear_yz = relax * stress[5] + grid_ratio * shear_mod * (
        backward_diff(padded[1], 0) + backward_diff(padded[2], 1)
    )
    return jnp.stack([normal_x, normal_y, normal_z, shear_xy, shear_xz, shear_yz])


def layer_values(layer, table):
    levels = jnp.arange(table.shape[0], dtype=jnp.int32)
    onehot = (layer[:, None] == levels[None, :]).astype(table.dtype)
    return jnp.sum(onehot * table[None, :], axis=1)[:, None, None]


def with_faces(fields):
    padded = extended(fields, (("gx", 1), ("gy", 2)), 1)
    return jnp.pad(padded, ((0, 0), (0, 0), (0, 0), (1, 1)))


def footprint_matches(cell_ids, footprint):
    piers = footprint.shape[0]
    equal = (cell_ids[:, None] == footprint.reshape(-1)[None, :]).astype(jnp.float32)
    return jnp.sum(equal.reshape(cell_ids.shape[0], piers, FOOT), axis=2)


def damp_columns(velocity, inverse):
    pencils = lax.all_to_all(velocity, "gx", split_axis=3, concat_axis=1, tiled=True)
    shape = pencils.shape
    flat = pencils.reshape(shape[0], shape[1], shape[2] * shape[3])
    damped = jnp.einsum("zk,fkm->fzm", inverse, flat, precision=lax.Precision.HIGHEST).reshape(
        shape
    )
    return lax.all_to_all(damped, "gx", split_axis=1, concat_axis=3, tiled=True)


def body(
    velocity,
    stress,
    pier_velocity,
    buoyancy,
    layer,
    lame_table,
    shear_table,
    relax_table,
    impedance,
    footprint,
    damp_inverse,
):
    depth_cells, side_cells, line_cells = (velocity.shape[1], velocity.shape[2], velocity.shape[3])
    own_piers = pier_velocity.shape[1]
    lame_first = layer_values(layer, lame_table)
    shear_mod = layer_values(layer, shear_table)
    relax = layer_values(layer, relax_table)
    row_start = lax.axis_index("gy") * side_cells
    cell_ids = row_start * line_cells + jnp.arange(side_cells * line_cells, dtype=jnp.int32)
    selector = footprint_matches(cell_ids, footprint)
    own_foot = lax.dynamic_slice_in_dim(footprint, lax.axis_index("gy") * own_piers, own_piers, 0)
    for time_step in range(STEPS):
        padded = with_faces(stress)
        velocity = move_velocity(velocity, padded, buoyancy)
        vertical = velocity[2].reshape(depth_cells, side_cells * line_cells)
        piece = lax.all_gather(velocity[2], "gy", axis=1, tiled=True)
        count = piece.shape[1]
        piece_ids = jnp.arange(count * line_cells, dtype=jnp.int32)
        picks = footprint_matches(piece_ids, own_foot)
        flat = piece.reshape(depth_cells, count * line_cells)
        summed = jnp.dot(
            flat, picks, precision=lax.Precision.HIGHEST, preferred_element_type=jnp.float32
        )
        mean_speed = summed / FOOT
        force = impedance[None, :] * (pier_velocity - mean_speed)
        pier_velocity = pier_velocity - pier_gain * force
        all_force = lax.all_gather(force, "gy", axis=1, tiled=True)
        pushed = jnp.dot(
            all_force,
            selector.T,
            precision=lax.Precision.HIGHEST,
            preferred_element_type=jnp.float32,
        )
        vertical = vertical + soil_gain * pushed
        velocity = jnp.stack(
            [velocity[0], velocity[1], vertical.reshape(depth_cells, side_cells, line_cells)]
        )
        velocity = damp_columns(velocity, damp_inverse)
        padded = with_faces(velocity)
        stress = move_stress(stress, padded, lame_first, shear_mod, relax)
    return (velocity, stress, pier_velocity)


SIDE = 4
LANES = 128
ROWS = 8
MESH = pl.DeviceIdType.MESH
Z_GHOSTS = ((2, -1), (4, 1), (5, 1))
Y_GHOSTS = ((1, -1), (3, 1), (5, 1))


def shift_x(a, ahead):
    lane = lax.broadcasted_iota(jnp.int32, a.shape, 1)
    width = a.shape[1]
    if ahead:
        return jnp.where(lane == width - 1, 0.0, pltpu.roll(a, width - 1, 1))
    return jnp.where(lane == 0, 0.0, pltpu.roll(a, 1, 1))


def fused(
    n, ng, v_hbm, s_hbm, b_hbm, layer_ref, lame_ref, shear_ref, relax_ref, foot_ref, w_ref, imp_ref, damp_ref,
    v_out, s_out, w_out,
    v_ext, s_ext, buoy, coef, acc, pin, pout, um, wbuf, square, sg_send, sg_recv, yg_send, yg_recv,
    load_sem, zs_send, zs_recv, cf_send, cf_recv, ys_send, ys_recv,
    f_send, f_recv, r_send, r_recv, u_send, u_recv, y_send, y_recv, o_sem,
):
    me = lax.axis_index("gx")
    g = lax.axis_index("gy")
    depth, side, line = buoy.shape
    tiles = line // LANES
    inner = pl.ds(ROWS, side)

    def piece(j):
        return (
            pl.ds(pl.multiple_of((j // tiles) * ROWS, ROWS), ROWS),
            pl.ds(pl.multiple_of((j % tiles) * LANES, LANES), LANES),
        )

    loads = {}
    for slot, f in enumerate((1, 3, 5, 2, 4, 0)):
        loads[("s", f)] = pltpu.make_async_copy(
            s_hbm.at[f], s_ext.at[f, pl.ds(1, depth), inner, :], load_sem.at[slot]
        )
    loads["b"] = pltpu.make_async_copy(b_hbm, buoy, load_sem.at[6])
    for f in range(3):
        loads[("v", f)] = pltpu.make_async_copy(
            v_hbm.at[f], v_ext.at[f, pl.ds(1, depth), inner, :], load_sem.at[7 + f]
        )
    for copy in loads.values():
        copy.start()

    plane = jnp.zeros((side, line), jnp.float32)
    for f, way in Z_GHOSTS:
        s_ext[f, 0 if way < 0 else depth + 1, inner, :] = plane
    edge = jnp.zeros((ROWS, line), jnp.float32)

    def clear(k, carry):
        for f, way in Y_GHOSTS:
            s_ext[f, k, pl.ds(0 if way < 0 else ROWS + side, ROWS), :] = edge
        for f in range(3 * STEPS):
            v_ext[f, k, pl.ds(0, ROWS), :] = edge
            v_ext[f, k, pl.ds(ROWS + side, ROWS), :] = edge
        return carry

    lax.fori_loop(0, depth + 2, clear, 0)
    for k in range(depth):
        for c, table in enumerate((lame_ref, shear_ref, relax_ref)):
            coef[c, k + 1] = jnp.full((ROWS, LANES), table[layer_ref[k]], jnp.float32)
    for c in range(3):
        coef[c, 0] = jnp.zeros((ROWS, LANES), jnp.float32)
        coef[c, depth + 1] = jnp.zeros((ROWS, LANES), jnp.float32)
        pout[c, 0] = jnp.zeros((ROWS, LANES), jnp.float32)
        pout[c, n * depth + 1] = jnp.zeros((ROWS, LANES), jnp.float32)

    barrier = pltpu.get_barrier_semaphore()
    for d in range(1, n):
        pl.semaphore_signal(
            barrier, inc=1, device_id=(lax.rem(me + d, n), g), device_id_type=MESH
        )
    for d in range(1, ng):
        pl.semaphore_signal(
            barrier, inc=1, device_id=(me, lax.rem(g + d, ng)), device_id_type=MESH
        )
    pl.semaphore_wait(barrier, n - 1 + ng - 1)

    def z_copy(i):
        f, way = Z_GHOSTS[i]
        return pltpu.make_async_remote_copy(
            src_ref=s_hbm.at[f, depth - 1 if way < 0 else 0],
            dst_ref=s_ext.at[f, 0 if way < 0 else depth + 1, inner, :],
            send_sem=zs_send.at[i],
            recv_sem=zs_recv.at[i],
            device_id=(me - way, g),
            device_id_type=MESH,
        )

    def c_copy(way):
        i = (way + 1) // 2
        return pltpu.make_async_remote_copy(
            src_ref=coef.at[:, depth if way < 0 else 1],
            dst_ref=coef.at[:, 0 if way < 0 else depth + 1],
            send_sem=cf_send.at[i],
            recv_sem=cf_recv.at[i],
            device_id=(me - way, g),
            device_id_type=MESH,
        )

    def y_stress(i):
        f, way = Y_GHOSTS[i]
        return pltpu.make_async_remote_copy(
            src_ref=sg_send.at[i],
            dst_ref=sg_recv.at[i],
            send_sem=ys_send.at[i],
            recv_sem=ys_recv.at[i],
            device_id=(me, g - way),
            device_id_type=MESH,
        )

    not_ends = {
        -1: (me > 0, me < n - 1, g > 0, g < ng - 1),
        1: (me < n - 1, me > 0, g < ng - 1, g > 0),
    }

    for i, (f, way) in enumerate(Z_GHOSTS):
        @pl.when(not_ends[way][1])
        def _(i=i):
            z_copy(i).start()
    for way in (-1, 1):
        @pl.when(not_ends[way][1])
        def _(way=way):
            c_copy(way).start()
    for i, (f, way) in enumerate(Y_GHOSTS):
        loads[("s", f)].wait()
        sg_send[i] = s_ext[f, pl.ds(1, depth), ROWS + side - 1 if way < 0 else ROWS, :]

        @pl.when(not_ends[way][3])
        def _(i=i):
            y_stress(i).start()
    for key, copy in loads.items():
        if key not in (("s", 1), ("s", 3), ("s", 5)):
            copy.wait()

    ids = lax.broadcasted_iota(jnp.int32, (side, LANES), 0) + g * side
    by_lane = lax.broadcasted_iota(jnp.int32, (side, LANES), 1)
    by_row = lax.broadcasted_iota(jnp.int32, (LANES, LANES), 0)
    first = jnp.full((side, LANES), -64, jnp.int32)
    begin = jnp.full((LANES, LANES), -64, jnp.int32)
    for p in range(foot_ref.shape[0]):
        first = jnp.where(by_lane == p, foot_ref[p, 0] // line, first)
        begin = jnp.where(by_row == p, foot_ref[p, 0] % line, begin)
    in_rows = jnp.where((ids >= first) & (ids < first + SIDE), 1.0, 0.0)
    across = lax.broadcasted_iota(jnp.int32, (LANES, line), 1)
    start = jnp.concatenate([begin] * tiles, axis=1)
    in_cols = jnp.where((across >= start) & (across < start + SIDE), 1.0, 0.0)

    for i, (f, way) in enumerate(Z_GHOSTS):
        @pl.when(not_ends[way][0])
        def _(i=i):
            z_copy(i).wait_recv()

        @pl.when(not_ends[way][1])
        def _(i=i):
            z_copy(i).wait_send()
    for way in (-1, 1):
        @pl.when(not_ends[way][0])
        def _(way=way):
            c_copy(way).wait_recv()

        @pl.when(not_ends[way][1])
        def _(way=way):
            c_copy(way).wait_send()
    for i, (f, way) in enumerate(Y_GHOSTS):
        @pl.when(not_ends[way][2])
        def _(i=i, f=f, way=way):
            y_stress(i).wait_recv()
            s_ext[f, pl.ds(1, depth), ROWS - 1 if way < 0 else ROWS + side, :] = sg_recv[i]

        @pl.when(not_ends[way][3])
        def _(i=i):
            y_stress(i).wait_send()

    def cells(ref, f, k, shift=0, begin=ROWS, rows=None):
        return ref[f, k, pl.ds(begin + shift, side if rows is None else rows), :]

    base = [0]

    def own_w():
        own = w_ref.shape[0]
        square[...] = jnp.zeros((LANES, LANES), jnp.float32)
        square[pl.ds(0, own), pl.ds(0, depth)] = w_ref[...]
        return pltpu.roll(jnp.transpose(square[...])[0:depth], g * own, 1)

    def own_impedance():
        lane = lax.broadcasted_iota(jnp.int32, (ROWS, LANES), 1)
        values = jnp.zeros((ROWS, LANES), jnp.float32)
        for i in range(imp_ref.shape[0]):
            values = jnp.where(lane == g * imp_ref.shape[0] + i, imp_ref[i], values)
        return values

    def speed_x(i, carry):
        k = i + 1
        xx, xy, xz = cells(s_ext, 0, k), cells(s_ext, 3, k), cells(s_ext, 4, k)
        total = (xx - shift_x(xx, False)) + (cells(s_ext, 3, k, 1) - xy)
        total = total + (cells(s_ext, 4, k + 1) - xz)
        acc[0, i] = cells(v_ext, base[0] + 0, k) + (grid_ratio * buoy[i]) * total
        return carry

    def speed_y(i, carry):
        k = i + 1
        xy, yy, yz = cells(s_ext, 3, k), cells(s_ext, 1, k), cells(s_ext, 5, k)
        total = (shift_x(xy, True) - xy) + (yy - cells(s_ext, 1, k, -1))
        total = total + (cells(s_ext, 5, k + 1) - yz)
        acc[1, i] = cells(v_ext, base[0] + 1, k) + (grid_ratio * buoy[i]) * total
        return carry

    def speed_z(i, carry):
        k = i + 1
        xz, yz, zz = cells(s_ext, 4, k), cells(s_ext, 5, k), cells(s_ext, 2, k)
        total = (shift_x(xz, True) - xz) + (cells(s_ext, 5, k, 1) - yz)
        total = total + (zz - cells(s_ext, 2, k - 1))
        acc[2, i] = cells(v_ext, base[0] + 2, k) + (grid_ratio * buoy[i]) * total
        return carry

    def wide(c, k, rows):
        tile = jnp.concatenate([coef[c, k]] * tiles, axis=1)
        return jnp.concatenate([tile] * (rows // ROWS), axis=0)

    def normals(k, begin, rows, which=(0, 1, 2)):
        at = functools.partial(cells, begin=begin, rows=rows)
        lame, shear, relax = (wide(c, k, rows) for c in range(3))
        vx, vy, vz = at(v_ext, base[0] + 0, k), at(v_ext, base[0] + 1, k), at(v_ext, base[0] + 2, k)
        ex = shift_x(vx, True) - vx
        ey = at(v_ext, base[0] + 1, k, 1) - vy
        ez = at(v_ext, base[0] + 2, k + 1) - vz
        modulus = lame + 2.0 * shear
        for f in which:
            own, others = ((ex, ey + ez), (ey, ex + ez), (ez, ex + ey))[f]
            s_ext[f, k, pl.ds(begin, rows), :] = relax * at(s_ext, f, k) + grid_ratio * (
                modulus * own + lame * others
            )

    def shears(k, begin, rows, which):
        at = functools.partial(cells, begin=begin, rows=rows)
        shear, relax = grid_ratio * wide(1, k, rows), wide(2, k, rows)
        for f in which:
            if f == 3:
                vy = at(v_ext, base[0] + 1, k)
                strain = (at(v_ext, base[0] + 0, k) - at(v_ext, base[0] + 0, k, -1)) + (vy - shift_x(vy, False))
            elif f == 4:
                vz = at(v_ext, base[0] + 2, k)
                strain = (at(v_ext, base[0] + 0, k) - at(v_ext, base[0] + 0, k - 1)) + (vz - shift_x(vz, False))
            else:
                strain = (at(v_ext, base[0] + 1, k) - at(v_ext, base[0] + 1, k - 1)) + (
                    at(v_ext, base[0] + 2, k) - at(v_ext, base[0] + 2, k, -1)
                )
            s_ext[f, k, pl.ds(begin, rows), :] = relax * at(s_ext, f, k) + shear * strain

    def there(step, f, d):
        t = lax.rem(me + d, n)
        ys, xs = piece(t)
        src = acc.at[f, :, ys, xs]
        dst = pin.at[f, pl.ds(me * depth, depth)]
        if d == 0:
            return pltpu.make_async_copy(src, dst, f_recv.at[step, f])
        return pltpu.make_async_remote_copy(
            src_ref=src, dst_ref=dst, send_sem=f_send.at[step, f],
            recv_sem=f_recv.at[step, f], device_id=(t, g), device_id_type=MESH,
        )

    def back(step, f, d):
        t = lax.rem(me + d, n)
        ys, xs = pl.ds(pl.multiple_of((me // tiles) * ROWS + ROWS, ROWS), ROWS), piece(me)[1]
        last = step == STEPS - 1
        low, count = (1 if last and f == 2 else 0), depth + (1 if last else 2)
        src = pout.at[f, pl.ds(t * depth + low, count)]
        dst = v_ext.at[3 * step + f, pl.ds(low, count), ys, xs]
        if d == 0:
            return pltpu.make_async_copy(src, dst, r_recv.at[step, f])
        return pltpu.make_async_remote_copy(
            src_ref=src, dst_ref=dst, send_sem=r_send.at[step, f],
            recv_sem=r_recv.at[step, f], device_id=(t, g), device_id_type=MESH,
        )

    def start_all(make, step, f):
        for d in list(range(1, n)) + [0]:
            make(step, f, d).start()

    def settle(ref, sem):
        pltpu.make_async_copy(ref, ref, sem).wait()

    def planes_back(step, f):
        last = step == STEPS - 1
        return (1 if last and f == 2 else 0), depth + (1 if last else 2)

    def sent_there(step, f):
        settle(pin.at[f, pl.ds(0, (n - 1) * depth)], f_send.at[step, f])

    def got_there(step, f):
        settle(pin.at[f], f_recv.at[step, f])

    def sent_back(step, f):
        settle(pout.at[f, pl.ds(0, (n - 1) * planes_back(step, f)[1])], r_send.at[step, f])

    def got_back(step, f):
        low, count = planes_back(step, f)
        settle(v_ext.at[3 * step + f, pl.ds(low, count), inner, :], r_recv.at[step, f])

    def share(step, d):
        return pltpu.make_async_remote_copy(
            src_ref=um.at[step, 0], dst_ref=um.at[step, d],
            send_sem=u_send.at[step, d], recv_sem=u_recv.at[step, d],
            device_id=(me, lax.rem(g + d, ng)), device_id_type=MESH,
        )

    def y_speed(step, f, i):
        return pltpu.make_async_remote_copy(
            src_ref=yg_send.at[step, f, i], dst_ref=yg_recv.at[step, f, i],
            send_sem=y_send.at[step, f, i], recv_sem=y_recv.at[step, f, i],
            device_id=(me, g + 1 - 2 * i), device_id_type=MESH,
        )

    has_next, has_last = g < ng - 1, g > 0
    planes = pl.ds(0, depth + 2)

    def stress_xy():
        def at(i, carry):
            shears(i + 1, ROWS, ROWS + side, (3,))
            return carry

        lax.fori_loop(0, depth, at, 0)

        @pl.when(g == ng - 1)
        def _():
            s_ext[3, planes, ROWS + side, :] = jnp.zeros((depth + 2, line), jnp.float32)

    def stress_xz():
        def at(i, carry):
            normals(i + 1, ROWS, side, (0,))
            shears(i + 1, ROWS, side, (4,))
            return carry

        lax.fori_loop(0, depth, at, 0)
        shears(depth + 1, ROWS, side, (4,))

    def stress_yz():
        def at(i, carry):
            normals(i + 1, 0, ROWS + side, (1,))
            shears(i + 1, ROWS, ROWS + side, (5,))
            return carry

        lax.fori_loop(0, depth, at, 0)
        shears(depth + 1, ROWS, side, (5,))

        @pl.when(g == 0)
        def _():
            s_ext[1, planes, ROWS - 1, :] = jnp.zeros((depth + 2, line), jnp.float32)

        @pl.when(g == ng - 1)
        def _():
            s_ext[5, planes, ROWS + side, :] = jnp.zeros((depth + 2, line), jnp.float32)

    def stress_zz():
        def at(i, carry):
            normals(i, ROWS, side, (2,))
            return carry

        lax.fori_loop(0, depth + 1, at, 0)

    def v_copy(f):
        return pltpu.make_async_copy(
            v_ext.at[3 * (STEPS - 1) + f, pl.ds(1, depth), inner, :], v_out.at[f], o_sem.at[f]
        )

    def out_copy(f):
        return pltpu.make_async_copy(
            s_ext.at[f, pl.ds(1, depth), inner, :], s_out.at[f], o_sem.at[3 + f]
        )

    def arrive(f, step):
        got_back(step, f)
        yg_send[step, f, 0] = v_ext[3 * step + f, planes, ROWS + side - 1, :]
        yg_send[step, f, 1] = v_ext[3 * step + f, planes, ROWS, :]

        @pl.when(has_next)
        def _():
            y_speed(step, f, 0).start()

        @pl.when(has_last)
        def _():
            y_speed(step, f, 1).start()
        if step == STEPS - 1:
            v_copy(f).start()

    def edges(f, step):
        @pl.when(has_last)
        def _():
            y_speed(step, f, 0).wait_recv()
            v_ext[3 * step + f, planes, ROWS - 1, :] = yg_recv[step, f, 0]
            y_speed(step, f, 1).wait_send()

        @pl.when(has_next)
        def _():
            y_speed(step, f, 1).wait_recv()
            v_ext[3 * step + f, planes, ROWS + side, :] = yg_recv[step, f, 1]
            y_speed(step, f, 0).wait_send()

    for step in range(STEPS):
        if step > 0:
            for f in range(3):
                sent_there(step - 1, f)
        if step > 0:
            stress_xz()
        lax.fori_loop(0, depth, speed_x, 0)
        start_all(there, step, 0)
        if step > 0:
            edges(2, step - 1)
            stress_yz()
        lax.fori_loop(0, depth, speed_y, 0)
        start_all(there, step, 1)
        if step > 0:
            stress_zz()
        lax.fori_loop(0, depth, speed_z, 0)
        flat = acc[2].reshape(depth * side, line)
        part = lax.dot_general(
            flat, in_cols, (((1,), (1,)), ((), ())),
            precision=lax.Precision.HIGHEST, preferred_element_type=jnp.float32,
        ).reshape(depth, side, LANES)
        um[step, 0, pl.ds(0, depth), :] = jnp.sum(part * in_rows[None], axis=1)
        um[step, 0, pl.ds(depth, depth), :] = own_w()
        um[step, 0, pl.ds(2 * depth, ROWS), :] = own_impedance()
        for d in range(1, ng):
            share(step, d).start()
        for d in range(1, ng):
            share(step, d).wait()
        every = um[step, 0]
        for d in range(1, ng):
            every = every + um[step, d]
        w = every[depth : 2 * depth] if step == 0 else wbuf[...]
        force = every[2 * depth : 2 * depth + 1] * (w - every[0:depth] / FOOT)
        wbuf[...] = w - pier_gain * force
        spread = (force[:, None, :] * in_rows[None]).reshape(depth * side, LANES)
        pushed = jnp.dot(
            spread, in_cols, precision=lax.Precision.HIGHEST, preferred_element_type=jnp.float32
        )
        acc[2] = acc[2] + soil_gain * pushed.reshape(depth, side, line)
        start_all(there, step, 2)

        for f in range(3):
            got_there(step, f)
            if step > 0:
                sent_back(step - 1, f)
            full = jnp.concatenate([pin[f, :, y, :] for y in range(ROWS)], axis=1)
            damped = jnp.dot(
                damp_ref[...], full, precision=lax.Precision.HIGHEST,
                preferred_element_type=jnp.float32,
            )
            for y in range(ROWS):
                pout[f, pl.ds(1, n * depth), y, :] = damped[:, y * LANES : (y + 1) * LANES]
            start_all(back, step, f)
        base[0] = 3 * step
        arrive(0, step)
        arrive(1, step)
        edges(0, step)
        edges(1, step)
        if step < STEPS - 1:
            stress_xy()
            arrive(2, step)
        else:
            def last_xy(i, carry):
                shears(i + 1, ROWS, side, (3,))
                return carry

            def last_rest(i, carry):
                normals(i + 1, ROWS, side)
                shears(i + 1, ROWS, side, (4,))
                return carry

            def last_yz(i, carry):
                shears(i + 1, ROWS, side, (5,))
                return carry

            lax.fori_loop(0, depth, last_xy, 0)
            out_copy(3).start()
            arrive(2, step)
            lax.fori_loop(0, depth, last_rest, 0)
            for f in (0, 1, 2, 4):
                out_copy(f).start()
            edges(2, step)
            lax.fori_loop(0, depth, last_yz, 0)
            out_copy(5).start()

    own = w_ref.shape[0]
    square[...] = jnp.zeros((LANES, LANES), jnp.float32)
    square[pl.ds(0, depth), :] = pltpu.roll(wbuf[...], lax.rem(LANES - g * own, LANES), 1)
    w_out[...] = jnp.transpose(square[...])[0:own, 0:depth]
    for f in range(3):
        sent_there(STEPS - 1, f)
        sent_back(STEPS - 1, f)
    for f in range(3):
        v_copy(f).wait()
    for f in range(6):
        out_copy(f).wait()


def deliver(v_ref, s_ref, w_ref, v_out, s_out, w_out, sem):
    pairs = ((v_ref, v_out), (s_ref, s_out), (w_ref, w_out))
    copies = [pltpu.make_async_copy(a, b, sem.at[i]) for i, (a, b) in enumerate(pairs)]
    for copy in copies:
        copy.start()
    for copy in copies:
        copy.wait()


def fused_body(
    n, ng, velocity, stress, pier_velocity, buoyancy, layer, lame_table, shear_table, relax_table,
    impedance, footprint, damp_inverse,
):
    depth, side, line = buoyancy.shape
    own = pier_velocity.shape[1]
    f32 = jnp.float32
    hbm = pl.BlockSpec(memory_space=pl.ANY)
    vmem = pl.BlockSpec(memory_space=pltpu.VMEM)
    smem = pl.BlockSpec(memory_space=pltpu.SMEM)
    dma = pltpu.SemaphoreType.DMA
    tall = side + 2 * ROWS
    stage = 2 * depth + ROWS
    v, s, w = pl.pallas_call(
        functools.partial(fused, n, ng),
        out_shape=(
            jax.ShapeDtypeStruct(velocity.shape, f32),
            jax.ShapeDtypeStruct(stress.shape, f32),
            jax.ShapeDtypeStruct((own, depth), f32),
        ),
        in_specs=[hbm] * 3 + [smem] * 5 + [vmem, smem, vmem],
        out_specs=(hbm, hbm, vmem),
        scratch_shapes=[
            pltpu.VMEM((3 * STEPS, depth + 2, tall, line), f32),
            pltpu.VMEM((6, depth + 2, tall, line), f32),
            pltpu.VMEM((depth, side, line), f32),
            pltpu.VMEM((3, depth + 2, ROWS, LANES), f32),
            pltpu.VMEM((3, depth, side, line), f32),
            pltpu.VMEM((3, n * depth, ROWS, LANES), f32),
            pltpu.VMEM((3, n * depth + 2, ROWS, LANES), f32),
            pltpu.VMEM((STEPS, ng, stage, LANES), f32),
            pltpu.VMEM((depth, LANES), f32),
            pltpu.VMEM((LANES, LANES), f32),
            pltpu.VMEM((3, depth, line), f32),
            pltpu.VMEM((3, depth, line), f32),
            pltpu.VMEM((STEPS, 3, 2, depth + 2, line), f32),
            pltpu.VMEM((STEPS, 3, 2, depth + 2, line), f32),
            dma((10,)), dma((3,)), dma((3,)), dma((2,)), dma((2,)), dma((3,)), dma((3,)),
            dma((STEPS, 3)), dma((STEPS, 3)), dma((STEPS, 3)), dma((STEPS, 3)),
            dma((STEPS, ng)), dma((STEPS, ng)), dma((STEPS, 3, 2)), dma((STEPS, 3, 2)),
            dma((9,)),
        ],
        compiler_params=pltpu.CompilerParams(
            collective_id=0, has_side_effects=True, vmem_limit_bytes=60 * 1024 * 1024
        ),
    )(
        velocity, stress, buoyancy, layer, lame_table, shear_table, relax_table,
        footprint, pier_velocity.T, impedance, damp_inverse,
    )
    v, s, w = pl.pallas_call(
        deliver,
        out_shape=tuple(jax.ShapeDtypeStruct(a.shape, f32) for a in (v, s, w)),
        in_specs=[hbm] * 3,
        out_specs=(hbm,) * 3,
        scratch_shapes=[dma((3,))],
    )(v, s, w)
    return v, s, w.T


def whole_tiles(mesh, velocity, pier_velocity):
    n, ng = mesh.shape["gx"], mesh.shape["gy"]
    depth, side, line = velocity.shape[1] // n, velocity.shape[2] // ng, velocity.shape[3]
    return (
        line % LANES == 0
        and side % ROWS == 0
        and depth % ROWS == 0
        and (side // ROWS) * (line // LANES) == n
        and pier_velocity.shape[1] <= LANES
    )


def solution(mesh):
    placed = (
        P(None, "gx", "gy", None),
        P(None, "gx", "gy", None),
        P("gx", "gy"),
        P("gx", "gy", None),
        P("gx"),
        P(),
        P(),
        P(),
        P("gy"),
        P(),
        P(),
    )

    def run(*args):
        n, ng = mesh.shape["gx"], mesh.shape["gy"]
        if whole_tiles(mesh, args[0], args[2]):
            part = functools.partial(fused_body, n, ng)
        else:
            part = body
        return mapped(part)(*args)

    def mapped(part):
        return jax.shard_map(
            part,
            mesh=mesh,
            in_specs=placed,
            out_specs=(P(None, "gx", "gy", None), P(None, "gx", "gy", None), P("gx", "gy")),
            check_vma=False,
        )

    return run
```

```python
import functools
import jax
import jax.numpy as jnp
from jax import lax
from jax.experimental import pallas as pl
from jax.experimental.pallas import tpu as pltpu
from jax.sharding import PartitionSpec as P

STEPS = 2
FOOT = 16


grid_ratio = 0.25
soil_gain = 0.2
pier_gain = 0.5


def extended(cells, sides, width):
    for axis, dim in sides:
        count = lax.axis_size(axis)
        ends = count - 1
        head = lax.slice_in_dim(cells, 0, width, axis=dim)
        tail = lax.slice_in_dim(cells, cells.shape[dim] - width, cells.shape[dim], axis=dim)
        cells = jnp.concatenate(
            [
                lax.ppermute(tail, axis, [(i, (i + 1) % count) for i in range(ends)]),
                cells,
                lax.ppermute(head, axis, [((i + 1) % count, i) for i in range(ends)]),
            ],
            axis=dim,
        )
    return cells


def forward_diff(padded, along):
    center = padded[1:-1, 1:-1, 1:-1]
    if along == 0:
        return padded[2:, 1:-1, 1:-1] - center
    if along == 1:
        return padded[1:-1, 2:, 1:-1] - center
    return padded[1:-1, 1:-1, 2:] - center


def backward_diff(padded, along):
    center = padded[1:-1, 1:-1, 1:-1]
    if along == 0:
        return center - padded[:-2, 1:-1, 1:-1]
    if along == 1:
        return center - padded[1:-1, :-2, 1:-1]
    return center - padded[1:-1, 1:-1, :-2]


def move_velocity(velocity, padded, buoyancy):
    scaled = grid_ratio * buoyancy
    first = velocity[0] + scaled * (
        backward_diff(padded[0], 2) + forward_diff(padded[3], 1) + forward_diff(padded[4], 0)
    )
    second = velocity[1] + scaled * (
        forward_diff(padded[3], 2) + backward_diff(padded[1], 1) + forward_diff(padded[5], 0)
    )
    third = velocity[2] + scaled * (
        forward_diff(padded[4], 2) + forward_diff(padded[5], 1) + backward_diff(padded[2], 0)
    )
    return jnp.stack([first, second, third])


def move_stress(stress, padded, lame_first, shear_mod, relax):
    strain_x = forward_diff(padded[0], 2)
    strain_y = forward_diff(padded[1], 1)
    strain_z = forward_diff(padded[2], 0)
    modulus = lame_first + 2.0 * shear_mod
    normal_x = relax * stress[0] + grid_ratio * (
        modulus * strain_x + lame_first * (strain_y + strain_z)
    )
    normal_y = relax * stress[1] + grid_ratio * (
        modulus * strain_y + lame_first * (strain_x + strain_z)
    )
    normal_z = relax * stress[2] + grid_ratio * (
        modulus * strain_z + lame_first * (strain_x + strain_y)
    )
    shear_xy = relax * stress[3] + grid_ratio * shear_mod * (
        backward_diff(padded[0], 1) + backward_diff(padded[1], 2)
    )
    shear_xz = relax * stress[4] + grid_ratio * shear_mod * (
        backward_diff(padded[0], 0) + backward_diff(padded[2], 2)
    )
    shear_yz = relax * stress[5] + grid_ratio * shear_mod * (
        backward_diff(padded[1], 0) + backward_diff(padded[2], 1)
    )
    return jnp.stack([normal_x, normal_y, normal_z, shear_xy, shear_xz, shear_yz])


def layer_values(layer, table):
    levels = jnp.arange(table.shape[0], dtype=jnp.int32)
    onehot = (layer[:, None] == levels[None, :]).astype(table.dtype)
    return jnp.sum(onehot * table[None, :], axis=1)[:, None, None]


def with_faces(fields):
    padded = extended(fields, (("gx", 1), ("gy", 2)), 1)
    return jnp.pad(padded, ((0, 0), (0, 0), (0, 0), (1, 1)))


def footprint_matches(cell_ids, footprint):
    piers = footprint.shape[0]
    equal = (cell_ids[:, None] == footprint.reshape(-1)[None, :]).astype(jnp.float32)
    return jnp.sum(equal.reshape(cell_ids.shape[0], piers, FOOT), axis=2)


def damp_columns(velocity, inverse):
    pencils = lax.all_to_all(velocity, "gx", split_axis=3, concat_axis=1, tiled=True)
    shape = pencils.shape
    flat = pencils.reshape(shape[0], shape[1], shape[2] * shape[3])
    damped = jnp.einsum("zk,fkm->fzm", inverse, flat, precision=lax.Precision.HIGHEST).reshape(
        shape
    )
    return lax.all_to_all(damped, "gx", split_axis=1, concat_axis=3, tiled=True)


def body(
    velocity,
    stress,
    pier_velocity,
    buoyancy,
    layer,
    lame_table,
    shear_table,
    relax_table,
    impedance,
    footprint,
    damp_inverse,
):
    depth_cells, side_cells, line_cells = (velocity.shape[1], velocity.shape[2], velocity.shape[3])
    own_piers = pier_velocity.shape[1]
    lame_first = layer_values(layer, lame_table)
    shear_mod = layer_values(layer, shear_table)
    relax = layer_values(layer, relax_table)
    row_start = lax.axis_index("gy") * side_cells
    cell_ids = row_start * line_cells + jnp.arange(side_cells * line_cells, dtype=jnp.int32)
    selector = footprint_matches(cell_ids, footprint)
    own_foot = lax.dynamic_slice_in_dim(footprint, lax.axis_index("gy") * own_piers, own_piers, 0)
    for time_step in range(STEPS):
        padded = with_faces(stress)
        velocity = move_velocity(velocity, padded, buoyancy)
        vertical = velocity[2].reshape(depth_cells, side_cells * line_cells)
        piece = lax.all_gather(velocity[2], "gy", axis=1, tiled=True)
        count = piece.shape[1]
        piece_ids = jnp.arange(count * line_cells, dtype=jnp.int32)
        picks = footprint_matches(piece_ids, own_foot)
        flat = piece.reshape(depth_cells, count * line_cells)
        summed = jnp.dot(
            flat, picks, precision=lax.Precision.HIGHEST, preferred_element_type=jnp.float32
        )
        mean_speed = summed / FOOT
        force = impedance[None, :] * (pier_velocity - mean_speed)
        pier_velocity = pier_velocity - pier_gain * force
        all_force = lax.all_gather(force, "gy", axis=1, tiled=True)
        pushed = jnp.dot(
            all_force,
            selector.T,
            precision=lax.Precision.HIGHEST,
            preferred_element_type=jnp.float32,
        )
        vertical = vertical + soil_gain * pushed
        velocity = jnp.stack(
            [velocity[0], velocity[1], vertical.reshape(depth_cells, side_cells, line_cells)]
        )
        velocity = damp_columns(velocity, damp_inverse)
        padded = with_faces(velocity)
        stress = move_stress(stress, padded, lame_first, shear_mod, relax)
    return (velocity, stress, pier_velocity)


SIDE = 4
LANES = 128
ROWS = 8
MESH = pl.DeviceIdType.MESH
Z_GHOSTS = ((2, -1), (4, 1), (5, 1))
Y_GHOSTS = ((1, -1), (3, 1), (5, 1))


def shift_x(a, ahead):
    lane = lax.broadcasted_iota(jnp.int32, a.shape, 1)
    width = a.shape[1]
    if ahead:
        return jnp.where(lane == width - 1, 0.0, pltpu.roll(a, width - 1, 1))
    return jnp.where(lane == 0, 0.0, pltpu.roll(a, 1, 1))


def fused(
    n, ng, v_hbm, s_hbm, b_hbm, layer_ref, lame_ref, shear_ref, relax_ref, foot_ref, w_ref, imp_ref, damp_ref,
    v_ext, s_ext, w_out,
    buoy, coef, acc, pin, pout, um, wbuf, square, sg_send, sg_recv, yg_send, yg_recv,
    load_sem, zs_send, zs_recv, cf_send, cf_recv, ys_send, ys_recv,
    f_send, f_recv, r_send, r_recv, u_send, u_recv, y_send, y_recv,
):
    me = lax.axis_index("gx")
    g = lax.axis_index("gy")
    depth, side, line = buoy.shape
    tiles = line // LANES
    inner = pl.ds(ROWS, side)

    def piece(j):
        return (
            pl.ds(pl.multiple_of((j // tiles) * ROWS, ROWS), ROWS),
            pl.ds(pl.multiple_of((j % tiles) * LANES, LANES), LANES),
        )

    loads = {}
    for slot, f in enumerate((1, 3, 5, 2, 4, 0)):
        loads[("s", f)] = pltpu.make_async_copy(
            s_hbm.at[f], s_ext.at[f, pl.ds(1, depth), inner, :], load_sem.at[slot]
        )
    loads["b"] = pltpu.make_async_copy(b_hbm, buoy, load_sem.at[6])
    for f in range(3):
        loads[("v", f)] = pltpu.make_async_copy(
            v_hbm.at[f], v_ext.at[f, pl.ds(1, depth), inner, :], load_sem.at[7 + f]
        )
    for copy in loads.values():
        copy.start()

    plane = jnp.zeros((side, line), jnp.float32)
    for f, way in Z_GHOSTS:
        s_ext[f, 0 if way < 0 else depth + 1, inner, :] = plane
    edge = jnp.zeros((ROWS, line), jnp.float32)

    def clear(k, carry):
        for f, way in Y_GHOSTS:
            s_ext[f, k, pl.ds(0 if way < 0 else ROWS + side, ROWS), :] = edge
        for f in range(3 * STEPS):
            v_ext[f, k, pl.ds(0, ROWS), :] = edge
            v_ext[f, k, pl.ds(ROWS + side, ROWS), :] = edge
        return carry

    lax.fori_loop(0, depth + 2, clear, 0)
    for k in range(depth):
        for c, table in enumerate((lame_ref, shear_ref, relax_ref)):
            coef[c, k + 1] = jnp.full((ROWS, LANES), table[layer_ref[k]], jnp.float32)
    for c in range(3):
        coef[c, 0] = jnp.zeros((ROWS, LANES), jnp.float32)
        coef[c, depth + 1] = jnp.zeros((ROWS, LANES), jnp.float32)
        pout[c, 0] = jnp.zeros((ROWS, LANES), jnp.float32)
        pout[c, n * depth + 1] = jnp.zeros((ROWS, LANES), jnp.float32)

    barrier = pltpu.get_barrier_semaphore()
    for d in range(1, n):
        pl.semaphore_signal(
            barrier, inc=1, device_id=(lax.rem(me + d, n), g), device_id_type=MESH
        )
    for d in range(1, ng):
        pl.semaphore_signal(
            barrier, inc=1, device_id=(me, lax.rem(g + d, ng)), device_id_type=MESH
        )
    pl.semaphore_wait(barrier, n - 1 + ng - 1)

    def z_copy(i):
        f, way = Z_GHOSTS[i]
        return pltpu.make_async_remote_copy(
            src_ref=s_hbm.at[f, depth - 1 if way < 0 else 0],
            dst_ref=s_ext.at[f, 0 if way < 0 else depth + 1, inner, :],
            send_sem=zs_send.at[i],
            recv_sem=zs_recv.at[i],
            device_id=(me - way, g),
            device_id_type=MESH,
        )

    def c_copy(way):
        i = (way + 1) // 2
        return pltpu.make_async_remote_copy(
            src_ref=coef.at[:, depth if way < 0 else 1],
            dst_ref=coef.at[:, 0 if way < 0 else depth + 1],
            send_sem=cf_send.at[i],
            recv_sem=cf_recv.at[i],
            device_id=(me - way, g),
            device_id_type=MESH,
        )

    def y_stress(i):
        f, way = Y_GHOSTS[i]
        return pltpu.make_async_remote_copy(
            src_ref=sg_send.at[i],
            dst_ref=sg_recv.at[i],
            send_sem=ys_send.at[i],
            recv_sem=ys_recv.at[i],
            device_id=(me, g - way),
            device_id_type=MESH,
        )

    not_ends = {
        -1: (me > 0, me < n - 1, g > 0, g < ng - 1),
        1: (me < n - 1, me > 0, g < ng - 1, g > 0),
    }

    for i, (f, way) in enumerate(Z_GHOSTS):
        @pl.when(not_ends[way][1])
        def _(i=i):
            z_copy(i).start()
    for way in (-1, 1):
        @pl.when(not_ends[way][1])
        def _(way=way):
            c_copy(way).start()
    for i, (f, way) in enumerate(Y_GHOSTS):
        loads[("s", f)].wait()
        sg_send[i] = s_ext[f, pl.ds(1, depth), ROWS + side - 1 if way < 0 else ROWS, :]

        @pl.when(not_ends[way][3])
        def _(i=i):
            y_stress(i).start()
    for key, copy in loads.items():
        if key not in (("s", 1), ("s", 3), ("s", 5)):
            copy.wait()

    ids = lax.broadcasted_iota(jnp.int32, (side, LANES), 0) + g * side
    by_lane = lax.broadcasted_iota(jnp.int32, (side, LANES), 1)
    by_row = lax.broadcasted_iota(jnp.int32, (LANES, LANES), 0)
    first = jnp.full((side, LANES), -64, jnp.int32)
    begin = jnp.full((LANES, LANES), -64, jnp.int32)
    for p in range(foot_ref.shape[0]):
        first = jnp.where(by_lane == p, foot_ref[p, 0] // line, first)
        begin = jnp.where(by_row == p, foot_ref[p, 0] % line, begin)
    in_rows = jnp.where((ids >= first) & (ids < first + SIDE), 1.0, 0.0)
    across = lax.broadcasted_iota(jnp.int32, (LANES, line), 1)
    start = jnp.concatenate([begin] * tiles, axis=1)
    in_cols = jnp.where((across >= start) & (across < start + SIDE), 1.0, 0.0)

    for i, (f, way) in enumerate(Z_GHOSTS):
        @pl.when(not_ends[way][0])
        def _(i=i):
            z_copy(i).wait_recv()

        @pl.when(not_ends[way][1])
        def _(i=i):
            z_copy(i).wait_send()
    for way in (-1, 1):
        @pl.when(not_ends[way][0])
        def _(way=way):
            c_copy(way).wait_recv()

        @pl.when(not_ends[way][1])
        def _(way=way):
            c_copy(way).wait_send()
    for i, (f, way) in enumerate(Y_GHOSTS):
        @pl.when(not_ends[way][2])
        def _(i=i, f=f, way=way):
            y_stress(i).wait_recv()
            s_ext[f, pl.ds(1, depth), ROWS - 1 if way < 0 else ROWS + side, :] = sg_recv[i]

        @pl.when(not_ends[way][3])
        def _(i=i):
            y_stress(i).wait_send()

    def cells(ref, f, k, shift=0, begin=ROWS, rows=None):
        return ref[f, k, pl.ds(begin + shift, side if rows is None else rows), :]

    base = [0]

    def own_w():
        own = w_ref.shape[0]
        square[...] = jnp.zeros((LANES, LANES), jnp.float32)
        square[pl.ds(0, own), pl.ds(0, depth)] = w_ref[...]
        return pltpu.roll(jnp.transpose(square[...])[0:depth], g * own, 1)

    def own_impedance():
        lane = lax.broadcasted_iota(jnp.int32, (ROWS, LANES), 1)
        values = jnp.zeros((ROWS, LANES), jnp.float32)
        for i in range(imp_ref.shape[0]):
            values = jnp.where(lane == g * imp_ref.shape[0] + i, imp_ref[i], values)
        return values

    def speed_x(i, carry):
        k = i + 1
        xx, xy, xz = cells(s_ext, 0, k), cells(s_ext, 3, k), cells(s_ext, 4, k)
        total = (xx - shift_x(xx, False)) + (cells(s_ext, 3, k, 1) - xy)
        total = total + (cells(s_ext, 4, k + 1) - xz)
        acc[0, i] = cells(v_ext, base[0] + 0, k) + (grid_ratio * buoy[i]) * total
        return carry

    def speed_y(i, carry):
        k = i + 1
        xy, yy, yz = cells(s_ext, 3, k), cells(s_ext, 1, k), cells(s_ext, 5, k)
        total = (shift_x(xy, True) - xy) + (yy - cells(s_ext, 1, k, -1))
        total = total + (cells(s_ext, 5, k + 1) - yz)
        acc[1, i] = cells(v_ext, base[0] + 1, k) + (grid_ratio * buoy[i]) * total
        return carry

    def speed_z(i, carry):
        k = i + 1
        xz, yz, zz = cells(s_ext, 4, k), cells(s_ext, 5, k), cells(s_ext, 2, k)
        total = (shift_x(xz, True) - xz) + (cells(s_ext, 5, k, 1) - yz)
        total = total + (zz - cells(s_ext, 2, k - 1))
        acc[2, i] = cells(v_ext, base[0] + 2, k) + (grid_ratio * buoy[i]) * total
        return carry

    def wide(c, k, rows):
        tile = jnp.concatenate([coef[c, k]] * tiles, axis=1)
        return jnp.concatenate([tile] * (rows // ROWS), axis=0)

    def normals(k, begin, rows, which=(0, 1, 2)):
        at = functools.partial(cells, begin=begin, rows=rows)
        lame, shear, relax = (wide(c, k, rows) for c in range(3))
        vx, vy, vz = at(v_ext, base[0] + 0, k), at(v_ext, base[0] + 1, k), at(v_ext, base[0] + 2, k)
        ex = shift_x(vx, True) - vx
        ey = at(v_ext, base[0] + 1, k, 1) - vy
        ez = at(v_ext, base[0] + 2, k + 1) - vz
        modulus = lame + 2.0 * shear
        for f in which:
            own, others = ((ex, ey + ez), (ey, ex + ez), (ez, ex + ey))[f]
            s_ext[f, k, pl.ds(begin, rows), :] = relax * at(s_ext, f, k) + grid_ratio * (
                modulus * own + lame * others
            )

    def shears(k, begin, rows, which):
        at = functools.partial(cells, begin=begin, rows=rows)
        shear, relax = grid_ratio * wide(1, k, rows), wide(2, k, rows)
        for f in which:
            if f == 3:
                vy = at(v_ext, base[0] + 1, k)
                strain = (at(v_ext, base[0] + 0, k) - at(v_ext, base[0] + 0, k, -1)) + (vy - shift_x(vy, False))
            elif f == 4:
                vz = at(v_ext, base[0] + 2, k)
                strain = (at(v_ext, base[0] + 0, k) - at(v_ext, base[0] + 0, k - 1)) + (vz - shift_x(vz, False))
            else:
                strain = (at(v_ext, base[0] + 1, k) - at(v_ext, base[0] + 1, k - 1)) + (
                    at(v_ext, base[0] + 2, k) - at(v_ext, base[0] + 2, k, -1)
                )
            s_ext[f, k, pl.ds(begin, rows), :] = relax * at(s_ext, f, k) + shear * strain

    def there(step, f, d):
        t = lax.rem(me + d, n)
        ys, xs = piece(t)
        src = acc.at[f, :, ys, xs]
        dst = pin.at[f, pl.ds(me * depth, depth)]
        if d == 0:
            return pltpu.make_async_copy(src, dst, f_recv.at[step, f])
        return pltpu.make_async_remote_copy(
            src_ref=src, dst_ref=dst, send_sem=f_send.at[step, f],
            recv_sem=f_recv.at[step, f], device_id=(t, g), device_id_type=MESH,
        )

    def back(step, f, d):
        t = lax.rem(me + d, n)
        ys, xs = pl.ds(pl.multiple_of((me // tiles) * ROWS + ROWS, ROWS), ROWS), piece(me)[1]
        last = step == STEPS - 1
        low, count = (1 if last and f == 2 else 0), depth + (1 if last else 2)
        src = pout.at[f, pl.ds(t * depth + low, count)]
        dst = v_ext.at[3 * step + f, pl.ds(low, count), ys, xs]
        if d == 0:
            return pltpu.make_async_copy(src, dst, r_recv.at[step, f])
        return pltpu.make_async_remote_copy(
            src_ref=src, dst_ref=dst, send_sem=r_send.at[step, f],
            recv_sem=r_recv.at[step, f], device_id=(t, g), device_id_type=MESH,
        )

    def start_all(make, step, f):
        for d in list(range(1, n)) + [0]:
            make(step, f, d).start()

    def settle(ref, sem):
        pltpu.make_async_copy(ref, ref, sem).wait()

    def planes_back(step, f):
        last = step == STEPS - 1
        return (1 if last and f == 2 else 0), depth + (1 if last else 2)

    def sent_there(step, f):
        settle(pin.at[f, pl.ds(0, (n - 1) * depth)], f_send.at[step, f])

    def got_there(step, f):
        settle(pin.at[f], f_recv.at[step, f])

    def sent_back(step, f):
        settle(pout.at[f, pl.ds(0, (n - 1) * planes_back(step, f)[1])], r_send.at[step, f])

    def got_back(step, f):
        low, count = planes_back(step, f)
        settle(v_ext.at[3 * step + f, pl.ds(low, count), inner, :], r_recv.at[step, f])

    def share(step, d):
        return pltpu.make_async_remote_copy(
            src_ref=um.at[step, 0], dst_ref=um.at[step, d],
            send_sem=u_send.at[step, d], recv_sem=u_recv.at[step, d],
            device_id=(me, lax.rem(g + d, ng)), device_id_type=MESH,
        )

    def y_speed(step, f, i):
        return pltpu.make_async_remote_copy(
            src_ref=yg_send.at[step, f, i], dst_ref=yg_recv.at[step, f, i],
            send_sem=y_send.at[step, f, i], recv_sem=y_recv.at[step, f, i],
            device_id=(me, g + 1 - 2 * i), device_id_type=MESH,
        )

    has_next, has_last = g < ng - 1, g > 0
    planes = pl.ds(0, depth + 2)

    def stress_xy():
        def at(i, carry):
            shears(i + 1, ROWS, ROWS + side, (3,))
            return carry

        lax.fori_loop(0, depth, at, 0)

        @pl.when(g == ng - 1)
        def _():
            s_ext[3, planes, ROWS + side, :] = jnp.zeros((depth + 2, line), jnp.float32)

    def stress_xz():
        def at(i, carry):
            normals(i + 1, ROWS, side, (0,))
            shears(i + 1, ROWS, side, (4,))
            return carry

        lax.fori_loop(0, depth, at, 0)
        shears(depth + 1, ROWS, side, (4,))

    def stress_yz():
        def at(i, carry):
            normals(i + 1, 0, ROWS + side, (1,))
            shears(i + 1, ROWS, ROWS + side, (5,))
            return carry

        lax.fori_loop(0, depth, at, 0)
        shears(depth + 1, ROWS, side, (5,))

        @pl.when(g == 0)
        def _():
            s_ext[1, planes, ROWS - 1, :] = jnp.zeros((depth + 2, line), jnp.float32)

        @pl.when(g == ng - 1)
        def _():
            s_ext[5, planes, ROWS + side, :] = jnp.zeros((depth + 2, line), jnp.float32)

    def stress_zz():
        def at(i, carry):
            normals(i, ROWS, side, (2,))
            return carry

        lax.fori_loop(0, depth + 1, at, 0)

    def arrive(f, step):
        got_back(step, f)
        yg_send[step, f, 0] = v_ext[3 * step + f, planes, ROWS + side - 1, :]
        yg_send[step, f, 1] = v_ext[3 * step + f, planes, ROWS, :]

        @pl.when(has_next)
        def _():
            y_speed(step, f, 0).start()

        @pl.when(has_last)
        def _():
            y_speed(step, f, 1).start()

    def edges(f, step):
        @pl.when(has_last)
        def _():
            y_speed(step, f, 0).wait_recv()
            v_ext[3 * step + f, planes, ROWS - 1, :] = yg_recv[step, f, 0]
            y_speed(step, f, 1).wait_send()

        @pl.when(has_next)
        def _():
            y_speed(step, f, 1).wait_recv()
            v_ext[3 * step + f, planes, ROWS + side, :] = yg_recv[step, f, 1]
            y_speed(step, f, 0).wait_send()

    for step in range(STEPS):
        if step > 0:
            for f in range(3):
                sent_there(step - 1, f)
        if step > 0:
            stress_xz()
        lax.fori_loop(0, depth, speed_x, 0)
        start_all(there, step, 0)
        if step > 0:
            edges(2, step - 1)
            stress_yz()
        lax.fori_loop(0, depth, speed_y, 0)
        start_all(there, step, 1)
        if step > 0:
            stress_zz()
        lax.fori_loop(0, depth, speed_z, 0)
        flat = acc[2].reshape(depth * side, line)
        part = lax.dot_general(
            flat, in_cols, (((1,), (1,)), ((), ())),
            precision=lax.Precision.HIGHEST, preferred_element_type=jnp.float32,
        ).reshape(depth, side, LANES)
        um[step, 0, pl.ds(0, depth), :] = jnp.sum(part * in_rows[None], axis=1)
        um[step, 0, pl.ds(depth, depth), :] = own_w()
        um[step, 0, pl.ds(2 * depth, ROWS), :] = own_impedance()
        for d in range(1, ng):
            share(step, d).start()
        for d in range(1, ng):
            share(step, d).wait()
        every = um[step, 0]
        for d in range(1, ng):
            every = every + um[step, d]
        w = every[depth : 2 * depth] if step == 0 else wbuf[...]
        force = every[2 * depth : 2 * depth + 1] * (w - every[0:depth] / FOOT)
        wbuf[...] = w - pier_gain * force
        spread = (force[:, None, :] * in_rows[None]).reshape(depth * side, LANES)
        pushed = jnp.dot(
            spread, in_cols, precision=lax.Precision.HIGHEST, preferred_element_type=jnp.float32
        )
        acc[2] = acc[2] + soil_gain * pushed.reshape(depth, side, line)
        start_all(there, step, 2)

        for f in range(3):
            got_there(step, f)
            if step > 0:
                sent_back(step - 1, f)
            full = jnp.concatenate([pin[f, :, y, :] for y in range(ROWS)], axis=1)
            damped = jnp.dot(
                damp_ref[...], full, precision=lax.Precision.HIGHEST,
                preferred_element_type=jnp.float32,
            )
            for y in range(ROWS):
                pout[f, pl.ds(1, n * depth), y, :] = damped[:, y * LANES : (y + 1) * LANES]
            start_all(back, step, f)
        base[0] = 3 * step
        arrive(0, step)
        arrive(1, step)
        edges(0, step)
        edges(1, step)
        if step < STEPS - 1:
            stress_xy()
            arrive(2, step)
        else:
            def last_xy(i, carry):
                shears(i + 1, ROWS, side, (3,))
                return carry

            def last_rest(i, carry):
                normals(i + 1, ROWS, side)
                shears(i + 1, ROWS, side, (4,))
                return carry

            def last_yz(i, carry):
                shears(i + 1, ROWS, side, (5,))
                return carry

            lax.fori_loop(0, depth, last_xy, 0)
            arrive(2, step)
            lax.fori_loop(0, depth, last_rest, 0)
            edges(2, step)
            lax.fori_loop(0, depth, last_yz, 0)

    own = w_ref.shape[0]
    square[...] = jnp.zeros((LANES, LANES), jnp.float32)
    square[pl.ds(0, depth), :] = pltpu.roll(wbuf[...], lax.rem(LANES - g * own, LANES), 1)
    w_out[...] = jnp.transpose(square[...])[0:own, 0:depth]
    for f in range(3):
        sent_there(STEPS - 1, f)
        sent_back(STEPS - 1, f)


def deliver(v_ref, s_ref, w_ref, v_out, s_out, w_out, sem):
    depth, side = v_out.shape[1:3]
    inside = pl.ds(1, depth), pl.ds(ROWS, side)
    pairs = (
        (v_ref.at[(pl.ds(3 * (STEPS - 1), 3),) + inside], v_out),
        (s_ref.at[(pl.ds(0, 6),) + inside], s_out),
        (w_ref, w_out),
    )
    copies = [pltpu.make_async_copy(a, b, sem.at[i]) for i, (a, b) in enumerate(pairs)]
    for copy in copies:
        copy.start()
    for copy in copies:
        copy.wait()


def fused_body(
    n, ng, velocity, stress, pier_velocity, buoyancy, layer, lame_table, shear_table, relax_table,
    impedance, footprint, damp_inverse,
):
    depth, side, line = buoyancy.shape
    own = pier_velocity.shape[1]
    f32 = jnp.float32
    hbm = pl.BlockSpec(memory_space=pltpu.HBM)
    vmem = pl.BlockSpec(memory_space=pltpu.VMEM)
    smem = pl.BlockSpec(memory_space=pltpu.SMEM)
    dma = pltpu.SemaphoreType.DMA
    tall = side + 2 * ROWS
    stage = 2 * depth + ROWS
    v, s, w = pl.pallas_call(
        functools.partial(fused, n, ng),
        out_shape=(
            pltpu.VMEM((3 * STEPS, depth + 2, tall, line), f32),
            pltpu.VMEM((6, depth + 2, tall, line), f32),
            pltpu.VMEM((own, depth), f32),
        ),
        in_specs=[hbm] * 3 + [smem] * 5 + [vmem, smem, vmem],
        out_specs=(vmem, vmem, vmem),
        scratch_shapes=[
            pltpu.VMEM((depth, side, line), f32),
            pltpu.VMEM((3, depth + 2, ROWS, LANES), f32),
            pltpu.VMEM((3, depth, side, line), f32),
            pltpu.VMEM((3, n * depth, ROWS, LANES), f32),
            pltpu.VMEM((3, n * depth + 2, ROWS, LANES), f32),
            pltpu.VMEM((STEPS, ng, stage, LANES), f32),
            pltpu.VMEM((depth, LANES), f32),
            pltpu.VMEM((LANES, LANES), f32),
            pltpu.VMEM((3, depth, line), f32),
            pltpu.VMEM((3, depth, line), f32),
            pltpu.VMEM((STEPS, 3, 2, depth + 2, line), f32),
            pltpu.VMEM((STEPS, 3, 2, depth + 2, line), f32),
            dma((10,)), dma((3,)), dma((3,)), dma((2,)), dma((2,)), dma((3,)), dma((3,)),
            dma((STEPS, 3)), dma((STEPS, 3)), dma((STEPS, 3)), dma((STEPS, 3)),
            dma((STEPS, ng)), dma((STEPS, ng)), dma((STEPS, 3, 2)), dma((STEPS, 3, 2)),
        ],
        compiler_params=pltpu.CompilerParams(
            collective_id=0, has_side_effects=True, vmem_limit_bytes=48 * 1024 * 1024
        ),
    )(
        velocity, stress, buoyancy, layer, lame_table, shear_table, relax_table,
        footprint, pier_velocity.T, impedance, damp_inverse,
    )
    v, s, w = pl.pallas_call(
        deliver,
        out_shape=tuple(
            jax.ShapeDtypeStruct(a, f32) for a in (velocity.shape, stress.shape, (own, depth))
        ),
        in_specs=[vmem] * 3,
        out_specs=(hbm,) * 3,
        scratch_shapes=[dma((3,))],
        compiler_params=pltpu.CompilerParams(vmem_limit_bytes=8 * 1024 * 1024),
    )(v, s, w)
    return v, s, w.T


def whole_tiles(mesh, velocity, pier_velocity):
    n, ng = mesh.shape["gx"], mesh.shape["gy"]
    depth, side, line = velocity.shape[1] // n, velocity.shape[2] // ng, velocity.shape[3]
    return (
        line % LANES == 0
        and side % ROWS == 0
        and depth % ROWS == 0
        and (side // ROWS) * (line // LANES) == n
        and pier_velocity.shape[1] <= LANES
    )


def solution(mesh):
    placed = (
        P(None, "gx", "gy", None),
        P(None, "gx", "gy", None),
        P("gx", "gy"),
        P("gx", "gy", None),
        P("gx"),
        P(),
        P(),
        P(),
        P("gy"),
        P(),
        P(),
    )

    def run(*args):
        n, ng = mesh.shape["gx"], mesh.shape["gy"]
        if whole_tiles(mesh, args[0], args[2]):
            part = functools.partial(fused_body, n, ng)
        else:
            part = body
        return mapped(part)(*args)

    def mapped(part):
        return jax.shard_map(
            part,
            mesh=mesh,
            in_specs=placed,
            out_specs=(P(None, "gx", "gy", None), P(None, "gx", "gy", None), P("gx", "gy")),
            check_vma=False,
        )

    return run
```

```python
import functools
import jax
import jax.numpy as jnp
from jax import lax
from jax.experimental import pallas as pl
from jax.experimental.pallas import tpu as pltpu
from jax.sharding import PartitionSpec as P

STEPS = 2
FOOT = 16


grid_ratio = 0.25
soil_gain = 0.2
pier_gain = 0.5


def extended(cells, sides, width):
    for axis, dim in sides:
        count = lax.axis_size(axis)
        ends = count - 1
        head = lax.slice_in_dim(cells, 0, width, axis=dim)
        tail = lax.slice_in_dim(cells, cells.shape[dim] - width, cells.shape[dim], axis=dim)
        cells = jnp.concatenate(
            [
                lax.ppermute(tail, axis, [(i, (i + 1) % count) for i in range(ends)]),
                cells,
                lax.ppermute(head, axis, [((i + 1) % count, i) for i in range(ends)]),
            ],
            axis=dim,
        )
    return cells


def forward_diff(padded, along):
    center = padded[1:-1, 1:-1, 1:-1]
    if along == 0:
        return padded[2:, 1:-1, 1:-1] - center
    if along == 1:
        return padded[1:-1, 2:, 1:-1] - center
    return padded[1:-1, 1:-1, 2:] - center


def backward_diff(padded, along):
    center = padded[1:-1, 1:-1, 1:-1]
    if along == 0:
        return center - padded[:-2, 1:-1, 1:-1]
    if along == 1:
        return center - padded[1:-1, :-2, 1:-1]
    return center - padded[1:-1, 1:-1, :-2]


def move_velocity(velocity, padded, buoyancy):
    scaled = grid_ratio * buoyancy
    first = velocity[0] + scaled * (
        backward_diff(padded[0], 2) + forward_diff(padded[3], 1) + forward_diff(padded[4], 0)
    )
    second = velocity[1] + scaled * (
        forward_diff(padded[3], 2) + backward_diff(padded[1], 1) + forward_diff(padded[5], 0)
    )
    third = velocity[2] + scaled * (
        forward_diff(padded[4], 2) + forward_diff(padded[5], 1) + backward_diff(padded[2], 0)
    )
    return jnp.stack([first, second, third])


def move_stress(stress, padded, lame_first, shear_mod, relax):
    strain_x = forward_diff(padded[0], 2)
    strain_y = forward_diff(padded[1], 1)
    strain_z = forward_diff(padded[2], 0)
    modulus = lame_first + 2.0 * shear_mod
    normal_x = relax * stress[0] + grid_ratio * (
        modulus * strain_x + lame_first * (strain_y + strain_z)
    )
    normal_y = relax * stress[1] + grid_ratio * (
        modulus * strain_y + lame_first * (strain_x + strain_z)
    )
    normal_z = relax * stress[2] + grid_ratio * (
        modulus * strain_z + lame_first * (strain_x + strain_y)
    )
    shear_xy = relax * stress[3] + grid_ratio * shear_mod * (
        backward_diff(padded[0], 1) + backward_diff(padded[1], 2)
    )
    shear_xz = relax * stress[4] + grid_ratio * shear_mod * (
        backward_diff(padded[0], 0) + backward_diff(padded[2], 2)
    )
    shear_yz = relax * stress[5] + grid_ratio * shear_mod * (
        backward_diff(padded[1], 0) + backward_diff(padded[2], 1)
    )
    return jnp.stack([normal_x, normal_y, normal_z, shear_xy, shear_xz, shear_yz])


def layer_values(layer, table):
    levels = jnp.arange(table.shape[0], dtype=jnp.int32)
    onehot = (layer[:, None] == levels[None, :]).astype(table.dtype)
    return jnp.sum(onehot * table[None, :], axis=1)[:, None, None]


def with_faces(fields):
    padded = extended(fields, (("gx", 1), ("gy", 2)), 1)
    return jnp.pad(padded, ((0, 0), (0, 0), (0, 0), (1, 1)))


def footprint_matches(cell_ids, footprint):
    piers = footprint.shape[0]
    equal = (cell_ids[:, None] == footprint.reshape(-1)[None, :]).astype(jnp.float32)
    return jnp.sum(equal.reshape(cell_ids.shape[0], piers, FOOT), axis=2)


def damp_columns(velocity, inverse):
    pencils = lax.all_to_all(velocity, "gx", split_axis=3, concat_axis=1, tiled=True)
    shape = pencils.shape
    flat = pencils.reshape(shape[0], shape[1], shape[2] * shape[3])
    damped = jnp.einsum("zk,fkm->fzm", inverse, flat, precision=lax.Precision.HIGHEST).reshape(
        shape
    )
    return lax.all_to_all(damped, "gx", split_axis=1, concat_axis=3, tiled=True)


def body(
    velocity,
    stress,
    pier_velocity,
    buoyancy,
    layer,
    lame_table,
    shear_table,
    relax_table,
    impedance,
    footprint,
    damp_inverse,
):
    depth_cells, side_cells, line_cells = (velocity.shape[1], velocity.shape[2], velocity.shape[3])
    own_piers = pier_velocity.shape[1]
    lame_first = layer_values(layer, lame_table)
    shear_mod = layer_values(layer, shear_table)
    relax = layer_values(layer, relax_table)
    row_start = lax.axis_index("gy") * side_cells
    cell_ids = row_start * line_cells + jnp.arange(side_cells * line_cells, dtype=jnp.int32)
    selector = footprint_matches(cell_ids, footprint)
    own_foot = lax.dynamic_slice_in_dim(footprint, lax.axis_index("gy") * own_piers, own_piers, 0)
    for time_step in range(STEPS):
        padded = with_faces(stress)
        velocity = move_velocity(velocity, padded, buoyancy)
        vertical = velocity[2].reshape(depth_cells, side_cells * line_cells)
        piece = lax.all_gather(velocity[2], "gy", axis=1, tiled=True)
        count = piece.shape[1]
        piece_ids = jnp.arange(count * line_cells, dtype=jnp.int32)
        picks = footprint_matches(piece_ids, own_foot)
        flat = piece.reshape(depth_cells, count * line_cells)
        summed = jnp.dot(
            flat, picks, precision=lax.Precision.HIGHEST, preferred_element_type=jnp.float32
        )
        mean_speed = summed / FOOT
        force = impedance[None, :] * (pier_velocity - mean_speed)
        pier_velocity = pier_velocity - pier_gain * force
        all_force = lax.all_gather(force, "gy", axis=1, tiled=True)
        pushed = jnp.dot(
            all_force,
            selector.T,
            precision=lax.Precision.HIGHEST,
            preferred_element_type=jnp.float32,
        )
        vertical = vertical + soil_gain * pushed
        velocity = jnp.stack(
            [velocity[0], velocity[1], vertical.reshape(depth_cells, side_cells, line_cells)]
        )
        velocity = damp_columns(velocity, damp_inverse)
        padded = with_faces(velocity)
        stress = move_stress(stress, padded, lame_first, shear_mod, relax)
    return (velocity, stress, pier_velocity)


SIDE = 4
LANES = 128
ROWS = 8
BLOCK = 4
MESH = pl.DeviceIdType.MESH
Z_GHOSTS = ((2, -1), (4, 1), (5, 1))
Y_GHOSTS = ((1, -1), (3, 1), (5, 1))


def fused(
    n, ng, v_hbm, s_hbm, b_hbm, layer_ref, lame_ref, shear_ref, relax_ref, foot_ref, w_ref, imp_ref, damp_ref,
    v_ext, s_ext, w_out,
    buoy, coef, acc, pin, pout, um, fall, wbuf, square, part, rows_of, cols_t, cols_of, spread, damp_cat, damp_own,
    load_sem, zs_send, zs_recv, cf_send, cf_recv, ys_send, ys_recv,
    f_send, f_recv, r_send, r_recv, u_send, u_recv, p_send, p_recv, y_send, y_recv,
):
    me = lax.axis_index("gx")
    g = lax.axis_index("gy")
    depth, side, line = buoy.shape
    tiles = line // LANES
    share_rows = side // n
    inner = pl.ds(ROWS, side)
    own = w_ref.shape[0]
    f32, bf16 = jnp.float32, jnp.bfloat16
    above, below = ROWS - 1, ROWS + side

    def lanes(c):
        return pl.ds(c * LANES, LANES)

    def settle(ref, sem):
        pltpu.make_async_copy(ref, ref, sem).wait()

    loads = []
    for c in range(tiles):
        loads.append((
            pltpu.make_async_copy(
                s_hbm.at[:, :, :, lanes(c)], s_ext.at[:, pl.ds(1, depth), inner, lanes(c)], load_sem.at[c]
            ),
            pltpu.make_async_copy(b_hbm.at[:, :, lanes(c)], buoy.at[:, :, lanes(c)], load_sem.at[tiles + c]),
            pltpu.make_async_copy(
                v_hbm.at[:, :, :, lanes(c)], v_ext.at[pl.ds(0, 3), pl.ds(1, depth), inner, lanes(c)],
                load_sem.at[2 * tiles + c],
            ),
        ))
        for copy in loads[c]:
            copy.start()

    plane = jnp.zeros((side, line), f32)
    for f, way in Z_GHOSTS:
        s_ext[f, 0 if way < 0 else depth + 1, inner, :] = plane
    edge = jnp.zeros((depth + 2, line), f32)
    for f, way in Y_GHOSTS:
        s_ext[f, :, above if way < 0 else below, :] = edge
    for f in range(3 * STEPS):
        v_ext[f, :, above, :] = edge
        v_ext[f, :, below, :] = edge
    for k in range(depth):
        for c, (table, scale) in enumerate(((lame_ref, grid_ratio), (shear_ref, grid_ratio), (relax_ref, 1.0))):
            coef[c, k + 1] = jnp.full((side, LANES), scale * table[layer_ref[k]], f32)
    for c in range(3):
        coef[c, 0] = jnp.zeros((side, LANES), f32)
        coef[c, depth + 1] = jnp.zeros((side, LANES), f32)
        pout[c, 0] = jnp.zeros((ROWS, LANES), f32)
        pout[c, n * depth + 1] = jnp.zeros((ROWS, LANES), f32)

    barrier = pltpu.get_barrier_semaphore()
    for d in range(1, n):
        pl.semaphore_signal(
            barrier, inc=1, device_id=(lax.rem(me + d, n), g), device_id_type=MESH
        )
    for d in range(1, ng):
        pl.semaphore_signal(
            barrier, inc=1, device_id=(me, lax.rem(g + d, ng)), device_id_type=MESH
        )
    pl.semaphore_wait(barrier, n - 1 + ng - 1)

    def z_copy(i):
        f, way = Z_GHOSTS[i]
        return pltpu.make_async_remote_copy(
            src_ref=s_hbm.at[f, depth - 1 if way < 0 else 0],
            dst_ref=s_ext.at[f, 0 if way < 0 else depth + 1, inner, :],
            send_sem=zs_send.at[i], recv_sem=zs_recv.at[i],
            device_id=(me - way, g), device_id_type=MESH,
        )

    def c_copy(way):
        i = (way + 1) // 2
        return pltpu.make_async_remote_copy(
            src_ref=coef.at[:, depth if way < 0 else 1],
            dst_ref=coef.at[:, 0 if way < 0 else depth + 1],
            send_sem=cf_send.at[i], recv_sem=cf_recv.at[i],
            device_id=(me - way, g), device_id_type=MESH,
        )

    def y_stress(i):
        f, way = Y_GHOSTS[i]
        return pltpu.make_async_remote_copy(
            src_ref=s_hbm.at[f, :, pl.ds(side - 1 if way < 0 else 0, 1), :],
            dst_ref=s_ext.at[f, pl.ds(1, depth), pl.ds(above if way < 0 else below, 1), :],
            send_sem=ys_send.at[i], recv_sem=ys_recv.at[i],
            device_id=(me, g - way), device_id_type=MESH,
        )

    not_ends = {
        -1: (me > 0, me < n - 1, g > 0, g < ng - 1),
        1: (me < n - 1, me > 0, g < ng - 1, g > 0),
    }
    ghosts = [(z_copy, i, not_ends[way][0:2]) for i, (f, way) in enumerate(Z_GHOSTS)]
    ghosts += [(y_stress, i, not_ends[way][2:4]) for i, (f, way) in enumerate(Y_GHOSTS)]
    ghosts += [(c_copy, way, not_ends[way][0:2]) for way in (-1, 1)]
    for make, i, (gets, sends) in ghosts:
        @pl.when(sends)
        def _(make=make, i=i):
            make(i).start()

    ids = lax.broadcasted_iota(jnp.int32, (side, LANES), 0) + g * side
    lane_id = lax.broadcasted_iota(jnp.int32, (2 * LANES, LANES), 1)
    row_id = lax.rem(lax.broadcasted_iota(jnp.int32, (2 * LANES, LANES), 0), LANES)
    first = jnp.full((1, LANES), -64, jnp.int32)
    begin_lane = jnp.full((1, LANES), -64, jnp.int32)
    begin_row = jnp.full((2 * LANES, LANES), -64, jnp.int32)
    for p in range(foot_ref.shape[0]):
        first = jnp.where(lane_id[0:1] == p, foot_ref[p, 0] // line, first)
        begin_lane = jnp.where(lane_id[0:1] == p, foot_ref[p, 0] % line, begin_lane)
        begin_row = jnp.where(row_id == p, foot_ref[p, 0] % line, begin_row)
    rows_of[...] = jnp.where((ids >= first) & (ids < first + SIDE), 1.0, 0.0)
    for c in range(tiles):
        at = row_id + c * LANES
        cols_t[c] = jnp.where((at >= begin_lane) & (at < begin_lane + SIDE), 1.0, 0.0).astype(bf16)
        at = lane_id + c * LANES
        cols_of[:, lanes(c)] = jnp.where((at >= begin_row) & (at < begin_row + SIDE), 1.0, 0.0).astype(bf16)

    def halves(a):
        high = a.astype(bf16)
        return high, (a - high.astype(f32)).astype(bf16)

    high, low = halves(damp_ref[...])
    damp_cat[...] = jnp.concatenate([high, high, low], axis=1)
    damp_own[...] = jnp.zeros_like(damp_own)
    damp_own[pl.ds(1, depth), :] = damp_ref[pl.ds(pl.multiple_of(me * depth, depth), depth), :]

    @pl.when(me > 0)
    def _():
        damp_own[pl.ds(0, 1), :] = damp_ref[pl.ds(me * depth - 1, 1), :]

    @pl.when(me < n - 1)
    def _():
        damp_own[pl.ds(depth + 1, 1), :] = damp_ref[pl.ds((me + 1) * depth, 1), :]

    square[...] = jnp.zeros((LANES, LANES), f32)
    square[pl.ds(0, own), pl.ds(0, depth)] = w_ref[...]
    wbuf[...] = pltpu.roll(jnp.transpose(square[...])[0:depth], g * own, 1)
    impedance = jnp.zeros((ROWS, LANES), f32)
    for i in range(imp_ref.shape[0]):
        impedance = jnp.where(lane_id[0:ROWS] == g * own + i, imp_ref[i], impedance)

    def look(ref, f, k, count, c, dy=0, dz=0):
        return ref[f, pl.ds(k + dz, count), pl.ds(ROWS + dy, side), lanes(c)].reshape(count * side, LANES)

    def row(ref, f, c, at, dz=0):
        return ref[f, pl.ds(1 + dz, depth), at, lanes(c)]

    def ahead(get, c):
        cell = get(c)
        lane = lax.broadcasted_iota(jnp.int32, cell.shape, 1)
        other = 0.0 if c == tiles - 1 else pltpu.roll(get(c + 1), LANES - 1, 1)
        return jnp.where(lane == LANES - 1, other, pltpu.roll(cell, LANES - 1, 1))

    def behind(get, c):
        cell = get(c)
        lane = lax.broadcasted_iota(jnp.int32, cell.shape, 1)
        other = 0.0 if c == 0 else pltpu.roll(get(c - 1), 1, 1)
        return jnp.where(lane == 0, other, pltpu.roll(cell, 1, 1))

    def blocks(run, size=BLOCK):
        def at(i, carry):
            run(1 + i * size, size)
            return carry

        lax.fori_loop(0, depth // size, at, 0)

    def moduli(k, count):
        return [coef[c, pl.ds(k, count)].reshape(count * side, LANES) for c in range(3)]

    def put(ref, f, k, count, c, value):
        ref[f, pl.ds(k, count), inner, lanes(c)] = value.reshape(count, side, LANES)

    def speeds(step, c):
        base = 3 * (step - 1) if step > 0 else 0

        def run(k, count):
            at = functools.partial(look, s_ext)
            scaled = grid_ratio * buoy[pl.ds(k - 1, count), :, lanes(c)].reshape(count * side, LANES)
            xx, yy, zz, xy, xz, yz = (at(f, k, count, c) for f in range(6))
            total = (xx - behind(lambda c: at(0, k, count, c), c)) + (at(3, k, count, c, 1) - xy)
            total = total + (at(4, k, count, c, 0, 1) - xz)
            values = [total]
            total = (ahead(lambda c: at(3, k, count, c), c) - xy) + (yy - at(1, k, count, c, -1))
            values.append(total + (at(5, k, count, c, 0, 1) - yz))
            total = (ahead(lambda c: at(4, k, count, c), c) - xz) + (at(5, k, count, c, 1) - yz)
            values.append(total + (zz - at(2, k, count, c, 0, -1)))
            for f in range(3):
                value = look(v_ext, base + f, k, count, c) + scaled * values[f]
                acc[f, pl.ds(k - 1, count), :, lanes(c)] = value.reshape(count, side, LANES)

        blocks(run)
        high, low = halves(acc[2, :, :, lanes(c)].reshape(depth * side, LANES))
        term = jnp.dot(jnp.concatenate([high, low], axis=1), cols_t[c], preferred_element_type=f32)
        part[...] = term if c == 0 else part[...] + term

    def shears(step, c, with_ghosts, which=(3, 4, 5)):
        at = functools.partial(look, v_ext)
        x, y, z = (3 * step + f for f in range(3))

        def run(k, count, which=which):
            lame, shear, relax = moduli(k, count)
            for f in which:
                if f == 3:
                    strain = (at(x, k, count, c) - at(x, k, count, c, -1)) + (
                        at(y, k, count, c) - behind(lambda c: at(y, k, count, c), c)
                    )
                elif f == 4:
                    strain = (at(x, k, count, c) - at(x, k, count, c, 0, -1)) + (
                        at(z, k, count, c) - behind(lambda c: at(z, k, count, c), c)
                    )
                else:
                    strain = (at(y, k, count, c) - at(y, k, count, c, 0, -1)) + (
                        at(z, k, count, c) - at(z, k, count, c, -1)
                    )
                put(s_ext, f, k, count, c, relax * look(s_ext, f, k, count, c) + shear * strain)

        blocks(run)
        if with_ghosts:
            run(depth + 1, 1, (4, 5))
            shear, relax = (coef[i, pl.ds(1, depth), 0, :] for i in (1, 2))
            y_at = functools.partial(row, v_ext, y, at=below)
            strain = (row(v_ext, x, c, below) - row(v_ext, x, c, below - 1)) + (
                y_at(c) - behind(lambda c: y_at(c), c)
            )
            xy = relax * row(s_ext, 3, c, below) + shear * strain
            strain = (y_at(c) - y_at(c, dz=-1)) + (row(v_ext, z, c, below) - row(v_ext, z, c, below - 1))
            yz = relax * row(s_ext, 5, c, below) + shear * strain
            s_ext[3, pl.ds(1, depth), below, lanes(c)] = jnp.where(g == ng - 1, 0.0, xy)
            s_ext[5, pl.ds(1, depth), below, lanes(c)] = jnp.where(g == ng - 1, 0.0, yz)

    def normals(step, c, with_ghosts):
        at = functools.partial(look, v_ext)
        x, y, z = (3 * step + f for f in range(3))

        def run(k, count, which=(0, 1, 2)):
            lame, shear, relax = moduli(k, count)
            ex = ahead(lambda c: at(x, k, count, c), c) - at(x, k, count, c)
            ey = at(y, k, count, c, 1) - at(y, k, count, c)
            ez = at(z, k, count, c, 0, 1) - at(z, k, count, c)
            trace = lame * ((ex + ey) + ez)
            twice = shear + shear
            for f in which:
                value = relax * look(s_ext, f, k, count, c) + (twice * (ex, ey, ez)[f] + trace)
                put(s_ext, f, k, count, c, value)

        blocks(run)
        if with_ghosts:
            run(0, 1, (2,))
            lame, shear, relax = (coef[i, pl.ds(1, depth), 0, :] for i in range(3))
            x_at = functools.partial(row, v_ext, x, at=above)
            ex = ahead(lambda c: x_at(c), c) - x_at(c)
            ey = row(v_ext, y, c, ROWS) - row(v_ext, y, c, above)
            ez = row(v_ext, z, c, above, 1) - row(v_ext, z, c, above)
            yy = relax * row(s_ext, 1, c, above) + ((shear + shear) * ey + lame * ((ex + ey) + ez))
            s_ext[1, pl.ds(1, depth), above, lanes(c)] = jnp.where(g == 0, 0.0, yy)

    def mine(t):
        return pl.ds(t * share_rows, share_rows)

    def there(step, c, d):
        t = lax.rem(me + d, n)
        src = acc.at[:, :, mine(t), lanes(c)]
        dst = pin.at[:, pl.ds(me * depth, depth), mine(c), :]
        if d == 0:
            return pltpu.make_async_copy(src, dst, f_recv.at[step, c])
        return pltpu.make_async_remote_copy(
            src_ref=src, dst_ref=dst, send_sem=f_send.at[step, c],
            recv_sem=f_recv.at[step, c], device_id=(t, g), device_id_type=MESH,
        )

    def back(step, c, d):
        t = lax.rem(me + d, n)
        pieces = ((0, 3, 0, depth + 2),)
        if step == STEPS - 1:
            pieces = ((0, 2, 0, depth + 1), (2, 1, 1, depth + 1))
        copies = []
        for f, fields, low, count in pieces:
            src = pout.at[pl.ds(f, fields), pl.ds(t * depth + low, count), mine(c), :]
            dst = v_ext.at[
                pl.ds(3 * step + f, fields), pl.ds(low, count), pl.ds(ROWS + me * share_rows, share_rows), lanes(c)
            ]
            if d == 0:
                copies.append(pltpu.make_async_copy(src, dst, r_recv.at[step, c]))
            else:
                copies.append(pltpu.make_async_remote_copy(
                    src_ref=src, dst_ref=dst, send_sem=r_send.at[step, c],
                    recv_sem=r_recv.at[step, c], device_id=(t, g), device_id_type=MESH,
                ))
        return copies

    def count_back(step):
        return depth + (1 if step == STEPS - 1 else 2)

    def start_there(step, c):
        for d in list(range(1, n)) + [0]:
            there(step, c, d).start()

    def start_back(step, c):
        for d in list(range(1, n)) + [0]:
            for copy in back(step, c, d):
                copy.start()

    def sent_there(step, c):
        settle(pin.at[:, pl.ds(0, (n - 1) * depth), mine(c), :], f_send.at[step, c])

    def got_there(step, c):
        settle(pin.at[:, :, mine(c), :], f_recv.at[step, c])

    def sent_back(step, c):
        settle(pout.at[:, pl.ds(0, (n - 1) * count_back(step)), mine(c), :], r_send.at[step, c])

    def got_back(step, c):
        settle(
            v_ext.at[pl.ds(3 * step, 3), pl.ds(0, count_back(step)), inner, lanes(c)], r_recv.at[step, c]
        )

    def damp(step, c):
        got_there(step, c)
        if step > 0:
            sent_back(step - 1, c)
        for f in range(3):
            terms = []
            for r in range(share_rows):
                high, low = halves(pin[f, :, share_rows * c + r, :])
                terms.append(jnp.concatenate([high, low, high], axis=0))
            damped = jnp.dot(damp_cat[...], jnp.concatenate(terms, axis=1), preferred_element_type=f32)
            for r in range(share_rows):
                pout[f, pl.ds(1, n * depth), share_rows * c + r, :] = damped[:, r * LANES : (r + 1) * LANES]
        start_back(step, c)

    def share(step, d):
        return pltpu.make_async_remote_copy(
            src_ref=um.at[step, 0], dst_ref=um.at[step, d],
            send_sem=u_send.at[step], recv_sem=u_recv.at[step],
            device_id=(me, lax.rem(g + d, ng)), device_id_type=MESH,
        )

    def forces(step, d):
        block = pl.ds(pl.multiple_of(me * depth, depth), depth)
        return pltpu.make_async_remote_copy(
            src_ref=fall.at[step, block], dst_ref=fall.at[step, block],
            send_sem=p_send.at[step], recv_sem=p_recv.at[step],
            device_id=(lax.rem(me + d, n), g), device_id_type=MESH,
        )

    def pier_means(step):
        masked = part[...].reshape(depth, side, LANES) * rows_of[...][None]
        um[step, 0, pl.ds(0, depth), :] = jnp.sum(masked, axis=1)
        um[step, 0, pl.ds(depth, depth), :] = wbuf[...]
        um[step, 0, pl.ds(2 * depth, ROWS), :] = impedance
        for d in range(1, ng):
            share(step, d).start()

    def pier_forces(step):
        settle(um.at[step, pl.ds(1, ng - 1)], u_recv.at[step])
        settle(um.at[step, pl.ds(1, ng - 1)], u_send.at[step])
        every = um[step, 0]
        for d in range(1, ng):
            every = every + um[step, d]
        w = every[depth : 2 * depth] if step == 0 else wbuf[...]
        force = every[2 * depth : 2 * depth + 1] * (w - every[0:depth] / FOOT)
        wbuf[...] = w - pier_gain * force
        fall[step, pl.ds(pl.multiple_of(me * depth, depth), depth), :] = soil_gain * force
        for d in range(1, n):
            forces(step, d).start()

    def pier_spread(step):
        settle(fall.at[step, pl.ds(0, (n - 1) * depth)], p_recv.at[step])
        settle(fall.at[step, pl.ds(0, (n - 1) * depth)], p_send.at[step])
        pushed = jnp.dot(
            damp_own[...], fall[step], precision=lax.Precision.HIGHEST, preferred_element_type=f32
        )[0 : depth + 2]
        wide = (pushed[:, None, :] * rows_of[...][None]).reshape((depth + 2) * side, LANES)
        spread[...] = jnp.concatenate(halves(wide), axis=1)

    def y_speed(step, c, i):
        low, count = (0, depth + 2) if step < STEPS - 1 else (1, depth)
        fields, planes = pl.ds(3 * step, 3), pl.ds(low, count)
        return pltpu.make_async_remote_copy(
            src_ref=v_ext.at[fields, planes, pl.ds(below - 1 if i == 0 else ROWS, 1), lanes(c)],
            dst_ref=v_ext.at[fields, planes, pl.ds(above if i == 0 else below, 1), lanes(c)],
            send_sem=y_send.at[step, c, i], recv_sem=y_recv.at[step, c, i],
            device_id=(me, g + 1 - 2 * i), device_id_type=MESH,
        )

    has_next, has_last = g < ng - 1, g > 0

    def arrive(step, c):
        got_back(step, c)
        low, count = (0, depth + 2) if step < STEPS - 1 else (1, depth + 1)
        term = jnp.dot(
            spread[pl.ds(low * side, count * side), :], cols_of[:, lanes(c)], preferred_element_type=f32
        )
        put(v_ext, 3 * step + 2, low, count, c, look(v_ext, 3 * step + 2, low, count, c) + term)

        @pl.when(has_next)
        def _():
            y_speed(step, c, 0).start()

        @pl.when(has_last)
        def _():
            y_speed(step, c, 1).start()

    def edges(step, c):
        @pl.when(has_last)
        def _():
            y_speed(step, c, 0).wait_recv()
            y_speed(step, c, 1).wait_send()

        @pl.when(has_next)
        def _():
            y_speed(step, c, 1).wait_recv()
            y_speed(step, c, 0).wait_send()

    def load(c):
        for copy in loads[c]:
            copy.wait()

    for make, i, (gets, sends) in ghosts:
        @pl.when(gets)
        def _(make=make, i=i):
            make(i).wait_recv()

        @pl.when(sends)
        def _(make=make, i=i):
            make(i).wait_send()

    last = tiles - 1

    def first_speeds(c):
        if c == 0:
            load(0)
        if c < last:
            load(c + 1)
        speeds(0, c)

    def next_speeds(step, c):
        sent_there(step - 1, c)
        speeds(step, c)

    for c in range(tiles):
        first_speeds(c)
        if c < 2:
            start_there(0, c)
    pier_means(0)
    for step in range(STEPS):
        for c in range(tiles):
            damp(step, c)
            if step == 0 and c + 2 < tiles:
                start_there(0, c + 2)
            if c == 0:
                pier_forces(step)
            if c == 2:
                pier_spread(step)
        more = step < STEPS - 1
        for c in range(tiles):
            arrive(step, c)
            if c > 0:
                edges(step, c - 1)
                shears(step, c - 1, more)
            if c > 1:
                normals(step, c - 2, more)
                if more:
                    next_speeds(step + 1, c - 2)
                    start_there(step + 1, c - 2)
        normals_last = last - 1
        if not more:
            normals(step, last - 1, more)
        edges(step, last)
        shears(step, last, more)
        if more:
            normals(step, last - 1, more)
            next_speeds(step + 1, last - 1)
            start_there(step + 1, last - 1)
        normals(step, last, more)
        if more:
            next_speeds(step + 1, last)
            start_there(step + 1, last)
            pier_means(step + 1)

    square[...] = jnp.zeros((LANES, LANES), f32)
    square[pl.ds(0, depth), :] = pltpu.roll(wbuf[...], lax.rem(LANES - g * own, LANES), 1)
    w_out[...] = jnp.transpose(square[...])[0:own, 0:depth]
    for c in range(tiles):
        sent_there(STEPS - 1, c)
        sent_back(STEPS - 1, c)


def deliver(v_ref, s_ref, w_ref, v_out, s_out, w_out, sem):
    depth, side = v_out.shape[1:3]
    inside = pl.ds(1, depth), pl.ds(ROWS, side)
    pairs = (
        (v_ref.at[(pl.ds(3 * (STEPS - 1), 3),) + inside], v_out),
        (s_ref.at[(pl.ds(0, 6),) + inside], s_out),
        (w_ref, w_out),
    )
    copies = [pltpu.make_async_copy(a, b, sem.at[i]) for i, (a, b) in enumerate(pairs)]
    for copy in copies:
        copy.start()
    for copy in copies:
        copy.wait()


def fused_body(
    n, ng, velocity, stress, pier_velocity, buoyancy, layer, lame_table, shear_table, relax_table,
    impedance, footprint, damp_inverse,
):
    depth, side, line = buoyancy.shape
    own = pier_velocity.shape[1]
    f32 = jnp.float32
    hbm = pl.BlockSpec(memory_space=pltpu.HBM)
    vmem = pl.BlockSpec(memory_space=pltpu.VMEM)
    smem = pl.BlockSpec(memory_space=pltpu.SMEM)
    dma = pltpu.SemaphoreType.DMA
    tall = side + 2 * ROWS
    stage = 2 * depth + ROWS
    tiles = line // LANES
    v, s, w = pl.pallas_call(
        functools.partial(fused, n, ng),
        out_shape=(
            pltpu.VMEM((3 * STEPS, depth + 2, tall, line), f32),
            pltpu.VMEM((6, depth + 2, tall, line), f32),
            pltpu.VMEM((own, depth), f32),
        ),
        in_specs=[hbm] * 3 + [smem] * 5 + [vmem, smem, vmem],
        out_specs=(vmem, vmem, vmem),
        scratch_shapes=[
            pltpu.VMEM((depth, side, line), f32),
            pltpu.VMEM((3, depth + 2, side, LANES), f32),
            pltpu.VMEM((3, depth, side, line), f32),
            pltpu.VMEM((3, n * depth, ROWS, LANES), f32),
            pltpu.VMEM((3, n * depth + 2, ROWS, LANES), f32),
            pltpu.VMEM((STEPS, ng, stage, LANES), f32),
            pltpu.VMEM((STEPS, n * depth, LANES), f32),
            pltpu.VMEM((depth, LANES), f32),
            pltpu.VMEM((LANES, LANES), f32),
            pltpu.VMEM((depth * side, LANES), f32),
            pltpu.VMEM((side, LANES), f32),
            pltpu.VMEM((tiles, 2 * LANES, LANES), jnp.bfloat16),
            pltpu.VMEM((2 * LANES, line), jnp.bfloat16),
            pltpu.VMEM(((depth + 2) * side, 2 * LANES), jnp.bfloat16),
            pltpu.VMEM((n * depth, 3 * n * depth), jnp.bfloat16),
            pltpu.VMEM((depth + ROWS, n * depth), f32),
            dma((3 * tiles,)), dma((3,)), dma((3,)), dma((2,)), dma((2,)), dma((3,)), dma((3,)),
            dma((STEPS, tiles)), dma((STEPS, tiles)), dma((STEPS, tiles)), dma((STEPS, tiles)),
            dma((STEPS,)), dma((STEPS,)), dma((STEPS,)), dma((STEPS,)),
            dma((STEPS, tiles, 2)), dma((STEPS, tiles, 2)),
        ],
        compiler_params=pltpu.CompilerParams(
            collective_id=0, has_side_effects=True, vmem_limit_bytes=48 * 1024 * 1024
        ),
    )(
        velocity, stress, buoyancy, layer, lame_table, shear_table, relax_table,
        footprint, pier_velocity.T, impedance, damp_inverse,
    )
    v, s, w = pl.pallas_call(
        deliver,
        out_shape=tuple(
            jax.ShapeDtypeStruct(a, f32) for a in (velocity.shape, stress.shape, (own, depth))
        ),
        in_specs=[vmem] * 3,
        out_specs=(hbm,) * 3,
        scratch_shapes=[dma((3,))],
        compiler_params=pltpu.CompilerParams(vmem_limit_bytes=8 * 1024 * 1024),
    )(v, s, w)
    return v, s, w.T


def whole_tiles(mesh, velocity, pier_velocity):
    n, ng = mesh.shape["gx"], mesh.shape["gy"]
    depth, side, line = velocity.shape[1] // n, velocity.shape[2] // ng, velocity.shape[3]
    return (
        line % LANES == 0
        and side % 16 == 0
        and side % n == 0
        and depth % ROWS == 0
        and (side // n) * (line // LANES) == ROWS
        and n * depth % LANES == 0
        and pier_velocity.shape[1] <= LANES
    )


def solution(mesh):
    placed = (
        P(None, "gx", "gy", None),
        P(None, "gx", "gy", None),
        P("gx", "gy"),
        P("gx", "gy", None),
        P("gx"),
        P(),
        P(),
        P(),
        P("gy"),
        P(),
        P(),
    )

    def run(*args):
        n, ng = mesh.shape["gx"], mesh.shape["gy"]
        if whole_tiles(mesh, args[0], args[2]):
            part = functools.partial(fused_body, n, ng)
        else:
            part = body
        return mapped(part)(*args)

    def mapped(part):
        return jax.shard_map(
            part,
            mesh=mesh,
            in_specs=placed,
            out_specs=(P(None, "gx", "gy", None), P(None, "gx", "gy", None), P("gx", "gy")),
            check_vma=False,
        )

    return run
```

```python
import functools
import jax
import jax.numpy as jnp
from jax import lax
from jax.experimental import pallas as pl
from jax.experimental.pallas import tpu as pltpu
from jax.sharding import PartitionSpec as P

STEPS = 2
FOOT = 16


grid_ratio = 0.25
soil_gain = 0.2
pier_gain = 0.5


def extended(cells, sides, width):
    for axis, dim in sides:
        count = lax.axis_size(axis)
        ends = count - 1
        head = lax.slice_in_dim(cells, 0, width, axis=dim)
        tail = lax.slice_in_dim(cells, cells.shape[dim] - width, cells.shape[dim], axis=dim)
        cells = jnp.concatenate(
            [
                lax.ppermute(tail, axis, [(i, (i + 1) % count) for i in range(ends)]),
                cells,
                lax.ppermute(head, axis, [((i + 1) % count, i) for i in range(ends)]),
            ],
            axis=dim,
        )
    return cells


def forward_diff(padded, along):
    center = padded[1:-1, 1:-1, 1:-1]
    if along == 0:
        return padded[2:, 1:-1, 1:-1] - center
    if along == 1:
        return padded[1:-1, 2:, 1:-1] - center
    return padded[1:-1, 1:-1, 2:] - center


def backward_diff(padded, along):
    center = padded[1:-1, 1:-1, 1:-1]
    if along == 0:
        return center - padded[:-2, 1:-1, 1:-1]
    if along == 1:
        return center - padded[1:-1, :-2, 1:-1]
    return center - padded[1:-1, 1:-1, :-2]


def move_velocity(velocity, padded, buoyancy):
    scaled = grid_ratio * buoyancy
    first = velocity[0] + scaled * (
        backward_diff(padded[0], 2) + forward_diff(padded[3], 1) + forward_diff(padded[4], 0)
    )
    second = velocity[1] + scaled * (
        forward_diff(padded[3], 2) + backward_diff(padded[1], 1) + forward_diff(padded[5], 0)
    )
    third = velocity[2] + scaled * (
        forward_diff(padded[4], 2) + forward_diff(padded[5], 1) + backward_diff(padded[2], 0)
    )
    return jnp.stack([first, second, third])


def move_stress(stress, padded, lame_first, shear_mod, relax):
    strain_x = forward_diff(padded[0], 2)
    strain_y = forward_diff(padded[1], 1)
    strain_z = forward_diff(padded[2], 0)
    modulus = lame_first + 2.0 * shear_mod
    normal_x = relax * stress[0] + grid_ratio * (
        modulus * strain_x + lame_first * (strain_y + strain_z)
    )
    normal_y = relax * stress[1] + grid_ratio * (
        modulus * strain_y + lame_first * (strain_x + strain_z)
    )
    normal_z = relax * stress[2] + grid_ratio * (
        modulus * strain_z + lame_first * (strain_x + strain_y)
    )
    shear_xy = relax * stress[3] + grid_ratio * shear_mod * (
        backward_diff(padded[0], 1) + backward_diff(padded[1], 2)
    )
    shear_xz = relax * stress[4] + grid_ratio * shear_mod * (
        backward_diff(padded[0], 0) + backward_diff(padded[2], 2)
    )
    shear_yz = relax * stress[5] + grid_ratio * shear_mod * (
        backward_diff(padded[1], 0) + backward_diff(padded[2], 1)
    )
    return jnp.stack([normal_x, normal_y, normal_z, shear_xy, shear_xz, shear_yz])


def layer_values(layer, table):
    levels = jnp.arange(table.shape[0], dtype=jnp.int32)
    onehot = (layer[:, None] == levels[None, :]).astype(table.dtype)
    return jnp.sum(onehot * table[None, :], axis=1)[:, None, None]


def with_faces(fields):
    padded = extended(fields, (("gx", 1), ("gy", 2)), 1)
    return jnp.pad(padded, ((0, 0), (0, 0), (0, 0), (1, 1)))


def footprint_matches(cell_ids, footprint):
    piers = footprint.shape[0]
    equal = (cell_ids[:, None] == footprint.reshape(-1)[None, :]).astype(jnp.float32)
    return jnp.sum(equal.reshape(cell_ids.shape[0], piers, FOOT), axis=2)


def damp_columns(velocity, inverse):
    pencils = lax.all_to_all(velocity, "gx", split_axis=3, concat_axis=1, tiled=True)
    shape = pencils.shape
    flat = pencils.reshape(shape[0], shape[1], shape[2] * shape[3])
    damped = jnp.einsum("zk,fkm->fzm", inverse, flat, precision=lax.Precision.HIGHEST).reshape(
        shape
    )
    return lax.all_to_all(damped, "gx", split_axis=1, concat_axis=3, tiled=True)


def body(
    velocity,
    stress,
    pier_velocity,
    buoyancy,
    layer,
    lame_table,
    shear_table,
    relax_table,
    impedance,
    footprint,
    damp_inverse,
):
    depth_cells, side_cells, line_cells = (velocity.shape[1], velocity.shape[2], velocity.shape[3])
    own_piers = pier_velocity.shape[1]
    lame_first = layer_values(layer, lame_table)
    shear_mod = layer_values(layer, shear_table)
    relax = layer_values(layer, relax_table)
    row_start = lax.axis_index("gy") * side_cells
    cell_ids = row_start * line_cells + jnp.arange(side_cells * line_cells, dtype=jnp.int32)
    selector = footprint_matches(cell_ids, footprint)
    own_foot = lax.dynamic_slice_in_dim(footprint, lax.axis_index("gy") * own_piers, own_piers, 0)
    for time_step in range(STEPS):
        padded = with_faces(stress)
        velocity = move_velocity(velocity, padded, buoyancy)
        vertical = velocity[2].reshape(depth_cells, side_cells * line_cells)
        piece = lax.all_gather(velocity[2], "gy", axis=1, tiled=True)
        count = piece.shape[1]
        piece_ids = jnp.arange(count * line_cells, dtype=jnp.int32)
        picks = footprint_matches(piece_ids, own_foot)
        flat = piece.reshape(depth_cells, count * line_cells)
        summed = jnp.dot(
            flat, picks, precision=lax.Precision.HIGHEST, preferred_element_type=jnp.float32
        )
        mean_speed = summed / FOOT
        force = impedance[None, :] * (pier_velocity - mean_speed)
        pier_velocity = pier_velocity - pier_gain * force
        all_force = lax.all_gather(force, "gy", axis=1, tiled=True)
        pushed = jnp.dot(
            all_force,
            selector.T,
            precision=lax.Precision.HIGHEST,
            preferred_element_type=jnp.float32,
        )
        vertical = vertical + soil_gain * pushed
        velocity = jnp.stack(
            [velocity[0], velocity[1], vertical.reshape(depth_cells, side_cells, line_cells)]
        )
        velocity = damp_columns(velocity, damp_inverse)
        padded = with_faces(velocity)
        stress = move_stress(stress, padded, lame_first, shear_mod, relax)
    return (velocity, stress, pier_velocity)


SIDE = 4
LANES = 128
ROWS = 8
BLOCK = 4
MESH = pl.DeviceIdType.MESH
Z_GHOSTS = ((2, -1), (4, 1), (5, 1))
Y_GHOSTS = ((1, -1), (3, 1), (5, 1))


def fused(
    n, ng, v_hbm, s_hbm, b_hbm, layer_hbm, lame_hbm, shear_hbm, relax_hbm, foot_hbm, w_hbm, imp_hbm, damp_hbm,
    v_ext, s_ext, w_out,
    layer_ref, lame_ref, shear_ref, relax_ref, foot_ref, w_ref, imp_ref, damp_ref, small_sem,
    buoy, coef, acc, ahead_of, pin, pout, um, fall, wbuf, gain, square, part, rows_of, cols_t, cols_of, spread, damp_cat, damp_own,
    load_sem, zs_send, zs_recv, cf_send, cf_recv, ys_send, ys_recv,
    f_send, f_recv, r_send, r_recv, u_send, u_recv, p_send, p_recv, y_send, y_recv,
):
    me = lax.axis_index("gx")
    g = lax.axis_index("gy")
    depth, side, line = buoy.shape
    tiles = line // LANES
    share_rows = side // n
    inner = pl.ds(ROWS, side)
    own = w_ref.shape[0]
    stage_rows = um.shape[2]
    f32, bf16 = jnp.float32, jnp.bfloat16
    above, below = ROWS - 1, ROWS + side

    def lanes(c):
        return pl.ds(c * LANES, LANES)

    def settle(ref, sem):
        pltpu.make_async_copy(ref, ref, sem).wait()

    loads = []
    for c in range(tiles):
        loads.append((
            pltpu.make_async_copy(
                s_hbm.at[:, :, :, lanes(c)], s_ext.at[:, pl.ds(1, depth), inner, lanes(c)], load_sem.at[c]
            ),
            pltpu.make_async_copy(b_hbm.at[:, :, lanes(c)], buoy.at[:, :, lanes(c)], load_sem.at[tiles + c]),
            pltpu.make_async_copy(
                v_hbm.at[:, :, :, lanes(c)], v_ext.at[pl.ds(0, 3), pl.ds(1, depth), inner, lanes(c)],
                load_sem.at[2 * tiles + c],
            ),
        ))
        for copy in loads[c]:
            copy.start()

    smalls = [
        pltpu.make_async_copy(src, dst, small_sem.at[i])
        for i, (src, dst) in enumerate((
            (layer_hbm, layer_ref), (lame_hbm, lame_ref), (shear_hbm, shear_ref), (relax_hbm, relax_ref),
            (foot_hbm, foot_ref), (w_hbm, w_ref), (imp_hbm, imp_ref), (damp_hbm, damp_ref),
        ))
    ]
    for copy in smalls:
        copy.start()
    barrier = pltpu.get_barrier_semaphore()
    for d in range(1, n):
        pl.semaphore_signal(
            barrier, inc=1, device_id=(lax.rem(me + d, n), g), device_id_type=MESH
        )
    for d in range(1, ng):
        pl.semaphore_signal(
            barrier, inc=1, device_id=(me, lax.rem(g + d, ng)), device_id_type=MESH
        )
    pl.semaphore_wait(barrier, n - 1 + ng - 1)

    def z_copy(i):
        f, way = Z_GHOSTS[i]
        return pltpu.make_async_remote_copy(
            src_ref=s_hbm.at[f, depth - 1 if way < 0 else 0],
            dst_ref=s_ext.at[f, 0 if way < 0 else depth + 1, inner, :],
            send_sem=zs_send.at[i], recv_sem=zs_recv.at[i],
            device_id=(me - way, g), device_id_type=MESH,
        )

    def c_copy(way):
        i = (way + 1) // 2
        return pltpu.make_async_remote_copy(
            src_ref=coef.at[:, depth if way < 0 else 1],
            dst_ref=coef.at[:, 0 if way < 0 else depth + 1],
            send_sem=cf_send.at[i], recv_sem=cf_recv.at[i],
            device_id=(me - way, g), device_id_type=MESH,
        )

    def y_stress(i):
        f, way = Y_GHOSTS[i]
        return pltpu.make_async_remote_copy(
            src_ref=s_hbm.at[f, :, pl.ds(side - 1 if way < 0 else 0, 1), :],
            dst_ref=s_ext.at[f, pl.ds(1, depth), pl.ds(above if way < 0 else below, 1), :],
            send_sem=ys_send.at[i], recv_sem=ys_recv.at[i],
            device_id=(me, g - way), device_id_type=MESH,
        )

    not_ends = {
        -1: (me > 0, me < n - 1, g > 0, g < ng - 1),
        1: (me < n - 1, me > 0, g < ng - 1, g > 0),
    }
    ghosts = [(z_copy, i, not_ends[way][0:2]) for i, (f, way) in enumerate(Z_GHOSTS)]
    ghosts += [(y_stress, i, not_ends[way][2:4]) for i, (f, way) in enumerate(Y_GHOSTS)]
    layers = [(c_copy, way, not_ends[way][0:2]) for way in (-1, 1)]
    def clear_stress():
        edge = jnp.zeros((depth + 2, line), f32)

        @pl.when(me == 0)
        def _():
            for f, way in Z_GHOSTS:
                if way < 0:
                    s_ext[f, 0, inner, :] = jnp.zeros((side, line), f32)

        @pl.when(me == n - 1)
        def _():
            for f, way in Z_GHOSTS:
                if way > 0:
                    s_ext[f, depth + 1, inner, :] = jnp.zeros((side, line), f32)

        @pl.when(g == 0)
        def _():
            for f, way in Y_GHOSTS:
                if way < 0:
                    s_ext[f, :, above, :] = edge

        @pl.when(g == ng - 1)
        def _():
            for f, way in Y_GHOSTS:
                if way > 0:
                    s_ext[f, :, below, :] = edge

    def clear_speeds():
        edge = jnp.zeros((depth + 2, line), f32)

        @pl.when(g == 0)
        def _():
            for f in range(3 * STEPS):
                v_ext[f, :, above, :] = edge

        @pl.when(g == ng - 1)
        def _():
            for f in range(3 * STEPS):
                v_ext[f, :, below, :] = edge
        for f in range(3):
            pout[f, 0] = jnp.zeros((ROWS, LANES), f32)
            pout[f, n * depth + 1] = jnp.zeros((ROWS, LANES), f32)

    def set_layers():
        for k in range(depth):
            for c, (table, scale) in enumerate(((lame_ref, grid_ratio), (shear_ref, grid_ratio), (relax_ref, 1.0))):
                coef[c, k + 1] = jnp.full((side, LANES), scale * table[layer_ref[k]], f32)
        for end, k in ((0, 0), (n - 1, depth + 1)):
            @pl.when(me == end)
            def _(k=k):
                for c in range(3):
                    coef[c, k] = jnp.zeros((side, LANES), f32)
        exchange(layers)

    def exchange(copies):
        for make, i, (gets, sends) in copies:
            @pl.when(sends)
            def _(make=make, i=i):
                make(i).start()

    def finish(copies):
        for make, i, (gets, sends) in copies:
            @pl.when(gets)
            def _(make=make, i=i):
                make(i).wait_recv()

            @pl.when(sends)
            def _(make=make, i=i):
                make(i).wait_send()

    def set_piers():
        ids = lax.broadcasted_iota(jnp.int32, (side, LANES), 0) + g * side
        lane_id = lax.broadcasted_iota(jnp.int32, (2 * LANES, LANES), 1)
        row_id = lax.broadcasted_iota(jnp.int32, (2 * LANES, LANES), 0) & (LANES - 1)
        first = jnp.full((1, LANES), -64, jnp.int32)
        begin_lane = jnp.full((1, LANES), -64, jnp.int32)
        begin_row = jnp.full((2 * LANES, LANES), -64, jnp.int32)
        for p in range(foot_ref.shape[0]):
            first = jnp.where(lane_id[0:1] == p, foot_ref[p, 0] // line, first)
            begin_lane = jnp.where(lane_id[0:1] == p, foot_ref[p, 0] % line, begin_lane)
            begin_row = jnp.where(row_id == p, foot_ref[p, 0] % line, begin_row)
        rows_of[...] = jnp.where((ids >= first) & (ids < first + SIDE), 1.0, 0.0)
        for c in range(tiles):
            at = row_id + c * LANES
            cols_t[c] = jnp.where((at >= begin_lane) & (at < begin_lane + SIDE), 1.0, 0.0).astype(bf16)
            at = lane_id + c * LANES
            cols_of[:, lanes(c)] = jnp.where((at >= begin_row) & (at < begin_row + SIDE), 1.0, 0.0).astype(bf16)
        square[...] = jnp.zeros((LANES, LANES), f32)
        square[pl.ds(0, own), pl.ds(0, depth)] = w_ref[...]
        wbuf[...] = pltpu.roll(jnp.transpose(square[...])[0:depth], g * own, 1)

    def halves(a):
        high = a.astype(bf16)
        return high, (a - high.astype(f32)).astype(bf16)

    def set_damping():
        high, low = halves(damp_ref[...])
        damp_cat[...] = jnp.concatenate([high, high, low], axis=1)
        damp_own[...] = jnp.zeros_like(damp_own)
        damp_own[pl.ds(1, depth), :] = damp_ref[pl.ds(pl.multiple_of(me * depth, depth), depth), :]

        @pl.when(me > 0)
        def _():
            damp_own[pl.ds(0, 1), :] = damp_ref[pl.ds(me * depth - 1, 1), :]

        @pl.when(me < n - 1)
        def _():
            damp_own[pl.ds(depth + 1, 1), :] = damp_ref[pl.ds((me + 1) * depth, 1), :]

    def own_impedance():
        impedance = jnp.zeros((ROWS, LANES), f32)
        for i in range(imp_ref.shape[0]):
            impedance = jnp.where(lax.broadcasted_iota(jnp.int32, (ROWS, LANES), 1) == g * own + i, imp_ref[i], impedance)
        return impedance

    def look(ref, f, k, count, c, dy=0, dz=0):
        return ref[f, pl.ds(k + dz, count), pl.ds(ROWS + dy, side), lanes(c)].reshape(count * side, LANES)

    def row(ref, f, c, at, dz=0):
        return ref[f, pl.ds(1 + dz, depth), at, lanes(c)]

    def ahead(get, c):
        cell = get(c)
        lane = lax.broadcasted_iota(jnp.int32, cell.shape, 1)
        other = 0.0 if c == tiles - 1 else pltpu.roll(get(c + 1), LANES - 1, 1)
        return jnp.where(lane == LANES - 1, other, pltpu.roll(cell, LANES - 1, 1))

    def behind(get, c):
        cell = get(c)
        lane = lax.broadcasted_iota(jnp.int32, cell.shape, 1)
        other = 0.0 if c == 0 else pltpu.roll(get(c - 1), 1, 1)
        return jnp.where(lane == 0, other, pltpu.roll(cell, 1, 1))

    def blocks(run, size=BLOCK):
        def at(i, carry):
            run(1 + i * size, size)
            return carry

        lax.fori_loop(0, depth // size, at, 0)

    def moduli(k, count):
        return [coef[c, pl.ds(k, count)].reshape(count * side, LANES) for c in range(3)]

    def put(ref, f, k, count, c, value):
        ref[f, pl.ds(k, count), inner, lanes(c)] = value.reshape(count, side, LANES)

    def early_speeds():
        def run(i, carry):
            k, count = 2 + 2 * i, 2
            at = functools.partial(look, s_ext)
            size = count * side
            scaled = grid_ratio * buoy[pl.ds(k - 1, count), :, lanes(0)].reshape(size, LANES)
            xx, yy, zz, xy, xz, yz = (at(f, k, count, 0) for f in range(6))
            total = (xx - behind(lambda c: at(0, k, count, c), 0)) + (pltpu.roll(xy, size - 1, 0) - xy)
            total = total + (at(4, k, count, 0, 0, 1) - xz)
            values = [total]
            total = (ahead(lambda c: at(3, k, count, c), 0) - xy) + (yy - pltpu.roll(yy, 1, 0))
            values.append(total + (at(5, k, count, 0, 0, 1) - yz))
            total = (ahead(lambda c: at(4, k, count, c), 0) - xz) + (pltpu.roll(yz, size - 1, 0) - yz)
            values.append(total + (zz - at(2, k, count, 0, 0, -1)))
            for f in range(3):
                value = look(v_ext, f, k, count, 0) + scaled * values[f]
                ahead_of[f, pl.ds(k - 1, count)] = value.reshape(count, side, LANES)
            return carry

        lax.fori_loop(0, (depth - 2) // 2, run, 0)

    def inner_peer(d):
        t = lax.rem(me + d, n)
        return t, (t > 0) & (t < n - 1)

    def early_copy(d, ref, low, count, at):
        t = lax.rem(me + d, n)
        return pltpu.make_async_remote_copy(
            src_ref=ref.at[:, pl.ds(low, count), mine(t), at],
            dst_ref=pin.at[:, pl.ds(me * depth + low, count), mine(0), :],
            send_sem=f_send.at[0, 0], recv_sem=f_recv.at[0, 0], device_id=(t, g), device_id_type=MESH,
        )

    def early_there():
        for d in range(1, n):
            @pl.when(inner_peer(d)[1])
            def _(d=d):
                early_copy(d, ahead_of, 1, depth - 2, pl.ds(0, LANES)).start()

    def late_there():
        for d in range(1, n):
            @pl.when(inner_peer(d)[1])
            def _(d=d):
                early_copy(d, acc, 0, 1, lanes(0)).start()
                early_copy(d, acc, depth - 1, 1, lanes(0)).start()

            @pl.when(jnp.logical_not(inner_peer(d)[1]))
            def _(d=d):
                there(0, 0, d).start()
        there(0, 0, 0).start()

    def speeds(step, c):
        base = 3 * (step - 1) if step > 0 else 0

        def run(k, count):
            at = functools.partial(look, s_ext)
            scaled = grid_ratio * buoy[pl.ds(k - 1, count), :, lanes(c)].reshape(count * side, LANES)
            xx, yy, zz, xy, xz, yz = (at(f, k, count, c) for f in range(6))
            total = (xx - behind(lambda c: at(0, k, count, c), c)) + (at(3, k, count, c, 1) - xy)
            total = total + (at(4, k, count, c, 0, 1) - xz)
            values = [total]
            total = (ahead(lambda c: at(3, k, count, c), c) - xy) + (yy - at(1, k, count, c, -1))
            values.append(total + (at(5, k, count, c, 0, 1) - yz))
            total = (ahead(lambda c: at(4, k, count, c), c) - xz) + (at(5, k, count, c, 1) - yz)
            values.append(total + (zz - at(2, k, count, c, 0, -1)))
            for f in range(3):
                value = look(v_ext, base + f, k, count, c) + scaled * values[f]
                acc[f, pl.ds(k - 1, count), :, lanes(c)] = value.reshape(count, side, LANES)

        blocks(run)

    def pier_part(c):
        high, low = halves(acc[2, :, :, lanes(c)].reshape(depth * side, LANES))
        term = jnp.dot(jnp.concatenate([high, low], axis=1), cols_t[c], preferred_element_type=f32)
        part[...] = term if c == 0 else part[...] + term

    def shears(step, c, with_ghosts, which=(3, 4, 5)):
        at = functools.partial(look, v_ext)
        x, y, z = (3 * step + f for f in range(3))

        def run(k, count, which=which):
            lame, shear, relax = moduli(k, count)
            for f in which:
                if f == 3:
                    strain = (at(x, k, count, c) - at(x, k, count, c, -1)) + (
                        at(y, k, count, c) - behind(lambda c: at(y, k, count, c), c)
                    )
                elif f == 4:
                    strain = (at(x, k, count, c) - at(x, k, count, c, 0, -1)) + (
                        at(z, k, count, c) - behind(lambda c: at(z, k, count, c), c)
                    )
                else:
                    strain = (at(y, k, count, c) - at(y, k, count, c, 0, -1)) + (
                        at(z, k, count, c) - at(z, k, count, c, -1)
                    )
                put(s_ext, f, k, count, c, relax * look(s_ext, f, k, count, c) + shear * strain)

        blocks(run)
        if with_ghosts:
            run(depth + 1, 1, (4, 5))
            shear, relax = (coef[i, pl.ds(1, depth), 0, :] for i in (1, 2))
            y_at = functools.partial(row, v_ext, y, at=below)
            strain = (row(v_ext, x, c, below) - row(v_ext, x, c, below - 1)) + (
                y_at(c) - behind(lambda c: y_at(c), c)
            )
            xy = relax * row(s_ext, 3, c, below) + shear * strain
            strain = (y_at(c) - y_at(c, dz=-1)) + (row(v_ext, z, c, below) - row(v_ext, z, c, below - 1))
            yz = relax * row(s_ext, 5, c, below) + shear * strain
            s_ext[3, pl.ds(1, depth), below, lanes(c)] = jnp.where(g == ng - 1, 0.0, xy)
            s_ext[5, pl.ds(1, depth), below, lanes(c)] = jnp.where(g == ng - 1, 0.0, yz)

    def normals(step, c, with_ghosts):
        at = functools.partial(look, v_ext)
        x, y, z = (3 * step + f for f in range(3))

        def run(k, count, which=(0, 1, 2)):
            lame, shear, relax = moduli(k, count)
            ex = ahead(lambda c: at(x, k, count, c), c) - at(x, k, count, c)
            ey = at(y, k, count, c, 1) - at(y, k, count, c)
            ez = at(z, k, count, c, 0, 1) - at(z, k, count, c)
            trace = lame * ((ex + ey) + ez)
            twice = shear + shear
            for f in which:
                value = relax * look(s_ext, f, k, count, c) + (twice * (ex, ey, ez)[f] + trace)
                put(s_ext, f, k, count, c, value)

        blocks(run)
        if with_ghosts:
            run(0, 1, (2,))
            lame, shear, relax = (coef[i, pl.ds(1, depth), 0, :] for i in range(3))
            x_at = functools.partial(row, v_ext, x, at=above)
            ex = ahead(lambda c: x_at(c), c) - x_at(c)
            ey = row(v_ext, y, c, ROWS) - row(v_ext, y, c, above)
            ez = row(v_ext, z, c, above, 1) - row(v_ext, z, c, above)
            yy = relax * row(s_ext, 1, c, above) + ((shear + shear) * ey + lame * ((ex + ey) + ez))
            s_ext[1, pl.ds(1, depth), above, lanes(c)] = jnp.where(g == 0, 0.0, yy)

    def mine(t):
        return pl.ds(t * share_rows, share_rows)

    def there(step, c, d):
        t = lax.rem(me + d, n)
        src = acc.at[:, :, mine(t), lanes(c)]
        dst = pin.at[:, pl.ds(me * depth, depth), mine(c), :]
        if d == 0:
            return pltpu.make_async_copy(src, dst, f_recv.at[step, c])
        return pltpu.make_async_remote_copy(
            src_ref=src, dst_ref=dst, send_sem=f_send.at[step, c],
            recv_sem=f_recv.at[step, c], device_id=(t, g), device_id_type=MESH,
        )

    def back(step, c, d):
        t = lax.rem(me + d, n)
        pieces = ((0, 3, 0, depth + 2),)
        if step == STEPS - 1:
            pieces = ((0, 2, 0, depth + 1), (2, 1, 1, depth + 1))
        copies = []
        for f, fields, low, count in pieces:
            src = pout.at[pl.ds(f, fields), pl.ds(t * depth + low, count), mine(c), :]
            dst = v_ext.at[
                pl.ds(3 * step + f, fields), pl.ds(low, count), pl.ds(ROWS + me * share_rows, share_rows), lanes(c)
            ]
            if d == 0:
                copies.append(pltpu.make_async_copy(src, dst, r_recv.at[step, c]))
            else:
                copies.append(pltpu.make_async_remote_copy(
                    src_ref=src, dst_ref=dst, send_sem=r_send.at[step, c],
                    recv_sem=r_recv.at[step, c], device_id=(t, g), device_id_type=MESH,
                ))
        return copies

    def count_back(step):
        return depth + (1 if step == STEPS - 1 else 2)

    def start_there(step, c):
        for d in list(range(1, n)) + [0]:
            there(step, c, d).start()

    def start_back(step, c):
        for d in list(range(1, n)) + [0]:
            for copy in back(step, c, d):
                copy.start()

    def sent_there(step, c):
        settle(pin.at[:, pl.ds(0, (n - 1) * depth), mine(c), :], f_send.at[step, c])

    def got_there(step, c):
        settle(pin.at[:, :, mine(c), :], f_recv.at[step, c])

    def sent_back(step, c):
        settle(pout.at[:, pl.ds(0, (n - 1) * count_back(step)), mine(c), :], r_send.at[step, c])

    def got_back(step, c):
        settle(
            v_ext.at[pl.ds(3 * step, 3), pl.ds(0, count_back(step)), inner, lanes(c)], r_recv.at[step, c]
        )

    def damp(step, c):
        got_there(step, c)
        if step > 0:
            sent_back(step - 1, c)
        for f in range(3):
            terms = []
            for r in range(share_rows):
                high, low = halves(pin[f, :, share_rows * c + r, :])
                terms.append(jnp.concatenate([high, low, high], axis=0))
            damped = jnp.dot(damp_cat[...], jnp.concatenate(terms, axis=1), preferred_element_type=f32)
            for r in range(share_rows):
                pout[f, pl.ds(1, n * depth), share_rows * c + r, :] = damped[:, r * LANES : (r + 1) * LANES]
        start_back(step, c)

    def shared(step):
        return pl.ds(0, stage_rows if step == 0 else depth)

    def share(step, d):
        return pltpu.make_async_remote_copy(
            src_ref=um.at[step, 0, shared(step)], dst_ref=um.at[step, d, shared(step)],
            send_sem=u_send.at[step], recv_sem=u_recv.at[step],
            device_id=(me, lax.rem(g + d, ng)), device_id_type=MESH,
        )

    def forces(step, d):
        block = pl.ds(pl.multiple_of(me * depth, depth), depth)
        return pltpu.make_async_remote_copy(
            src_ref=fall.at[step, block], dst_ref=fall.at[step, block],
            send_sem=p_send.at[step], recv_sem=p_recv.at[step],
            device_id=(lax.rem(me + d, n), g), device_id_type=MESH,
        )

    def pier_means(step):
        masked = part[...].reshape(depth, side, LANES) * rows_of[...][None]
        um[step, 0, pl.ds(0, depth), :] = jnp.sum(masked, axis=1)
        if step == 0:
            um[step, 0, pl.ds(depth, depth), :] = wbuf[...]
            um[step, 0, pl.ds(2 * depth, ROWS), :] = own_impedance()
        for d in range(1, ng):
            share(step, d).start()

    def pier_forces(step):
        settle(um.at[step, pl.ds(1, ng - 1), shared(step)], u_recv.at[step])
        settle(um.at[step, pl.ds(1, ng - 1), shared(step)], u_send.at[step])
        every = um[step, 0, shared(step), :]
        for d in range(1, ng):
            every = every + um[step, d, shared(step), :]
        if step == 0:
            wbuf[...] = every[depth : 2 * depth]
            gain[...] = every[2 * depth :]
        w = wbuf[...]
        force = gain[0:1, :] * (w - every[0:depth] / FOOT)
        wbuf[...] = w - pier_gain * force
        fall[step, pl.ds(pl.multiple_of(me * depth, depth), depth), :] = soil_gain * force
        for d in range(1, n):
            forces(step, d).start()

    def pier_spread(step):
        settle(fall.at[step, pl.ds(0, (n - 1) * depth)], p_recv.at[step])
        settle(fall.at[step, pl.ds(0, (n - 1) * depth)], p_send.at[step])
        pushed = jnp.dot(
            damp_own[...], fall[step], precision=lax.Precision.HIGHEST, preferred_element_type=f32
        )[0 : depth + 2]
        wide = (pushed[:, None, :] * rows_of[...][None]).reshape((depth + 2) * side, LANES)
        spread[...] = jnp.concatenate(halves(wide), axis=1)

    def y_speed(step, c, i):
        low, count = (0, depth + 2) if step < STEPS - 1 else (1, depth)
        fields, planes = pl.ds(3 * step, 3), pl.ds(low, count)
        return pltpu.make_async_remote_copy(
            src_ref=v_ext.at[fields, planes, pl.ds(below - 1 if i == 0 else ROWS, 1), lanes(c)],
            dst_ref=v_ext.at[fields, planes, pl.ds(above if i == 0 else below, 1), lanes(c)],
            send_sem=y_send.at[step, c, i], recv_sem=y_recv.at[step, c, i],
            device_id=(me, g + 1 - 2 * i), device_id_type=MESH,
        )

    has_next, has_last = g < ng - 1, g > 0

    def arrive(step, c):
        got_back(step, c)
        low, count = (0, depth + 2) if step < STEPS - 1 else (1, depth + 1)
        term = jnp.dot(
            spread[pl.ds(low * side, count * side), :], cols_of[:, lanes(c)], preferred_element_type=f32
        )
        put(v_ext, 3 * step + 2, low, count, c, look(v_ext, 3 * step + 2, low, count, c) + term)

        @pl.when(has_next)
        def _():
            y_speed(step, c, 0).start()

        @pl.when(has_last)
        def _():
            y_speed(step, c, 1).start()

    def edges(step, c):
        @pl.when(has_last)
        def _():
            y_speed(step, c, 0).wait_recv()
            y_speed(step, c, 1).wait_send()

        @pl.when(has_next)
        def _():
            y_speed(step, c, 1).wait_recv()
            y_speed(step, c, 0).wait_send()

    def load(c):
        for copy in loads[c]:
            copy.wait()

    last = tiles - 1

    def first_speeds(c):
        if 0 < c < last:
            load(c + 1)
        speeds(0, c)

    def next_speeds(step, c):
        sent_there(step - 1, c)
        speeds(step, c)
        if c == last:
            pier_part(c)
            pier_means(step)
        start_there(step, c)
        if c < last:
            pier_part(c)

    exchange(ghosts)
    for copy in smalls:
        copy.wait()
    load(0)
    load(1)
    early_speeds()
    early_there()
    clear_stress()
    finish(ghosts)
    first_speeds(0)
    late_there()
    set_piers()
    for c in range(1, tiles):
        first_speeds(c)
    for c in range(tiles):
        pier_part(c)
    pier_means(0)
    start_there(0, 1)
    set_layers()
    set_damping()
    clear_speeds()

    def next_stress(c):
        normals(0, c, True)
        next_speeds(1, c)

    def bend(step, c):
        edges(step, c)
        shears(step, c, step < STEPS - 1)

    pier_forces(0)
    damp(0, 0)
    start_there(0, 2)
    damp(0, 1)
    start_there(0, 3)
    pier_spread(0)
    damp(0, 2)
    damp(0, 3)
    finish(layers)
    arrive(0, 0)
    arrive(0, 1)
    bend(0, 0)
    arrive(0, 2)
    bend(0, 1)
    next_stress(0)
    arrive(0, 3)
    bend(0, 2)
    next_stress(1)
    bend(0, 3)
    next_stress(2)
    next_stress(3)
    damp(1, 0)
    pier_forces(1)
    damp(1, 1)
    damp(1, 2)
    pier_spread(1)
    damp(1, 3)
    arrive(1, 0)
    arrive(1, 1)
    bend(1, 0)
    arrive(1, 2)
    bend(1, 1)
    normals(1, 0, False)
    arrive(1, 3)
    bend(1, 2)
    normals(1, 1, False)
    normals(1, 2, False)
    bend(1, 3)
    normals(1, 3, False)

    square[...] = jnp.zeros((LANES, LANES), f32)
    square[pl.ds(0, depth), :] = pltpu.roll(wbuf[...], lax.rem(LANES - g * own, LANES), 1)
    w_out[...] = jnp.transpose(square[...])[0:own, 0:depth]
    for c in range(tiles):
        sent_there(STEPS - 1, c)
        sent_back(STEPS - 1, c)


def deliver(v_ref, s_ref, w_ref, v_out, s_out, w_out, sem):
    depth, side = v_out.shape[1:3]
    inside = pl.ds(1, depth), pl.ds(ROWS, side)
    pairs = [(w_ref, w_out)]
    pairs += [(s_ref.at[(f,) + inside], s_out.at[f]) for f in range(6)]
    pairs += [(v_ref.at[(3 * (STEPS - 1) + f,) + inside], v_out.at[f]) for f in range(3)]
    copies = [pltpu.make_async_copy(a, b, sem.at[i]) for i, (a, b) in enumerate(pairs)]
    for copy in copies:
        copy.start()
    for copy in copies:
        copy.wait()


def fused_body(
    n, ng, velocity, stress, pier_velocity, buoyancy, layer, lame_table, shear_table, relax_table,
    impedance, footprint, damp_inverse,
):
    depth, side, line = buoyancy.shape
    own = pier_velocity.shape[1]
    f32 = jnp.float32
    hbm = pl.BlockSpec(memory_space=pltpu.HBM)
    vmem = pl.BlockSpec(memory_space=pltpu.VMEM)
    dma = pltpu.SemaphoreType.DMA
    tall = side + 2 * ROWS
    stage = 2 * depth + ROWS
    tiles = line // LANES
    v, s, w = pl.pallas_call(
        functools.partial(fused, n, ng),
        out_shape=(
            pltpu.VMEM((3 * STEPS, depth + 2, tall, line), f32),
            pltpu.VMEM((6, depth + 2, tall, line), f32),
            pltpu.VMEM((own, depth), f32),
        ),
        in_specs=[hbm] * 11,
        out_specs=(vmem, vmem, vmem),
        scratch_shapes=[
            pltpu.SMEM(layer.shape, layer.dtype),
            pltpu.SMEM(lame_table.shape, f32),
            pltpu.SMEM(shear_table.shape, f32),
            pltpu.SMEM(relax_table.shape, f32),
            pltpu.SMEM(footprint.shape, footprint.dtype),
            pltpu.VMEM((own, depth), f32),
            pltpu.SMEM(impedance.shape, f32),
            pltpu.VMEM(damp_inverse.shape, f32),
            dma((8,)),
            pltpu.VMEM((depth, side, line), f32),
            pltpu.VMEM((3, depth + 2, side, LANES), f32),
            pltpu.VMEM((3, depth, side, line), f32),
            pltpu.VMEM((3, depth, side, LANES), f32),
            pltpu.VMEM((3, n * depth, ROWS, LANES), f32),
            pltpu.VMEM((3, n * depth + 2, ROWS, LANES), f32),
            pltpu.VMEM((STEPS, ng, stage, LANES), f32),
            pltpu.VMEM((STEPS, n * depth, LANES), f32),
            pltpu.VMEM((depth, LANES), f32),
            pltpu.VMEM((ROWS, LANES), f32),
            pltpu.VMEM((LANES, LANES), f32),
            pltpu.VMEM((depth * side, LANES), f32),
            pltpu.VMEM((side, LANES), f32),
            pltpu.VMEM((tiles, 2 * LANES, LANES), jnp.bfloat16),
            pltpu.VMEM((2 * LANES, line), jnp.bfloat16),
            pltpu.VMEM(((depth + 2) * side, 2 * LANES), jnp.bfloat16),
            pltpu.VMEM((n * depth, 3 * n * depth), jnp.bfloat16),
            pltpu.VMEM((depth + ROWS, n * depth), f32),
            dma((3 * tiles,)), dma((3,)), dma((3,)), dma((2,)), dma((2,)), dma((3,)), dma((3,)),
            dma((STEPS, tiles)), dma((STEPS, tiles)), dma((STEPS, tiles)), dma((STEPS, tiles)),
            dma((STEPS,)), dma((STEPS,)), dma((STEPS,)), dma((STEPS,)),
            dma((STEPS, tiles, 2)), dma((STEPS, tiles, 2)),
        ],
        compiler_params=pltpu.CompilerParams(
            collective_id=0, has_side_effects=True, vmem_limit_bytes=48 * 1024 * 1024
        ),
    )(
        velocity, stress, buoyancy, layer, lame_table, shear_table, relax_table,
        footprint, pier_velocity.T, impedance, damp_inverse,
    )
    v, s, w = pl.pallas_call(
        deliver,
        out_shape=tuple(
            jax.ShapeDtypeStruct(a, f32) for a in (velocity.shape, stress.shape, (own, depth))
        ),
        in_specs=[vmem] * 3,
        out_specs=(hbm,) * 3,
        scratch_shapes=[dma((10,))],
        compiler_params=pltpu.CompilerParams(vmem_limit_bytes=8 * 1024 * 1024),
    )(v, s, w)
    return v, s, w.T


def whole_tiles(mesh, velocity, pier_velocity):
    n, ng = mesh.shape["gx"], mesh.shape["gy"]
    depth, side, line = velocity.shape[1] // n, velocity.shape[2] // ng, velocity.shape[3]
    return (
        line % LANES == 0
        and side % 16 == 0
        and side % n == 0
        and depth % ROWS == 0
        and (side // n) * (line // LANES) == ROWS
        and n * depth % LANES == 0
        and pier_velocity.shape[1] <= LANES
    )


def solution(mesh):
    placed = (
        P(None, "gx", "gy", None),
        P(None, "gx", "gy", None),
        P("gx", "gy"),
        P("gx", "gy", None),
        P("gx"),
        P(),
        P(),
        P(),
        P("gy"),
        P(),
        P(),
    )

    def run(*args):
        n, ng = mesh.shape["gx"], mesh.shape["gy"]
        if whole_tiles(mesh, args[0], args[2]):
            part = functools.partial(fused_body, n, ng)
        else:
            part = body
        return mapped(part)(*args)

    def mapped(part):
        return jax.shard_map(
            part,
            mesh=mesh,
            in_specs=placed,
            out_specs=(P(None, "gx", "gy", None), P(None, "gx", "gy", None), P("gx", "gy")),
            check_vma=False,
        )

    return run
```

```python
import functools
import jax
import jax.numpy as jnp
from jax import lax
from jax.experimental import pallas as pl
from jax.experimental.pallas import tpu as pltpu
from jax.sharding import PartitionSpec as P

STEPS = 2
FOOT = 16


grid_ratio = 0.25
soil_gain = 0.2
pier_gain = 0.5


def extended(cells, sides, width):
    for axis, dim in sides:
        count = lax.axis_size(axis)
        ends = count - 1
        head = lax.slice_in_dim(cells, 0, width, axis=dim)
        tail = lax.slice_in_dim(cells, cells.shape[dim] - width, cells.shape[dim], axis=dim)
        cells = jnp.concatenate(
            [
                lax.ppermute(tail, axis, [(i, (i + 1) % count) for i in range(ends)]),
                cells,
                lax.ppermute(head, axis, [((i + 1) % count, i) for i in range(ends)]),
            ],
            axis=dim,
        )
    return cells


def forward_diff(padded, along):
    center = padded[1:-1, 1:-1, 1:-1]
    if along == 0:
        return padded[2:, 1:-1, 1:-1] - center
    if along == 1:
        return padded[1:-1, 2:, 1:-1] - center
    return padded[1:-1, 1:-1, 2:] - center


def backward_diff(padded, along):
    center = padded[1:-1, 1:-1, 1:-1]
    if along == 0:
        return center - padded[:-2, 1:-1, 1:-1]
    if along == 1:
        return center - padded[1:-1, :-2, 1:-1]
    return center - padded[1:-1, 1:-1, :-2]


def move_velocity(velocity, padded, buoyancy):
    scaled = grid_ratio * buoyancy
    first = velocity[0] + scaled * (
        backward_diff(padded[0], 2) + forward_diff(padded[3], 1) + forward_diff(padded[4], 0)
    )
    second = velocity[1] + scaled * (
        forward_diff(padded[3], 2) + backward_diff(padded[1], 1) + forward_diff(padded[5], 0)
    )
    third = velocity[2] + scaled * (
        forward_diff(padded[4], 2) + forward_diff(padded[5], 1) + backward_diff(padded[2], 0)
    )
    return jnp.stack([first, second, third])


def move_stress(stress, padded, lame_first, shear_mod, relax):
    strain_x = forward_diff(padded[0], 2)
    strain_y = forward_diff(padded[1], 1)
    strain_z = forward_diff(padded[2], 0)
    modulus = lame_first + 2.0 * shear_mod
    normal_x = relax * stress[0] + grid_ratio * (
        modulus * strain_x + lame_first * (strain_y + strain_z)
    )
    normal_y = relax * stress[1] + grid_ratio * (
        modulus * strain_y + lame_first * (strain_x + strain_z)
    )
    normal_z = relax * stress[2] + grid_ratio * (
        modulus * strain_z + lame_first * (strain_x + strain_y)
    )
    shear_xy = relax * stress[3] + grid_ratio * shear_mod * (
        backward_diff(padded[0], 1) + backward_diff(padded[1], 2)
    )
    shear_xz = relax * stress[4] + grid_ratio * shear_mod * (
        backward_diff(padded[0], 0) + backward_diff(padded[2], 2)
    )
    shear_yz = relax * stress[5] + grid_ratio * shear_mod * (
        backward_diff(padded[1], 0) + backward_diff(padded[2], 1)
    )
    return jnp.stack([normal_x, normal_y, normal_z, shear_xy, shear_xz, shear_yz])


def layer_values(layer, table):
    levels = jnp.arange(table.shape[0], dtype=jnp.int32)
    onehot = (layer[:, None] == levels[None, :]).astype(table.dtype)
    return jnp.sum(onehot * table[None, :], axis=1)[:, None, None]


def with_faces(fields):
    padded = extended(fields, (("gx", 1), ("gy", 2)), 1)
    return jnp.pad(padded, ((0, 0), (0, 0), (0, 0), (1, 1)))


def footprint_matches(cell_ids, footprint):
    piers = footprint.shape[0]
    equal = (cell_ids[:, None] == footprint.reshape(-1)[None, :]).astype(jnp.float32)
    return jnp.sum(equal.reshape(cell_ids.shape[0], piers, FOOT), axis=2)


def damp_columns(velocity, inverse):
    pencils = lax.all_to_all(velocity, "gx", split_axis=3, concat_axis=1, tiled=True)
    shape = pencils.shape
    flat = pencils.reshape(shape[0], shape[1], shape[2] * shape[3])
    damped = jnp.einsum("zk,fkm->fzm", inverse, flat, precision=lax.Precision.HIGHEST).reshape(
        shape
    )
    return lax.all_to_all(damped, "gx", split_axis=1, concat_axis=3, tiled=True)


def body(
    velocity,
    stress,
    pier_velocity,
    buoyancy,
    layer,
    lame_table,
    shear_table,
    relax_table,
    impedance,
    footprint,
    damp_inverse,
):
    depth_cells, side_cells, line_cells = (velocity.shape[1], velocity.shape[2], velocity.shape[3])
    own_piers = pier_velocity.shape[1]
    lame_first = layer_values(layer, lame_table)
    shear_mod = layer_values(layer, shear_table)
    relax = layer_values(layer, relax_table)
    row_start = lax.axis_index("gy") * side_cells
    cell_ids = row_start * line_cells + jnp.arange(side_cells * line_cells, dtype=jnp.int32)
    selector = footprint_matches(cell_ids, footprint)
    own_foot = lax.dynamic_slice_in_dim(footprint, lax.axis_index("gy") * own_piers, own_piers, 0)
    for time_step in range(STEPS):
        padded = with_faces(stress)
        velocity = move_velocity(velocity, padded, buoyancy)
        vertical = velocity[2].reshape(depth_cells, side_cells * line_cells)
        piece = lax.all_gather(velocity[2], "gy", axis=1, tiled=True)
        count = piece.shape[1]
        piece_ids = jnp.arange(count * line_cells, dtype=jnp.int32)
        picks = footprint_matches(piece_ids, own_foot)
        flat = piece.reshape(depth_cells, count * line_cells)
        summed = jnp.dot(
            flat, picks, precision=lax.Precision.HIGHEST, preferred_element_type=jnp.float32
        )
        mean_speed = summed / FOOT
        force = impedance[None, :] * (pier_velocity - mean_speed)
        pier_velocity = pier_velocity - pier_gain * force
        all_force = lax.all_gather(force, "gy", axis=1, tiled=True)
        pushed = jnp.dot(
            all_force,
            selector.T,
            precision=lax.Precision.HIGHEST,
            preferred_element_type=jnp.float32,
        )
        vertical = vertical + soil_gain * pushed
        velocity = jnp.stack(
            [velocity[0], velocity[1], vertical.reshape(depth_cells, side_cells, line_cells)]
        )
        velocity = damp_columns(velocity, damp_inverse)
        padded = with_faces(velocity)
        stress = move_stress(stress, padded, lame_first, shear_mod, relax)
    return (velocity, stress, pier_velocity)


SIDE = 4
LANES = 128
ROWS = 8
BLOCK = 4
MESH = pl.DeviceIdType.MESH
Z_GHOSTS = ((2, -1), (4, 1), (5, 1))
Y_GHOSTS = ((1, -1), (3, 1), (5, 1))


def fused(
    n, ng, v_hbm, s_hbm, b_hbm, layer_hbm, lame_hbm, shear_hbm, relax_hbm, foot_hbm, w_hbm, imp_hbm, damp_hbm,
    v_ext, s_ext, w_out,
    layer_ref, lame_ref, shear_ref, relax_ref, foot_ref, w_ref, imp_ref, damp_ref, small_sem,
    buoy, coef, acc, ahead_of, pin, pout, um, fall, wbuf, gain, square, part, rows_of, cols_t, cols_of, spread, damp_cat, damp_own,
    load_sem, zs_send, zs_recv, cf_send, cf_recv, ys_send, ys_recv,
    f_send, f_recv, r_send, r_recv, u_send, u_recv, p_send, p_recv, y_send, y_recv,
):
    me = lax.axis_index("gx")
    g = lax.axis_index("gy")
    depth, side, line = buoy.shape
    tiles = line // LANES
    share_rows = side // n
    inner = pl.ds(ROWS, side)
    own = w_ref.shape[0]
    stage_rows = um.shape[2]
    f32, bf16 = jnp.float32, jnp.bfloat16
    above, below = ROWS - 1, ROWS + side

    def lanes(c):
        return pl.ds(c * LANES, LANES)

    def settle(ref, sem):
        pltpu.make_async_copy(ref, ref, sem).wait()

    loads = []
    for c in range(tiles):
        loads.append((
            pltpu.make_async_copy(
                s_hbm.at[:, :, :, lanes(c)], s_ext.at[:, pl.ds(1, depth), inner, lanes(c)], load_sem.at[c]
            ),
            pltpu.make_async_copy(b_hbm.at[:, :, lanes(c)], buoy.at[:, :, lanes(c)], load_sem.at[tiles + c]),
            pltpu.make_async_copy(
                v_hbm.at[:, :, :, lanes(c)], v_ext.at[pl.ds(0, 3), pl.ds(1, depth), inner, lanes(c)],
                load_sem.at[2 * tiles + c],
            ),
        ))
        for copy in loads[c]:
            copy.start()

    smalls = [
        pltpu.make_async_copy(src, dst, small_sem.at[i])
        for i, (src, dst) in enumerate((
            (layer_hbm, layer_ref), (lame_hbm, lame_ref), (shear_hbm, shear_ref), (relax_hbm, relax_ref),
            (foot_hbm, foot_ref), (w_hbm, w_ref), (imp_hbm, imp_ref), (damp_hbm, damp_ref),
        ))
    ]
    for copy in smalls:
        copy.start()
    barrier = pltpu.get_barrier_semaphore()
    for d in range(1, n):
        pl.semaphore_signal(
            barrier, inc=1, device_id=(lax.rem(me + d, n), g), device_id_type=MESH
        )
    for d in range(1, ng):
        pl.semaphore_signal(
            barrier, inc=1, device_id=(me, lax.rem(g + d, ng)), device_id_type=MESH
        )
    pl.semaphore_wait(barrier, n - 1 + ng - 1)

    def z_copy(i):
        f, way = Z_GHOSTS[i]
        return pltpu.make_async_remote_copy(
            src_ref=s_hbm.at[f, depth - 1 if way < 0 else 0],
            dst_ref=s_ext.at[f, 0 if way < 0 else depth + 1, inner, :],
            send_sem=zs_send.at[i], recv_sem=zs_recv.at[i],
            device_id=(me - way, g), device_id_type=MESH,
        )

    def c_copy(way):
        i = (way + 1) // 2
        return pltpu.make_async_remote_copy(
            src_ref=coef.at[:, depth if way < 0 else 1],
            dst_ref=coef.at[:, 0 if way < 0 else depth + 1],
            send_sem=cf_send.at[i], recv_sem=cf_recv.at[i],
            device_id=(me - way, g), device_id_type=MESH,
        )

    def y_stress(i):
        f, way = Y_GHOSTS[i]
        return pltpu.make_async_remote_copy(
            src_ref=s_hbm.at[f, :, pl.ds(side - 1 if way < 0 else 0, 1), :],
            dst_ref=s_ext.at[f, pl.ds(1, depth), pl.ds(above if way < 0 else below, 1), :],
            send_sem=ys_send.at[i], recv_sem=ys_recv.at[i],
            device_id=(me, g - way), device_id_type=MESH,
        )

    not_ends = {
        -1: (me > 0, me < n - 1, g > 0, g < ng - 1),
        1: (me < n - 1, me > 0, g < ng - 1, g > 0),
    }
    ghosts = [(z_copy, i, not_ends[way][0:2]) for i, (f, way) in enumerate(Z_GHOSTS)]
    ghosts += [(y_stress, i, not_ends[way][2:4]) for i, (f, way) in enumerate(Y_GHOSTS)]
    layers = [(c_copy, way, not_ends[way][0:2]) for way in (-1, 1)]
    def clear_stress():
        edge = jnp.zeros((depth + 2, line), f32)

        @pl.when(me == 0)
        def _():
            for f, way in Z_GHOSTS:
                if way < 0:
                    s_ext[f, 0, inner, :] = jnp.zeros((side, line), f32)

        @pl.when(me == n - 1)
        def _():
            for f, way in Z_GHOSTS:
                if way > 0:
                    s_ext[f, depth + 1, inner, :] = jnp.zeros((side, line), f32)

        @pl.when(g == 0)
        def _():
            for f, way in Y_GHOSTS:
                if way < 0:
                    s_ext[f, :, above, :] = edge

        @pl.when(g == ng - 1)
        def _():
            for f, way in Y_GHOSTS:
                if way > 0:
                    s_ext[f, :, below, :] = edge

    def clear_speeds():
        edge = jnp.zeros((depth + 2, line), f32)

        @pl.when(g == 0)
        def _():
            for f in range(3 * STEPS):
                v_ext[f, :, above, :] = edge

        @pl.when(g == ng - 1)
        def _():
            for f in range(3 * STEPS):
                v_ext[f, :, below, :] = edge
        for f in range(3):
            pout[f, 0] = jnp.zeros((ROWS, LANES), f32)
            pout[f, n * depth + 1] = jnp.zeros((ROWS, LANES), f32)

    def set_layers():
        for k in range(depth):
            for c, (table, scale) in enumerate(((lame_ref, grid_ratio), (shear_ref, grid_ratio), (relax_ref, 1.0))):
                coef[c, k + 1] = jnp.full((side, LANES), scale * table[layer_ref[k]], f32)
        for end, k in ((0, 0), (n - 1, depth + 1)):
            @pl.when(me == end)
            def _(k=k):
                for c in range(3):
                    coef[c, k] = jnp.zeros((side, LANES), f32)
        exchange(layers)

    def exchange(copies):
        for make, i, (gets, sends) in copies:
            @pl.when(sends)
            def _(make=make, i=i):
                make(i).start()

    def finish(copies):
        for make, i, (gets, sends) in copies:
            @pl.when(gets)
            def _(make=make, i=i):
                make(i).wait_recv()

            @pl.when(sends)
            def _(make=make, i=i):
                make(i).wait_send()

    def set_piers():
        ids = lax.broadcasted_iota(jnp.int32, (side, LANES), 0) + g * side
        lane_id = lax.broadcasted_iota(jnp.int32, (2 * LANES, LANES), 1)
        row_id = lax.broadcasted_iota(jnp.int32, (2 * LANES, LANES), 0) & (LANES - 1)
        first = jnp.full((1, LANES), -64, jnp.int32)
        begin_lane = jnp.full((1, LANES), -64, jnp.int32)
        begin_row = jnp.full((2 * LANES, LANES), -64, jnp.int32)
        for p in range(foot_ref.shape[0]):
            first = jnp.where(lane_id[0:1] == p, foot_ref[p, 0] // line, first)
            begin_lane = jnp.where(lane_id[0:1] == p, foot_ref[p, 0] % line, begin_lane)
            begin_row = jnp.where(row_id == p, foot_ref[p, 0] % line, begin_row)
        rows_of[...] = jnp.where((ids >= first) & (ids < first + SIDE), 1.0, 0.0)
        for c in range(tiles):
            at = row_id + c * LANES
            cols_t[c] = jnp.where((at >= begin_lane) & (at < begin_lane + SIDE), 1.0, 0.0).astype(bf16)
            at = lane_id + c * LANES
            cols_of[:, lanes(c)] = jnp.where((at >= begin_row) & (at < begin_row + SIDE), 1.0, 0.0).astype(bf16)
        square[...] = jnp.zeros((LANES, LANES), f32)
        square[pl.ds(0, own), pl.ds(0, depth)] = w_ref[...]
        wbuf[...] = pltpu.roll(jnp.transpose(square[...])[0:depth], g * own, 1)

    def halves(a):
        high = a.astype(bf16)
        return high, (a - high.astype(f32)).astype(bf16)

    def set_damping():
        high, low = halves(damp_ref[...])
        damp_cat[...] = jnp.concatenate([high, high, low], axis=1)
        damp_own[...] = jnp.zeros_like(damp_own)
        damp_own[pl.ds(1, depth), :] = damp_ref[pl.ds(pl.multiple_of(me * depth, depth), depth), :]

        @pl.when(me > 0)
        def _():
            damp_own[pl.ds(0, 1), :] = damp_ref[pl.ds(me * depth - 1, 1), :]

        @pl.when(me < n - 1)
        def _():
            damp_own[pl.ds(depth + 1, 1), :] = damp_ref[pl.ds((me + 1) * depth, 1), :]

    def own_impedance():
        impedance = jnp.zeros((ROWS, LANES), f32)
        for i in range(imp_ref.shape[0]):
            impedance = jnp.where(lax.broadcasted_iota(jnp.int32, (ROWS, LANES), 1) == g * own + i, imp_ref[i], impedance)
        return impedance

    def look(ref, f, k, count, c, dy=0, dz=0):
        return ref[f, pl.ds(k + dz, count), pl.ds(ROWS + dy, side), lanes(c)].reshape(count * side, LANES)

    def row(ref, f, c, at, dz=0):
        return ref[f, pl.ds(1 + dz, depth), at, lanes(c)]

    def ahead(get, c):
        cell = get(c)
        lane = lax.broadcasted_iota(jnp.int32, cell.shape, 1)
        other = 0.0 if c == tiles - 1 else pltpu.roll(get(c + 1), LANES - 1, 1)
        return jnp.where(lane == LANES - 1, other, pltpu.roll(cell, LANES - 1, 1))

    def behind(get, c):
        cell = get(c)
        lane = lax.broadcasted_iota(jnp.int32, cell.shape, 1)
        other = 0.0 if c == 0 else pltpu.roll(get(c - 1), 1, 1)
        return jnp.where(lane == 0, other, pltpu.roll(cell, 1, 1))

    def blocks(run, size=BLOCK):
        def at(i, carry):
            run(1 + i * size, size)
            return carry

        lax.fori_loop(0, depth // size, at, 0)

    def moduli(k, count):
        return [coef[c, pl.ds(k, count)].reshape(count * side, LANES) for c in range(3)]

    def put(ref, f, k, count, c, value):
        ref[f, pl.ds(k, count), inner, lanes(c)] = value.reshape(count, side, LANES)

    def early_speeds():
        def run(i, carry):
            k, count = 2 + 2 * i, 2
            at = functools.partial(look, s_ext)
            size = count * side
            scaled = grid_ratio * buoy[pl.ds(k - 1, count), :, lanes(0)].reshape(size, LANES)
            xx, yy, zz, xy, xz, yz = (at(f, k, count, 0) for f in range(6))
            total = (xx - behind(lambda c: at(0, k, count, c), 0)) + (pltpu.roll(xy, size - 1, 0) - xy)
            total = total + (at(4, k, count, 0, 0, 1) - xz)
            values = [total]
            total = (ahead(lambda c: at(3, k, count, c), 0) - xy) + (yy - pltpu.roll(yy, 1, 0))
            values.append(total + (at(5, k, count, 0, 0, 1) - yz))
            total = (ahead(lambda c: at(4, k, count, c), 0) - xz) + (pltpu.roll(yz, size - 1, 0) - yz)
            values.append(total + (zz - at(2, k, count, 0, 0, -1)))
            for f in range(3):
                value = look(v_ext, f, k, count, 0) + scaled * values[f]
                ahead_of[f, pl.ds(k - 1, count)] = value.reshape(count, side, LANES)
            return carry

        lax.fori_loop(0, (depth - 2) // 2, run, 0)

    def inner_peer(d):
        t = lax.rem(me + d, n)
        return t, (t > 0) & (t < n - 1)

    def early_copy(d, ref, low, count, at):
        t = lax.rem(me + d, n)
        return pltpu.make_async_remote_copy(
            src_ref=ref.at[:, pl.ds(low, count), mine(t), at],
            dst_ref=pin.at[:, pl.ds(me * depth + low, count), mine(0), :],
            send_sem=f_send.at[0], recv_sem=f_recv.at[0], device_id=(t, g), device_id_type=MESH,
        )

    def early_there():
        for d in range(1, n):
            @pl.when(inner_peer(d)[1])
            def _(d=d):
                early_copy(d, ahead_of, 1, depth - 2, pl.ds(0, LANES)).start()

    def late_there():
        for d in range(1, n):
            @pl.when(inner_peer(d)[1])
            def _(d=d):
                early_copy(d, acc, 0, 1, lanes(0)).start()
                early_copy(d, acc, depth - 1, 1, lanes(0)).start()

            @pl.when(jnp.logical_not(inner_peer(d)[1]))
            def _(d=d):
                there(0, 0, d).start()
        there(0, 0, 0).start()

    def speeds(step, c):
        base = 3 * (step - 1) if step > 0 else 0

        def run(k, count):
            at = functools.partial(look, s_ext)
            scaled = grid_ratio * buoy[pl.ds(k - 1, count), :, lanes(c)].reshape(count * side, LANES)
            xx, yy, zz, xy, xz, yz = (at(f, k, count, c) for f in range(6))
            total = (xx - behind(lambda c: at(0, k, count, c), c)) + (at(3, k, count, c, 1) - xy)
            total = total + (at(4, k, count, c, 0, 1) - xz)
            values = [total]
            total = (ahead(lambda c: at(3, k, count, c), c) - xy) + (yy - at(1, k, count, c, -1))
            values.append(total + (at(5, k, count, c, 0, 1) - yz))
            total = (ahead(lambda c: at(4, k, count, c), c) - xz) + (at(5, k, count, c, 1) - yz)
            values.append(total + (zz - at(2, k, count, c, 0, -1)))
            for f in range(3):
                value = look(v_ext, base + f, k, count, c) + scaled * values[f]
                acc[f, pl.ds(k - 1, count), :, lanes(c)] = value.reshape(count, side, LANES)

        blocks(run)

    def pier_part(c):
        high, low = halves(acc[2, :, :, lanes(c)].reshape(depth * side, LANES))
        term = jnp.dot(jnp.concatenate([high, low], axis=1), cols_t[c], preferred_element_type=f32)
        part[...] = term if c == 0 else part[...] + term

    def shears(step, c, with_ghosts, which=(3, 4, 5)):
        at = functools.partial(look, v_ext)
        x, y, z = (3 * step + f for f in range(3))

        def run(k, count, which=which):
            lame, shear, relax = moduli(k, count)
            for f in which:
                if f == 3:
                    strain = (at(x, k, count, c) - at(x, k, count, c, -1)) + (
                        at(y, k, count, c) - behind(lambda c: at(y, k, count, c), c)
                    )
                elif f == 4:
                    strain = (at(x, k, count, c) - at(x, k, count, c, 0, -1)) + (
                        at(z, k, count, c) - behind(lambda c: at(z, k, count, c), c)
                    )
                else:
                    strain = (at(y, k, count, c) - at(y, k, count, c, 0, -1)) + (
                        at(z, k, count, c) - at(z, k, count, c, -1)
                    )
                put(s_ext, f, k, count, c, relax * look(s_ext, f, k, count, c) + shear * strain)

        blocks(run)
        if with_ghosts:
            run(depth + 1, 1, (4, 5))
            shear, relax = (coef[i, pl.ds(1, depth), 0, :] for i in (1, 2))
            y_at = functools.partial(row, v_ext, y, at=below)
            strain = (row(v_ext, x, c, below) - row(v_ext, x, c, below - 1)) + (
                y_at(c) - behind(lambda c: y_at(c), c)
            )
            xy = relax * row(s_ext, 3, c, below) + shear * strain
            strain = (y_at(c) - y_at(c, dz=-1)) + (row(v_ext, z, c, below) - row(v_ext, z, c, below - 1))
            yz = relax * row(s_ext, 5, c, below) + shear * strain
            s_ext[3, pl.ds(1, depth), below, lanes(c)] = jnp.where(g == ng - 1, 0.0, xy)
            s_ext[5, pl.ds(1, depth), below, lanes(c)] = jnp.where(g == ng - 1, 0.0, yz)

    def normals(step, c, with_ghosts):
        at = functools.partial(look, v_ext)
        x, y, z = (3 * step + f for f in range(3))

        def run(k, count, which=(0, 1, 2)):
            lame, shear, relax = moduli(k, count)
            ex = ahead(lambda c: at(x, k, count, c), c) - at(x, k, count, c)
            ey = at(y, k, count, c, 1) - at(y, k, count, c)
            ez = at(z, k, count, c, 0, 1) - at(z, k, count, c)
            trace = lame * ((ex + ey) + ez)
            twice = shear + shear
            for f in which:
                value = relax * look(s_ext, f, k, count, c) + (twice * (ex, ey, ez)[f] + trace)
                put(s_ext, f, k, count, c, value)

        blocks(run)
        if with_ghosts:
            run(0, 1, (2,))
            lame, shear, relax = (coef[i, pl.ds(1, depth), 0, :] for i in range(3))
            x_at = functools.partial(row, v_ext, x, at=above)
            ex = ahead(lambda c: x_at(c), c) - x_at(c)
            ey = row(v_ext, y, c, ROWS) - row(v_ext, y, c, above)
            ez = row(v_ext, z, c, above, 1) - row(v_ext, z, c, above)
            yy = relax * row(s_ext, 1, c, above) + ((shear + shear) * ey + lame * ((ex + ey) + ez))
            s_ext[1, pl.ds(1, depth), above, lanes(c)] = jnp.where(g == 0, 0.0, yy)

    def mine(t):
        return pl.ds(t * share_rows, share_rows)

    def there(step, c, d):
        t = lax.rem(me + d, n)
        src = acc.at[:, :, mine(t), lanes(c)]
        dst = pin.at[:, pl.ds(me * depth, depth), mine(c), :]
        if d == 0:
            return pltpu.make_async_copy(src, dst, f_recv.at[c])
        return pltpu.make_async_remote_copy(
            src_ref=src, dst_ref=dst, send_sem=f_send.at[c],
            recv_sem=f_recv.at[c], device_id=(t, g), device_id_type=MESH,
        )

    def back(step, c, d):
        t = lax.rem(me + d, n)
        pieces = ((0, 3, 0, depth + 2),)
        if step == STEPS - 1:
            pieces = ((0, 2, 0, depth + 1), (2, 1, 1, depth + 1))
        copies = []
        for f, fields, low, count in pieces:
            src = pout.at[pl.ds(f, fields), pl.ds(t * depth + low, count), mine(c), :]
            dst = v_ext.at[
                pl.ds(3 * step + f, fields), pl.ds(low, count), pl.ds(ROWS + me * share_rows, share_rows), lanes(c)
            ]
            if d == 0:
                copies.append(pltpu.make_async_copy(src, dst, r_recv.at[c]))
            else:
                copies.append(pltpu.make_async_remote_copy(
                    src_ref=src, dst_ref=dst, send_sem=r_send.at[c],
                    recv_sem=r_recv.at[c], device_id=(t, g), device_id_type=MESH,
                ))
        return copies

    def count_back(step):
        return depth + (1 if step == STEPS - 1 else 2)

    def start_there(step, c):
        for d in list(range(1, n)) + [0]:
            there(step, c, d).start()

    def start_back(step, c):
        for d in list(range(1, n)) + [0]:
            for copy in back(step, c, d):
                copy.start()

    def sent_there(step, c):
        settle(pin.at[:, pl.ds(0, (n - 1) * depth), mine(c), :], f_send.at[c])

    def got_there(step, c):
        settle(pin.at[:, :, mine(c), :], f_recv.at[c])

    def sent_back(step, c):
        settle(pout.at[:, pl.ds(0, (n - 1) * count_back(step)), mine(c), :], r_send.at[c])

    def got_back(step, c):
        settle(
            v_ext.at[pl.ds(3 * step, 3), pl.ds(0, count_back(step)), inner, lanes(c)], r_recv.at[c]
        )

    def damp(step, c):
        got_there(step, c)
        if step > 0:
            sent_back(step - 1, c)
        for f in range(3):
            terms = []
            for r in range(share_rows):
                high, low = halves(pin[f, :, share_rows * c + r, :])
                terms.append(jnp.concatenate([high, low, high], axis=0))
            damped = jnp.dot(damp_cat[...], jnp.concatenate(terms, axis=1), preferred_element_type=f32)
            for r in range(share_rows):
                pout[f, pl.ds(1, n * depth), share_rows * c + r, :] = damped[:, r * LANES : (r + 1) * LANES]
        start_back(step, c)

    def shared(step):
        return pl.ds(0, stage_rows if step == 0 else depth)

    def share(step, d):
        return pltpu.make_async_remote_copy(
            src_ref=um.at[step, 0, shared(step)], dst_ref=um.at[step, d, shared(step)],
            send_sem=u_send.at[step], recv_sem=u_recv.at[step],
            device_id=(me, lax.rem(g + d, ng)), device_id_type=MESH,
        )

    def forces(step, d):
        block = pl.ds(pl.multiple_of(me * depth, depth), depth)
        return pltpu.make_async_remote_copy(
            src_ref=fall.at[step, block], dst_ref=fall.at[step, block],
            send_sem=p_send.at[step], recv_sem=p_recv.at[step],
            device_id=(lax.rem(me + d, n), g), device_id_type=MESH,
        )

    def pier_means(step):
        masked = part[...].reshape(depth, side, LANES) * rows_of[...][None]
        um[step, 0, pl.ds(0, depth), :] = jnp.sum(masked, axis=1)
        if step == 0:
            um[step, 0, pl.ds(depth, depth), :] = wbuf[...]
            um[step, 0, pl.ds(2 * depth, ROWS), :] = own_impedance()
        for d in range(1, ng):
            share(step, d).start()

    def pier_forces(step):
        settle(um.at[step, pl.ds(1, ng - 1), shared(step)], u_recv.at[step])
        settle(um.at[step, pl.ds(1, ng - 1), shared(step)], u_send.at[step])
        every = um[step, 0, shared(step), :]
        for d in range(1, ng):
            every = every + um[step, d, shared(step), :]
        if step == 0:
            wbuf[...] = every[depth : 2 * depth]
            gain[...] = every[2 * depth :]
        w = wbuf[...]
        force = gain[0:1, :] * (w - every[0:depth] / FOOT)
        wbuf[...] = w - pier_gain * force
        fall[step, pl.ds(pl.multiple_of(me * depth, depth), depth), :] = soil_gain * force
        for d in range(1, n):
            forces(step, d).start()

    def pier_spread(step):
        settle(fall.at[step, pl.ds(0, (n - 1) * depth)], p_recv.at[step])
        settle(fall.at[step, pl.ds(0, (n - 1) * depth)], p_send.at[step])
        pushed = jnp.dot(
            damp_own[...], fall[step], precision=lax.Precision.HIGHEST, preferred_element_type=f32
        )[0 : depth + 2]
        wide = (pushed[:, None, :] * rows_of[...][None]).reshape((depth + 2) * side, LANES)
        spread[...] = jnp.concatenate(halves(wide), axis=1)

    def y_speed(step, c, i):
        low, count = (0, depth + 2) if step < STEPS - 1 else (1, depth)
        fields, planes = pl.ds(3 * step, 3), pl.ds(low, count)
        if step == STEPS - 1 and i == 1:
            fields = pl.ds(3 * step + 1, 1)
        return pltpu.make_async_remote_copy(
            src_ref=v_ext.at[fields, planes, pl.ds(below - 1 if i == 0 else ROWS, 1), lanes(c)],
            dst_ref=v_ext.at[fields, planes, pl.ds(above if i == 0 else below, 1), lanes(c)],
            send_sem=y_send.at[c, i], recv_sem=y_recv.at[c, i],
            device_id=(me, g + 1 - 2 * i), device_id_type=MESH,
        )

    has_next, has_last = g < ng - 1, g > 0

    def arrive(step, c):
        got_back(step, c)
        low, count = (0, depth + 2) if step < STEPS - 1 else (1, depth + 1)
        term = jnp.dot(
            spread[pl.ds(low * side, count * side), :], cols_of[:, lanes(c)], preferred_element_type=f32
        )
        put(v_ext, 3 * step + 2, low, count, c, look(v_ext, 3 * step + 2, low, count, c) + term)

        @pl.when(has_next)
        def _():
            y_speed(step, c, 0).start()

        @pl.when(has_last)
        def _():
            y_speed(step, c, 1).start()

    def edges(step, c):
        @pl.when(has_last)
        def _():
            y_speed(step, c, 0).wait_recv()
            y_speed(step, c, 1).wait_send()

        @pl.when(has_next)
        def _():
            y_speed(step, c, 1).wait_recv()
            y_speed(step, c, 0).wait_send()

    def load(c):
        for copy in loads[c]:
            copy.wait()

    last = tiles - 1

    def first_speeds(c):
        if 0 < c < last:
            load(c + 1)
        speeds(0, c)

    def next_speeds(step, c):
        sent_there(step - 1, c)
        speeds(step, c)
        if c == last:
            pier_part(c)
            pier_means(step)
        start_there(step, c)
        if c < last:
            pier_part(c)

    exchange(ghosts)
    for copy in smalls:
        copy.wait()
    load(0)
    load(1)
    early_speeds()
    early_there()
    clear_stress()
    finish(ghosts)
    first_speeds(0)
    late_there()
    first_speeds(1)
    start_there(0, 1)
    set_piers()
    for c in range(2, tiles):
        first_speeds(c)
    for c in range(tiles):
        pier_part(c)
    pier_means(0)
    set_layers()
    set_damping()
    clear_speeds()

    def next_stress(c):
        normals(0, c, True)
        next_speeds(1, c)

    def bend(step, c):
        edges(step, c)
        shears(step, c, step < STEPS - 1)

    pier_forces(0)
    damp(0, 0)
    start_there(0, 2)
    damp(0, 1)
    start_there(0, 3)
    pier_spread(0)
    damp(0, 2)
    damp(0, 3)
    finish(layers)
    arrive(0, 0)
    arrive(0, 1)
    bend(0, 0)
    arrive(0, 2)
    bend(0, 1)
    next_stress(0)
    arrive(0, 3)
    bend(0, 2)
    next_stress(1)
    bend(0, 3)
    next_stress(2)
    next_stress(3)
    damp(1, 0)
    pier_forces(1)
    damp(1, 1)
    damp(1, 2)
    pier_spread(1)
    damp(1, 3)
    arrive(1, 0)
    arrive(1, 1)
    bend(1, 0)
    arrive(1, 2)
    bend(1, 1)
    normals(1, 0, False)
    arrive(1, 3)
    bend(1, 2)
    normals(1, 1, False)
    normals(1, 2, False)
    bend(1, 3)
    normals(1, 3, False)

    square[...] = jnp.zeros((LANES, LANES), f32)
    square[pl.ds(0, depth), :] = pltpu.roll(wbuf[...], lax.rem(LANES - g * own, LANES), 1)
    w_out[...] = jnp.transpose(square[...])[0:own, 0:depth]
    for c in range(tiles):
        sent_there(STEPS - 1, c)
        sent_back(STEPS - 1, c)


def deliver(v_ref, s_ref, w_ref, v_out, s_out, w_out, sem):
    depth, side = v_out.shape[1:3]
    inside = pl.ds(1, depth), pl.ds(ROWS, side)
    pairs = (
        (s_ref.at[(pl.ds(0, 6),) + inside], s_out),
        (v_ref.at[(pl.ds(3 * (STEPS - 1), 3),) + inside], v_out),
        (w_ref, w_out),
    )
    copies = [pltpu.make_async_copy(a, b, sem.at[i]) for i, (a, b) in enumerate(pairs)]
    for copy in copies:
        copy.start()
    for copy in copies:
        copy.wait()


def fused_body(
    n, ng, velocity, stress, pier_velocity, buoyancy, layer, lame_table, shear_table, relax_table,
    impedance, footprint, damp_inverse,
):
    depth, side, line = buoyancy.shape
    own = pier_velocity.shape[1]
    f32 = jnp.float32
    hbm = pl.BlockSpec(memory_space=pltpu.HBM)
    vmem = pl.BlockSpec(memory_space=pltpu.VMEM)
    dma = pltpu.SemaphoreType.DMA
    tall = side + 2 * ROWS
    stage = 2 * depth + ROWS
    tiles = line // LANES
    v, s, w = pl.pallas_call(
        functools.partial(fused, n, ng),
        out_shape=(
            pltpu.VMEM((3 * STEPS, depth + 2, tall, line), f32),
            pltpu.VMEM((6, depth + 2, tall, line), f32),
            pltpu.VMEM((own, depth), f32),
        ),
        in_specs=[hbm] * 11,
        out_specs=(vmem, vmem, vmem),
        scratch_shapes=[
            pltpu.SMEM(layer.shape, layer.dtype),
            pltpu.SMEM(lame_table.shape, f32),
            pltpu.SMEM(shear_table.shape, f32),
            pltpu.SMEM(relax_table.shape, f32),
            pltpu.SMEM(footprint.shape, footprint.dtype),
            pltpu.VMEM((own, depth), f32),
            pltpu.SMEM(impedance.shape, f32),
            pltpu.VMEM(damp_inverse.shape, f32),
            dma((8,)),
            pltpu.VMEM((depth, side, line), f32),
            pltpu.VMEM((3, depth + 2, side, LANES), f32),
            pltpu.VMEM((3, depth, side, line), f32),
            pltpu.VMEM((3, depth, side, LANES), f32),
            pltpu.VMEM((3, n * depth, ROWS, LANES), f32),
            pltpu.VMEM((3, n * depth + 2, ROWS, LANES), f32),
            pltpu.VMEM((STEPS, ng, stage, LANES), f32),
            pltpu.VMEM((STEPS, n * depth, LANES), f32),
            pltpu.VMEM((depth, LANES), f32),
            pltpu.VMEM((ROWS, LANES), f32),
            pltpu.VMEM((LANES, LANES), f32),
            pltpu.VMEM((depth * side, LANES), f32),
            pltpu.VMEM((side, LANES), f32),
            pltpu.VMEM((tiles, 2 * LANES, LANES), jnp.bfloat16),
            pltpu.VMEM((2 * LANES, line), jnp.bfloat16),
            pltpu.VMEM(((depth + 2) * side, 2 * LANES), jnp.bfloat16),
            pltpu.VMEM((n * depth, 3 * n * depth), jnp.bfloat16),
            pltpu.VMEM((depth + ROWS, n * depth), f32),
            dma((3 * tiles,)), dma((3,)), dma((3,)), dma((2,)), dma((2,)), dma((3,)), dma((3,)),
            dma((tiles,)), dma((tiles,)), dma((tiles,)), dma((tiles,)),
            dma((STEPS,)), dma((STEPS,)), dma((STEPS,)), dma((STEPS,)),
            dma((tiles, 2)), dma((tiles, 2)),
        ],
        compiler_params=pltpu.CompilerParams(
            collective_id=0, has_side_effects=True, vmem_limit_bytes=48 * 1024 * 1024
        ),
    )(
        velocity, stress, buoyancy, layer, lame_table, shear_table, relax_table,
        footprint, pier_velocity.T, impedance, damp_inverse,
    )
    v, s, w = pl.pallas_call(
        deliver,
        out_shape=tuple(
            jax.ShapeDtypeStruct(a, f32) for a in (velocity.shape, stress.shape, (own, depth))
        ),
        in_specs=[vmem] * 3,
        out_specs=(hbm,) * 3,
        scratch_shapes=[dma((3,))],
        compiler_params=pltpu.CompilerParams(vmem_limit_bytes=8 * 1024 * 1024),
    )(v, s, w)
    return v, s, w.T


def whole_tiles(mesh, velocity, pier_velocity):
    n, ng = mesh.shape["gx"], mesh.shape["gy"]
    depth, side, line = velocity.shape[1] // n, velocity.shape[2] // ng, velocity.shape[3]
    return (
        line % LANES == 0
        and side % 16 == 0
        and side % n == 0
        and depth % ROWS == 0
        and (side // n) * (line // LANES) == ROWS
        and n * depth % LANES == 0
        and pier_velocity.shape[1] <= LANES
    )


def solution(mesh):
    placed = (
        P(None, "gx", "gy", None),
        P(None, "gx", "gy", None),
        P("gx", "gy"),
        P("gx", "gy", None),
        P("gx"),
        P(),
        P(),
        P(),
        P("gy"),
        P(),
        P(),
    )

    def run(*args):
        n, ng = mesh.shape["gx"], mesh.shape["gy"]
        if whole_tiles(mesh, args[0], args[2]):
            part = functools.partial(fused_body, n, ng)
        else:
            part = body
        return mapped(part)(*args)

    def mapped(part):
        return jax.shard_map(
            part,
            mesh=mesh,
            in_specs=placed,
            out_specs=(P(None, "gx", "gy", None), P(None, "gx", "gy", None), P("gx", "gy")),
            check_vma=False,
        )

    return run
```

```python
import functools
import jax
import jax.numpy as jnp
from jax import lax
from jax.experimental import pallas as pl
from jax.experimental.pallas import tpu as pltpu
from jax.sharding import PartitionSpec as P

STEPS = 2
FOOT = 16


grid_ratio = 0.25
soil_gain = 0.2
pier_gain = 0.5


def extended(cells, sides, width):
    for axis, dim in sides:
        count = lax.axis_size(axis)
        ends = count - 1
        head = lax.slice_in_dim(cells, 0, width, axis=dim)
        tail = lax.slice_in_dim(cells, cells.shape[dim] - width, cells.shape[dim], axis=dim)
        cells = jnp.concatenate(
            [
                lax.ppermute(tail, axis, [(i, (i + 1) % count) for i in range(ends)]),
                cells,
                lax.ppermute(head, axis, [((i + 1) % count, i) for i in range(ends)]),
            ],
            axis=dim,
        )
    return cells


def forward_diff(padded, along):
    center = padded[1:-1, 1:-1, 1:-1]
    if along == 0:
        return padded[2:, 1:-1, 1:-1] - center
    if along == 1:
        return padded[1:-1, 2:, 1:-1] - center
    return padded[1:-1, 1:-1, 2:] - center


def backward_diff(padded, along):
    center = padded[1:-1, 1:-1, 1:-1]
    if along == 0:
        return center - padded[:-2, 1:-1, 1:-1]
    if along == 1:
        return center - padded[1:-1, :-2, 1:-1]
    return center - padded[1:-1, 1:-1, :-2]


def move_velocity(velocity, padded, buoyancy):
    scaled = grid_ratio * buoyancy
    first = velocity[0] + scaled * (
        backward_diff(padded[0], 2) + forward_diff(padded[3], 1) + forward_diff(padded[4], 0)
    )
    second = velocity[1] + scaled * (
        forward_diff(padded[3], 2) + backward_diff(padded[1], 1) + forward_diff(padded[5], 0)
    )
    third = velocity[2] + scaled * (
        forward_diff(padded[4], 2) + forward_diff(padded[5], 1) + backward_diff(padded[2], 0)
    )
    return jnp.stack([first, second, third])


def move_stress(stress, padded, lame_first, shear_mod, relax):
    strain_x = forward_diff(padded[0], 2)
    strain_y = forward_diff(padded[1], 1)
    strain_z = forward_diff(padded[2], 0)
    modulus = lame_first + 2.0 * shear_mod
    normal_x = relax * stress[0] + grid_ratio * (
        modulus * strain_x + lame_first * (strain_y + strain_z)
    )
    normal_y = relax * stress[1] + grid_ratio * (
        modulus * strain_y + lame_first * (strain_x + strain_z)
    )
    normal_z = relax * stress[2] + grid_ratio * (
        modulus * strain_z + lame_first * (strain_x + strain_y)
    )
    shear_xy = relax * stress[3] + grid_ratio * shear_mod * (
        backward_diff(padded[0], 1) + backward_diff(padded[1], 2)
    )
    shear_xz = relax * stress[4] + grid_ratio * shear_mod * (
        backward_diff(padded[0], 0) + backward_diff(padded[2], 2)
    )
    shear_yz = relax * stress[5] + grid_ratio * shear_mod * (
        backward_diff(padded[1], 0) + backward_diff(padded[2], 1)
    )
    return jnp.stack([normal_x, normal_y, normal_z, shear_xy, shear_xz, shear_yz])


def layer_values(layer, table):
    levels = jnp.arange(table.shape[0], dtype=jnp.int32)
    onehot = (layer[:, None] == levels[None, :]).astype(table.dtype)
    return jnp.sum(onehot * table[None, :], axis=1)[:, None, None]


def with_faces(fields):
    padded = extended(fields, (("gx", 1), ("gy", 2)), 1)
    return jnp.pad(padded, ((0, 0), (0, 0), (0, 0), (1, 1)))


def footprint_matches(cell_ids, footprint):
    piers = footprint.shape[0]
    equal = (cell_ids[:, None] == footprint.reshape(-1)[None, :]).astype(jnp.float32)
    return jnp.sum(equal.reshape(cell_ids.shape[0], piers, FOOT), axis=2)


def damp_columns(velocity, inverse):
    pencils = lax.all_to_all(velocity, "gx", split_axis=3, concat_axis=1, tiled=True)
    shape = pencils.shape
    flat = pencils.reshape(shape[0], shape[1], shape[2] * shape[3])
    damped = jnp.einsum("zk,fkm->fzm", inverse, flat, precision=lax.Precision.HIGHEST).reshape(
        shape
    )
    return lax.all_to_all(damped, "gx", split_axis=1, concat_axis=3, tiled=True)


def body(
    velocity,
    stress,
    pier_velocity,
    buoyancy,
    layer,
    lame_table,
    shear_table,
    relax_table,
    impedance,
    footprint,
    damp_inverse,
):
    depth_cells, side_cells, line_cells = (velocity.shape[1], velocity.shape[2], velocity.shape[3])
    own_piers = pier_velocity.shape[1]
    lame_first = layer_values(layer, lame_table)
    shear_mod = layer_values(layer, shear_table)
    relax = layer_values(layer, relax_table)
    row_start = lax.axis_index("gy") * side_cells
    cell_ids = row_start * line_cells + jnp.arange(side_cells * line_cells, dtype=jnp.int32)
    selector = footprint_matches(cell_ids, footprint)
    own_foot = lax.dynamic_slice_in_dim(footprint, lax.axis_index("gy") * own_piers, own_piers, 0)
    for time_step in range(STEPS):
        padded = with_faces(stress)
        velocity = move_velocity(velocity, padded, buoyancy)
        vertical = velocity[2].reshape(depth_cells, side_cells * line_cells)
        piece = lax.all_gather(velocity[2], "gy", axis=1, tiled=True)
        count = piece.shape[1]
        piece_ids = jnp.arange(count * line_cells, dtype=jnp.int32)
        picks = footprint_matches(piece_ids, own_foot)
        flat = piece.reshape(depth_cells, count * line_cells)
        summed = jnp.dot(
            flat, picks, precision=lax.Precision.HIGHEST, preferred_element_type=jnp.float32
        )
        mean_speed = summed / FOOT
        force = impedance[None, :] * (pier_velocity - mean_speed)
        pier_velocity = pier_velocity - pier_gain * force
        all_force = lax.all_gather(force, "gy", axis=1, tiled=True)
        pushed = jnp.dot(
            all_force,
            selector.T,
            precision=lax.Precision.HIGHEST,
            preferred_element_type=jnp.float32,
        )
        vertical = vertical + soil_gain * pushed
        velocity = jnp.stack(
            [velocity[0], velocity[1], vertical.reshape(depth_cells, side_cells, line_cells)]
        )
        velocity = damp_columns(velocity, damp_inverse)
        padded = with_faces(velocity)
        stress = move_stress(stress, padded, lame_first, shear_mod, relax)
    return (velocity, stress, pier_velocity)


SIDE = 4
LANES = 128
ROWS = 8
BLOCK = 4
MESH = pl.DeviceIdType.MESH
Z_GHOSTS = ((2, -1), (4, 1), (5, 1))
Y_GHOSTS = ((1, -1), (3, 1), (5, 1))


def fused(
    n, ng, v_hbm, s_hbm, b_hbm, layer_hbm, lame_hbm, shear_hbm, relax_hbm, foot_hbm, w_hbm, imp_hbm, damp_hbm,
    v_ext, s_ext, w_out,
    layer_ref, lame_ref, shear_ref, relax_ref, foot_ref, w_ref, imp_ref, damp_ref, small_sem,
    buoy, coef, acc, ahead_of, pin, pout, um, fall, wbuf, gain, square, part, rows_of, cols_t, cols_of, spread, damp_cat, damp_own,
    load_sem, zs_send, zs_recv, cf_send, cf_recv, ys_send, ys_recv,
    f_send, f_recv, r_send, r_recv, u_send, u_recv, p_send, p_recv, y_send, y_recv,
):
    me = lax.axis_index("gx")
    g = lax.axis_index("gy")
    depth, side, line = buoy.shape
    tiles = line // LANES
    share_rows = side // n
    inner = pl.ds(ROWS, side)
    own = w_ref.shape[0]
    stage_rows = um.shape[2]
    f32, bf16 = jnp.float32, jnp.bfloat16
    above, below = ROWS - 1, ROWS + side

    def lanes(c):
        return pl.ds(c * LANES, LANES)

    def settle(ref, sem):
        pltpu.make_async_copy(ref, ref, sem).wait()

    loads = []
    for c in range(tiles):
        loads.append((
            pltpu.make_async_copy(
                s_hbm.at[:, :, :, lanes(c)], s_ext.at[:, pl.ds(1, depth), inner, lanes(c)], load_sem.at[c]
            ),
            pltpu.make_async_copy(b_hbm.at[:, :, lanes(c)], buoy.at[:, :, lanes(c)], load_sem.at[tiles + c]),
            pltpu.make_async_copy(
                v_hbm.at[:, :, :, lanes(c)], v_ext.at[pl.ds(0, 3), pl.ds(1, depth), inner, lanes(c)],
                load_sem.at[2 * tiles + c],
            ),
        ))
        for copy in loads[c]:
            copy.start()

    smalls = [
        pltpu.make_async_copy(src, dst, small_sem.at[i])
        for i, (src, dst) in enumerate((
            (layer_hbm, layer_ref), (lame_hbm, lame_ref), (shear_hbm, shear_ref), (relax_hbm, relax_ref),
            (foot_hbm, foot_ref), (w_hbm, w_ref), (imp_hbm, imp_ref), (damp_hbm, damp_ref),
        ))
    ]
    for copy in smalls:
        copy.start()
    barrier = pltpu.get_barrier_semaphore()
    for d in range(1, n):
        pl.semaphore_signal(
            barrier, inc=1, device_id=(lax.rem(me + d, n), g), device_id_type=MESH
        )
    for d in range(1, ng):
        pl.semaphore_signal(
            barrier, inc=1, device_id=(me, lax.rem(g + d, ng)), device_id_type=MESH
        )
    pl.semaphore_wait(barrier, n - 1 + ng - 1)

    def z_copy(i):
        f, way = Z_GHOSTS[i]
        return pltpu.make_async_remote_copy(
            src_ref=s_hbm.at[f, depth - 1 if way < 0 else 0],
            dst_ref=s_ext.at[f, 0 if way < 0 else depth + 1, inner, :],
            send_sem=zs_send.at[i], recv_sem=zs_recv.at[i],
            device_id=(me - way, g), device_id_type=MESH,
        )

    def c_copy(way):
        i = (way + 1) // 2
        return pltpu.make_async_remote_copy(
            src_ref=coef.at[:, depth if way < 0 else 1],
            dst_ref=coef.at[:, 0 if way < 0 else depth + 1],
            send_sem=cf_send.at[i], recv_sem=cf_recv.at[i],
            device_id=(me - way, g), device_id_type=MESH,
        )

    def y_stress(i):
        f, way = Y_GHOSTS[i]
        return pltpu.make_async_remote_copy(
            src_ref=s_hbm.at[f, :, pl.ds(side - 1 if way < 0 else 0, 1), :],
            dst_ref=s_ext.at[f, pl.ds(1, depth), pl.ds(above if way < 0 else below, 1), :],
            send_sem=ys_send.at[i], recv_sem=ys_recv.at[i],
            device_id=(me, g - way), device_id_type=MESH,
        )

    not_ends = {
        -1: (me > 0, me < n - 1, g > 0, g < ng - 1),
        1: (me < n - 1, me > 0, g < ng - 1, g > 0),
    }
    ghosts = [(z_copy, i, not_ends[way][0:2]) for i, (f, way) in enumerate(Z_GHOSTS)]
    ghosts += [(y_stress, i, not_ends[way][2:4]) for i, (f, way) in enumerate(Y_GHOSTS)]
    layers = [(c_copy, way, not_ends[way][0:2]) for way in (-1, 1)]
    def clear_stress():
        edge = jnp.zeros((depth + 2, line), f32)

        @pl.when(me == 0)
        def _():
            for f, way in Z_GHOSTS:
                if way < 0:
                    s_ext[f, 0, inner, :] = jnp.zeros((side, line), f32)

        @pl.when(me == n - 1)
        def _():
            for f, way in Z_GHOSTS:
                if way > 0:
                    s_ext[f, depth + 1, inner, :] = jnp.zeros((side, line), f32)

        @pl.when(g == 0)
        def _():
            for f, way in Y_GHOSTS:
                if way < 0:
                    s_ext[f, :, above, :] = edge

        @pl.when(g == ng - 1)
        def _():
            for f, way in Y_GHOSTS:
                if way > 0:
                    s_ext[f, :, below, :] = edge

    def clear_speeds():
        edge = jnp.zeros((depth + 2, line), f32)

        @pl.when(g == 0)
        def _():
            for f in range(3 * STEPS):
                v_ext[f, :, above, :] = edge

        @pl.when(g == ng - 1)
        def _():
            for f in range(3 * STEPS):
                v_ext[f, :, below, :] = edge
        for f in range(3):
            pout[f, 0] = jnp.zeros((ROWS, LANES), f32)
            pout[f, n * depth + 1] = jnp.zeros((ROWS, LANES), f32)

    def set_layers():
        for k in range(depth):
            for c, (table, scale) in enumerate(((lame_ref, grid_ratio), (shear_ref, grid_ratio), (relax_ref, 1.0))):
                coef[c, k + 1] = jnp.full((side, LANES), scale * table[layer_ref[k]], f32)
        for end, k in ((0, 0), (n - 1, depth + 1)):
            @pl.when(me == end)
            def _(k=k):
                for c in range(3):
                    coef[c, k] = jnp.zeros((side, LANES), f32)
        exchange(layers)

    def exchange(copies):
        for make, i, (gets, sends) in copies:
            @pl.when(sends)
            def _(make=make, i=i):
                make(i).start()

    def finish(copies):
        for make, i, (gets, sends) in copies:
            @pl.when(gets)
            def _(make=make, i=i):
                make(i).wait_recv()

            @pl.when(sends)
            def _(make=make, i=i):
                make(i).wait_send()

    def set_piers():
        ids = lax.broadcasted_iota(jnp.int32, (side, LANES), 0) + g * side
        lane_id = lax.broadcasted_iota(jnp.int32, (2 * LANES, LANES), 1)
        row_id = lax.broadcasted_iota(jnp.int32, (2 * LANES, LANES), 0) & (LANES - 1)
        first = jnp.full((1, LANES), -64, jnp.int32)
        begin_lane = jnp.full((1, LANES), -64, jnp.int32)
        begin_row = jnp.full((2 * LANES, LANES), -64, jnp.int32)
        for p in range(foot_ref.shape[0]):
            first = jnp.where(lane_id[0:1] == p, foot_ref[p, 0] // line, first)
            begin_lane = jnp.where(lane_id[0:1] == p, foot_ref[p, 0] % line, begin_lane)
            begin_row = jnp.where(row_id == p, foot_ref[p, 0] % line, begin_row)
        rows_of[...] = jnp.where((ids >= first) & (ids < first + SIDE), 1.0, 0.0)
        for c in range(tiles):
            at = row_id + c * LANES
            cols_t[c] = jnp.where((at >= begin_lane) & (at < begin_lane + SIDE), 1.0, 0.0).astype(bf16)
            at = lane_id + c * LANES
            cols_of[:, lanes(c)] = jnp.where((at >= begin_row) & (at < begin_row + SIDE), 1.0, 0.0).astype(bf16)
        square[...] = jnp.zeros((LANES, LANES), f32)
        square[pl.ds(0, own), pl.ds(0, depth)] = w_ref[...]
        wbuf[...] = pltpu.roll(jnp.transpose(square[...])[0:depth], g * own, 1)

    def halves(a):
        high = a.astype(bf16)
        return high, (a - high.astype(f32)).astype(bf16)

    def set_damping():
        high, low = halves(damp_ref[...])
        damp_cat[...] = jnp.concatenate([high, high, low], axis=1)
        damp_own[...] = jnp.zeros_like(damp_own)
        damp_own[pl.ds(1, depth), :] = damp_ref[pl.ds(pl.multiple_of(me * depth, depth), depth), :]

        @pl.when(me > 0)
        def _():
            damp_own[pl.ds(0, 1), :] = damp_ref[pl.ds(me * depth - 1, 1), :]

        @pl.when(me < n - 1)
        def _():
            damp_own[pl.ds(depth + 1, 1), :] = damp_ref[pl.ds((me + 1) * depth, 1), :]

    def own_impedance():
        impedance = jnp.zeros((ROWS, LANES), f32)
        for i in range(imp_ref.shape[0]):
            impedance = jnp.where(lax.broadcasted_iota(jnp.int32, (ROWS, LANES), 1) == g * own + i, imp_ref[i], impedance)
        return impedance

    def look(ref, f, k, count, c, dy=0, dz=0):
        return ref[f, pl.ds(k + dz, count), pl.ds(ROWS + dy, side), lanes(c)].reshape(count * side, LANES)

    def row(ref, f, c, at, dz=0):
        return ref[f, pl.ds(1 + dz, depth), at, lanes(c)]

    def ahead(get, c):
        cell = get(c)
        lane = lax.broadcasted_iota(jnp.int32, cell.shape, 1)
        other = 0.0 if c == tiles - 1 else pltpu.roll(get(c + 1), LANES - 1, 1)
        return jnp.where(lane == LANES - 1, other, pltpu.roll(cell, LANES - 1, 1))

    def behind(get, c):
        cell = get(c)
        lane = lax.broadcasted_iota(jnp.int32, cell.shape, 1)
        other = 0.0 if c == 0 else pltpu.roll(get(c - 1), 1, 1)
        return jnp.where(lane == 0, other, pltpu.roll(cell, 1, 1))

    def blocks(run, size=BLOCK):
        def at(i, carry):
            run(1 + i * size, size)
            return carry

        lax.fori_loop(0, depth // size, at, 0)

    def moduli(k, count):
        return [coef[c, pl.ds(k, count)].reshape(count * side, LANES) for c in range(3)]

    def put(ref, f, k, count, c, value):
        ref[f, pl.ds(k, count), inner, lanes(c)] = value.reshape(count, side, LANES)

    def early_speeds():
        def run(i, carry):
            k, count = 2 + 2 * i, 2
            at = functools.partial(look, s_ext)
            size = count * side
            scaled = grid_ratio * buoy[pl.ds(k - 1, count), :, lanes(0)].reshape(size, LANES)
            xx, yy, zz, xy, xz, yz = (at(f, k, count, 0) for f in range(6))
            total = (xx - behind(lambda c: at(0, k, count, c), 0)) + (pltpu.roll(xy, size - 1, 0) - xy)
            total = total + (at(4, k, count, 0, 0, 1) - xz)
            values = [total]
            total = (ahead(lambda c: at(3, k, count, c), 0) - xy) + (yy - pltpu.roll(yy, 1, 0))
            values.append(total + (at(5, k, count, 0, 0, 1) - yz))
            total = (ahead(lambda c: at(4, k, count, c), 0) - xz) + (pltpu.roll(yz, size - 1, 0) - yz)
            values.append(total + (zz - at(2, k, count, 0, 0, -1)))
            for f in range(3):
                value = look(v_ext, f, k, count, 0) + scaled * values[f]
                ahead_of[f, pl.ds(k - 1, count)] = value.reshape(count, side, LANES)
            return carry

        lax.fori_loop(0, (depth - 2) // 2, run, 0)

    def inner_peer(d):
        t = lax.rem(me + d, n)
        return t, (t > 0) & (t < n - 1)

    def early_copy(d, ref, low, count, at):
        t = lax.rem(me + d, n)
        return pltpu.make_async_remote_copy(
            src_ref=ref.at[:, pl.ds(low, count), mine(t), at],
            dst_ref=pin.at[:, pl.ds(me * depth + low, count), mine(0), :],
            send_sem=f_send.at[0], recv_sem=f_recv.at[0], device_id=(t, g), device_id_type=MESH,
        )

    def early_there():
        for d in range(1, n):
            @pl.when(inner_peer(d)[1])
            def _(d=d):
                early_copy(d, ahead_of, 1, depth - 2, pl.ds(0, LANES)).start()

    def late_there():
        for d in range(1, n):
            @pl.when(inner_peer(d)[1])
            def _(d=d):
                early_copy(d, acc, 0, 1, lanes(0)).start()
                early_copy(d, acc, depth - 1, 1, lanes(0)).start()

            @pl.when(jnp.logical_not(inner_peer(d)[1]))
            def _(d=d):
                there(0, 0, d).start()
        there(0, 0, 0).start()

    def speeds(step, c):
        base = 3 * (step - 1) if step > 0 else 0

        def run(k, count):
            at = functools.partial(look, s_ext)
            scaled = grid_ratio * buoy[pl.ds(k - 1, count), :, lanes(c)].reshape(count * side, LANES)
            xx, yy, zz, xy, xz, yz = (at(f, k, count, c) for f in range(6))
            total = (xx - behind(lambda c: at(0, k, count, c), c)) + (at(3, k, count, c, 1) - xy)
            total = total + (at(4, k, count, c, 0, 1) - xz)
            values = [total]
            total = (ahead(lambda c: at(3, k, count, c), c) - xy) + (yy - at(1, k, count, c, -1))
            values.append(total + (at(5, k, count, c, 0, 1) - yz))
            total = (ahead(lambda c: at(4, k, count, c), c) - xz) + (at(5, k, count, c, 1) - yz)
            values.append(total + (zz - at(2, k, count, c, 0, -1)))
            for f in range(3):
                value = look(v_ext, base + f, k, count, c) + scaled * values[f]
                acc[f, pl.ds(k - 1, count), :, lanes(c)] = value.reshape(count, side, LANES)

        blocks(run)

    def pier_part(c):
        high, low = halves(acc[2, :, :, lanes(c)].reshape(depth * side, LANES))
        term = jnp.dot(jnp.concatenate([high, low], axis=1), cols_t[c], preferred_element_type=f32)
        part[...] = term if c == 0 else part[...] + term

    def shears(step, c, with_ghosts, which=(3, 4, 5)):
        at = functools.partial(look, v_ext)
        x, y, z = (3 * step + f for f in range(3))

        def run(k, count, which=which):
            lame, shear, relax = moduli(k, count)
            for f in which:
                if f == 3:
                    strain = (at(x, k, count, c) - at(x, k, count, c, -1)) + (
                        at(y, k, count, c) - behind(lambda c: at(y, k, count, c), c)
                    )
                elif f == 4:
                    strain = (at(x, k, count, c) - at(x, k, count, c, 0, -1)) + (
                        at(z, k, count, c) - behind(lambda c: at(z, k, count, c), c)
                    )
                else:
                    strain = (at(y, k, count, c) - at(y, k, count, c, 0, -1)) + (
                        at(z, k, count, c) - at(z, k, count, c, -1)
                    )
                put(s_ext, f, k, count, c, relax * look(s_ext, f, k, count, c) + shear * strain)

        blocks(run)
        if with_ghosts:
            run(depth + 1, 1, (4, 5))
            shear, relax = (coef[i, pl.ds(1, depth), 0, :] for i in (1, 2))
            y_at = functools.partial(row, v_ext, y, at=below)
            strain = (row(v_ext, x, c, below) - row(v_ext, x, c, below - 1)) + (
                y_at(c) - behind(lambda c: y_at(c), c)
            )
            xy = relax * row(s_ext, 3, c, below) + shear * strain
            strain = (y_at(c) - y_at(c, dz=-1)) + (row(v_ext, z, c, below) - row(v_ext, z, c, below - 1))
            yz = relax * row(s_ext, 5, c, below) + shear * strain
            s_ext[3, pl.ds(1, depth), below, lanes(c)] = jnp.where(g == ng - 1, 0.0, xy)
            s_ext[5, pl.ds(1, depth), below, lanes(c)] = jnp.where(g == ng - 1, 0.0, yz)

    def normals(step, c, with_ghosts):
        at = functools.partial(look, v_ext)
        x, y, z = (3 * step + f for f in range(3))

        def run(k, count, which=(0, 1, 2)):
            lame, shear, relax = moduli(k, count)
            ex = ahead(lambda c: at(x, k, count, c), c) - at(x, k, count, c)
            ey = at(y, k, count, c, 1) - at(y, k, count, c)
            ez = at(z, k, count, c, 0, 1) - at(z, k, count, c)
            trace = lame * ((ex + ey) + ez)
            twice = shear + shear
            for f in which:
                value = relax * look(s_ext, f, k, count, c) + (twice * (ex, ey, ez)[f] + trace)
                put(s_ext, f, k, count, c, value)

        blocks(run)
        if with_ghosts:
            run(0, 1, (2,))
            lame, shear, relax = (coef[i, pl.ds(1, depth), 0, :] for i in range(3))
            x_at = functools.partial(row, v_ext, x, at=above)
            ex = ahead(lambda c: x_at(c), c) - x_at(c)
            ey = row(v_ext, y, c, ROWS) - row(v_ext, y, c, above)
            ez = row(v_ext, z, c, above, 1) - row(v_ext, z, c, above)
            yy = relax * row(s_ext, 1, c, above) + ((shear + shear) * ey + lame * ((ex + ey) + ez))
            s_ext[1, pl.ds(1, depth), above, lanes(c)] = jnp.where(g == 0, 0.0, yy)

    def mine(t):
        return pl.ds(t * share_rows, share_rows)

    def there(step, c, d):
        t = lax.rem(me + d, n)
        src = acc.at[:, :, mine(t), lanes(c)]
        dst = pin.at[:, pl.ds(me * depth, depth), mine(c), :]
        if d == 0:
            return pltpu.make_async_copy(src, dst, f_recv.at[c])
        return pltpu.make_async_remote_copy(
            src_ref=src, dst_ref=dst, send_sem=f_send.at[c],
            recv_sem=f_recv.at[c], device_id=(t, g), device_id_type=MESH,
        )

    def back(step, c, d):
        t = lax.rem(me + d, n)
        pieces = ((0, 3, 0, depth + 2),)
        if step == STEPS - 1:
            pieces = ((0, 2, 0, depth + 1), (2, 1, 1, depth + 1))
        copies = []
        for f, fields, low, count in pieces:
            src = pout.at[pl.ds(f, fields), pl.ds(t * depth + low, count), mine(c), :]
            dst = v_ext.at[
                pl.ds(3 * step + f, fields), pl.ds(low, count), pl.ds(ROWS + me * share_rows, share_rows), lanes(c)
            ]
            if d == 0:
                copies.append(pltpu.make_async_copy(src, dst, r_recv.at[c]))
            else:
                copies.append(pltpu.make_async_remote_copy(
                    src_ref=src, dst_ref=dst, send_sem=r_send.at[c],
                    recv_sem=r_recv.at[c], device_id=(t, g), device_id_type=MESH,
                ))
        return copies

    def count_back(step):
        return depth + (1 if step == STEPS - 1 else 2)

    def start_there(step, c):
        for d in list(range(1, n)) + [0]:
            there(step, c, d).start()

    def start_back(step, c):
        for d in list(range(1, n)) + [0]:
            for copy in back(step, c, d):
                copy.start()

    def sent_there(step, c):
        settle(pin.at[:, pl.ds(0, (n - 1) * depth), mine(c), :], f_send.at[c])

    def got_there(step, c):
        settle(pin.at[:, :, mine(c), :], f_recv.at[c])

    def sent_back(step, c):
        settle(pout.at[:, pl.ds(0, (n - 1) * count_back(step)), mine(c), :], r_send.at[c])

    def got_back(step, c):
        settle(
            v_ext.at[pl.ds(3 * step, 3), pl.ds(0, count_back(step)), inner, lanes(c)], r_recv.at[c]
        )

    def damp(step, c):
        got_there(step, c)
        if step > 0:
            sent_back(step - 1, c)
        for f in range(3):
            terms = []
            for r in range(share_rows):
                high, low = halves(pin[f, :, share_rows * c + r, :])
                terms.append(jnp.concatenate([high, low, high], axis=0))
            damped = jnp.dot(damp_cat[...], jnp.concatenate(terms, axis=1), preferred_element_type=f32)
            for r in range(share_rows):
                pout[f, pl.ds(1, n * depth), share_rows * c + r, :] = damped[:, r * LANES : (r + 1) * LANES]
        start_back(step, c)

    def shared(step):
        return pl.ds(0, stage_rows if step == 0 else depth)

    def share(step, d):
        return pltpu.make_async_remote_copy(
            src_ref=um.at[step, 0, shared(step)], dst_ref=um.at[step, d, shared(step)],
            send_sem=u_send.at[step], recv_sem=u_recv.at[step],
            device_id=(me, lax.rem(g + d, ng)), device_id_type=MESH,
        )

    def forces(step, d):
        block = pl.ds(pl.multiple_of(me * depth, depth), depth)
        return pltpu.make_async_remote_copy(
            src_ref=fall.at[step, block], dst_ref=fall.at[step, block],
            send_sem=p_send.at[step], recv_sem=p_recv.at[step],
            device_id=(lax.rem(me + d, n), g), device_id_type=MESH,
        )

    def pier_means(step):
        masked = part[...].reshape(depth, side, LANES) * rows_of[...][None]
        um[step, 0, pl.ds(0, depth), :] = jnp.sum(masked, axis=1)
        if step == 0:
            um[step, 0, pl.ds(depth, depth), :] = wbuf[...]
            um[step, 0, pl.ds(2 * depth, ROWS), :] = own_impedance()
        for d in range(1, ng):
            share(step, d).start()

    def pier_forces(step):
        settle(um.at[step, pl.ds(1, ng - 1), shared(step)], u_recv.at[step])
        settle(um.at[step, pl.ds(1, ng - 1), shared(step)], u_send.at[step])
        every = um[step, 0, shared(step), :]
        for d in range(1, ng):
            every = every + um[step, d, shared(step), :]
        if step == 0:
            wbuf[...] = every[depth : 2 * depth]
            gain[...] = every[2 * depth :]
        w = wbuf[...]
        force = gain[0:1, :] * (w - every[0:depth] / FOOT)
        wbuf[...] = w - pier_gain * force
        fall[step, pl.ds(pl.multiple_of(me * depth, depth), depth), :] = soil_gain * force
        for d in range(1, n):
            forces(step, d).start()

    def pier_spread(step):
        settle(fall.at[step, pl.ds(0, (n - 1) * depth)], p_recv.at[step])
        settle(fall.at[step, pl.ds(0, (n - 1) * depth)], p_send.at[step])
        pushed = jnp.dot(
            damp_own[...], fall[step], precision=lax.Precision.HIGHEST, preferred_element_type=f32
        )[0 : depth + 2]
        wide = (pushed[:, None, :] * rows_of[...][None]).reshape((depth + 2) * side, LANES)
        spread[...] = jnp.concatenate(halves(wide), axis=1)

    def y_speed(step, c, i):
        low, count = (0, depth + 2) if step < STEPS - 1 else (1, depth)
        fields, planes = pl.ds(3 * step, 3), pl.ds(low, count)
        if step == STEPS - 1 and i == 1:
            fields = pl.ds(3 * step + 1, 1)
        return pltpu.make_async_remote_copy(
            src_ref=v_ext.at[fields, planes, pl.ds(below - 1 if i == 0 else ROWS, 1), lanes(c)],
            dst_ref=v_ext.at[fields, planes, pl.ds(above if i == 0 else below, 1), lanes(c)],
            send_sem=y_send.at[c, i], recv_sem=y_recv.at[c, i],
            device_id=(me, g + 1 - 2 * i), device_id_type=MESH,
        )

    has_next, has_last = g < ng - 1, g > 0

    def arrive(step, c):
        got_back(step, c)
        low, count = (0, depth + 2) if step < STEPS - 1 else (1, depth + 1)
        term = jnp.dot(
            spread[pl.ds(low * side, count * side), :], cols_of[:, lanes(c)], preferred_element_type=f32
        )
        put(v_ext, 3 * step + 2, low, count, c, look(v_ext, 3 * step + 2, low, count, c) + term)

        @pl.when(has_next)
        def _():
            y_speed(step, c, 0).start()

        @pl.when(has_last)
        def _():
            y_speed(step, c, 1).start()

    def edges(step, c):
        @pl.when(has_last)
        def _():
            y_speed(step, c, 0).wait_recv()
            y_speed(step, c, 1).wait_send()

        @pl.when(has_next)
        def _():
            y_speed(step, c, 1).wait_recv()
            y_speed(step, c, 0).wait_send()

    def load(c):
        for copy in loads[c]:
            copy.wait()

    last = tiles - 1

    def first_speeds(c):
        if 0 < c < last:
            load(c + 1)
        speeds(0, c)

    def next_speeds(step, c):
        sent_there(step - 1, c)
        speeds(step, c)
        if c == last:
            pier_part(c)
            pier_means(step)
        start_there(step, c)
        if c < last:
            pier_part(c)

    exchange(ghosts)
    for copy in smalls:
        copy.wait()
    load(0)
    load(1)
    early_speeds()
    early_there()
    clear_stress()
    finish(ghosts)
    first_speeds(0)
    late_there()
    first_speeds(1)
    start_there(0, 1)
    set_piers()
    for c in range(2, tiles):
        first_speeds(c)
    for c in range(tiles):
        pier_part(c)
    pier_means(0)
    set_layers()
    set_damping()
    clear_speeds()

    def next_stress(c):
        normals(0, c, True)
        next_speeds(1, c)

    def bend(step, c):
        edges(step, c)
        shears(step, c, step < STEPS - 1)

    pier_forces(0)
    damp(0, 0)
    start_there(0, 2)
    damp(0, 1)
    start_there(0, 3)
    pier_spread(0)
    damp(0, 2)
    damp(0, 3)
    finish(layers)
    arrive(0, 0)
    arrive(0, 1)
    bend(0, 0)
    arrive(0, 2)
    bend(0, 1)
    next_stress(0)
    arrive(0, 3)
    bend(0, 2)
    next_stress(1)
    bend(0, 3)
    next_stress(2)
    next_stress(3)
    damp(1, 0)
    pier_forces(1)
    damp(1, 1)
    damp(1, 2)
    pier_spread(1)
    damp(1, 3)
    square[...] = jnp.zeros((LANES, LANES), f32)
    square[pl.ds(0, depth), :] = pltpu.roll(wbuf[...], lax.rem(LANES - g * own, LANES), 1)
    w_out[...] = jnp.transpose(square[...])[0:own, 0:depth]
    for c in range(tiles):
        sent_there(STEPS - 1, c)
    arrive(1, 0)
    arrive(1, 1)
    bend(1, 0)
    arrive(1, 2)
    bend(1, 1)
    normals(1, 0, False)
    arrive(1, 3)
    bend(1, 2)
    normals(1, 1, False)
    normals(1, 2, False)
    bend(1, 3)
    normals(1, 3, False)

    for c in range(tiles):
        sent_back(STEPS - 1, c)


def deliver(v_ref, s_ref, w_ref, v_out, s_out, w_out, sem):
    depth, side = v_out.shape[1:3]
    inside = pl.ds(1, depth), pl.ds(ROWS, side)
    pairs = (
        (s_ref.at[(pl.ds(0, 6),) + inside], s_out),
        (v_ref.at[(pl.ds(3 * (STEPS - 1), 3),) + inside], v_out),
        (w_ref, w_out),
    )
    copies = [pltpu.make_async_copy(a, b, sem.at[i]) for i, (a, b) in enumerate(pairs)]
    for copy in copies:
        copy.start()
    for copy in copies:
        copy.wait()


def fused_body(
    n, ng, velocity, stress, pier_velocity, buoyancy, layer, lame_table, shear_table, relax_table,
    impedance, footprint, damp_inverse,
):
    depth, side, line = buoyancy.shape
    own = pier_velocity.shape[1]
    f32 = jnp.float32
    hbm = pl.BlockSpec(memory_space=pltpu.HBM)
    vmem = pl.BlockSpec(memory_space=pltpu.VMEM)
    dma = pltpu.SemaphoreType.DMA
    tall = side + 2 * ROWS
    stage = 2 * depth + ROWS
    tiles = line // LANES
    v, s, w = pl.pallas_call(
        functools.partial(fused, n, ng),
        out_shape=(
            pltpu.VMEM((3 * STEPS, depth + 2, tall, line), f32),
            pltpu.VMEM((6, depth + 2, tall, line), f32),
            pltpu.VMEM((own, depth), f32),
        ),
        in_specs=[hbm] * 11,
        out_specs=(vmem, vmem, vmem),
        scratch_shapes=[
            pltpu.SMEM(layer.shape, layer.dtype),
            pltpu.SMEM(lame_table.shape, f32),
            pltpu.SMEM(shear_table.shape, f32),
            pltpu.SMEM(relax_table.shape, f32),
            pltpu.SMEM(footprint.shape, footprint.dtype),
            pltpu.VMEM((own, depth), f32),
            pltpu.SMEM(impedance.shape, f32),
            pltpu.VMEM(damp_inverse.shape, f32),
            dma((8,)),
            pltpu.VMEM((depth, side, line), f32),
            pltpu.VMEM((3, depth + 2, side, LANES), f32),
            pltpu.VMEM((3, depth, side, line), f32),
            pltpu.VMEM((3, depth, side, LANES), f32),
            pltpu.VMEM((3, n * depth, ROWS, LANES), f32),
            pltpu.VMEM((3, n * depth + 2, ROWS, LANES), f32),
            pltpu.VMEM((STEPS, ng, stage, LANES), f32),
            pltpu.VMEM((STEPS, n * depth, LANES), f32),
            pltpu.VMEM((depth, LANES), f32),
            pltpu.VMEM((ROWS, LANES), f32),
            pltpu.VMEM((LANES, LANES), f32),
            pltpu.VMEM((depth * side, LANES), f32),
            pltpu.VMEM((side, LANES), f32),
            pltpu.VMEM((tiles, 2 * LANES, LANES), jnp.bfloat16),
            pltpu.VMEM((2 * LANES, line), jnp.bfloat16),
            pltpu.VMEM(((depth + 2) * side, 2 * LANES), jnp.bfloat16),
            pltpu.VMEM((n * depth, 3 * n * depth), jnp.bfloat16),
            pltpu.VMEM((depth + ROWS, n * depth), f32),
            dma((3 * tiles,)), dma((3,)), dma((3,)), dma((2,)), dma((2,)), dma((3,)), dma((3,)),
            dma((tiles,)), dma((tiles,)), dma((tiles,)), dma((tiles,)),
            dma((STEPS,)), dma((STEPS,)), dma((STEPS,)), dma((STEPS,)),
            dma((tiles, 2)), dma((tiles, 2)),
        ],
        compiler_params=pltpu.CompilerParams(
            collective_id=0, has_side_effects=True, vmem_limit_bytes=48 * 1024 * 1024
        ),
    )(
        velocity, stress, buoyancy, layer, lame_table, shear_table, relax_table,
        footprint, pier_velocity.T, impedance, damp_inverse,
    )
    v, s, w = pl.pallas_call(
        deliver,
        out_shape=tuple(
            jax.ShapeDtypeStruct(a, f32) for a in (velocity.shape, stress.shape, (own, depth))
        ),
        in_specs=[vmem] * 3,
        out_specs=(hbm,) * 3,
        scratch_shapes=[dma((3,))],
        compiler_params=pltpu.CompilerParams(vmem_limit_bytes=8 * 1024 * 1024),
    )(v, s, w)
    return v, s, w.T


def whole_tiles(mesh, velocity, pier_velocity):
    n, ng = mesh.shape["gx"], mesh.shape["gy"]
    depth, side, line = velocity.shape[1] // n, velocity.shape[2] // ng, velocity.shape[3]
    return (
        line % LANES == 0
        and side % 16 == 0
        and side % n == 0
        and depth % ROWS == 0
        and (side // n) * (line // LANES) == ROWS
        and n * depth % LANES == 0
        and pier_velocity.shape[1] <= LANES
    )


def solution(mesh):
    placed = (
        P(None, "gx", "gy", None),
        P(None, "gx", "gy", None),
        P("gx", "gy"),
        P("gx", "gy", None),
        P("gx"),
        P(),
        P(),
        P(),
        P("gy"),
        P(),
        P(),
    )

    def run(*args):
        n, ng = mesh.shape["gx"], mesh.shape["gy"]
        if whole_tiles(mesh, args[0], args[2]):
            part = functools.partial(fused_body, n, ng)
        else:
            part = body
        return mapped(part)(*args)

    def mapped(part):
        return jax.shard_map(
            part,
            mesh=mesh,
            in_specs=placed,
            out_specs=(P(None, "gx", "gy", None), P(None, "gx", "gy", None), P("gx", "gy")),
            check_vma=False,
        )

    return run
```
